128 devices in a mesh: ra: 8 (over x, core), dec: 16 (over z, y).
Axes of the slice: x: 4, y: 4, z: 4, core: 2. Of those that a mesh axis runs over, the one named last changes fastest.
Arguments:
- model: float32 [6, 2048, 4096], P(None, 'ra', 'dec'), may hold values from -6 to 6
- observed: float32 [4096, 4356], P(('ra', 'dec')), may hold values from -6 to 6
- inv_var: float32 [4096, 4356], P(('ra', 'dec')), may hold values from 0.1 to 10
- psf: float32 [4096, 3969], P(('ra', 'dec')), may hold values from -0.09375 to 0.09375
- target_dec: int32 [4096, 1], P('ra'), may hold values from 0 to 15; in each aligned block of 32 rows (0 to 31, 32 to 63, ...) at most 4 rows name the same one
- band: int32 [4096], P('ra'), may hold values from 0 to 5
- offset_ra: int32 [4096], P('ra'), may hold values from 0 to 252
- offset_dec: int32 [4096], P('ra'), may hold values from 0 to 252
Outputs:
- residual: float32 [4096, 4356], P(('ra', 'dec'))
- gradient: float32 [6, 2048, 4096], P(None, 'ra', 'dec')
The draws below stay inside these ranges and needn't reach their ends.
Inputs may be any that keep to these rules, and one draw needn't show every extreme that they name: `target_dec`: among the 32 exposures of one visit owner (aligned blocks of 32 rows), no declination index is named more than 4 times, and one is named exactly 4 times.
All inputs are finite; a program needn't handle non-finite values.
Results may differ from the reference program's by a relative error of at most 0.00012.
Values sent between devices are 32-bit elements; how exact they have to be, the bound alone decides.
A program may use at most 128 MiB of HBM per device.

```python
import math
import jax
import jax.numpy as jnp
import numpy as np
from jax import lax

B = 6
K = 63
C = 66
CAP = 4
E_DEV = 32
TRA = 256
TDEC = 256
P_SIZE = 128
H = 62
NRA = 2048
NDEC = 4096
EXPOSURES = 4096
N_DEC = 16


def with_ends(drawn, key, least, top_value):
    longest = drawn.shape.index(max(drawn.shape))
    spots = []
    for shift in (0, 1):
        where = [jax.random.randint(jax.random.fold_in(key, axis), (), 0, length) for axis, length in enumerate(drawn.shape)]
        where[longest] = (where[longest] + shift) % drawn.shape[longest]
        spots.append(tuple(where))
    return drawn.at[spots[0]].set(least).at[spots[1]].set(top_value)


def levels(own_key, extent, pieces, low, high):
    gain = 1.0
    for axis_at, blocks in pieces:
        steps = jax.random.uniform(jax.random.fold_in(jax.random.fold_in(own_key, 6), axis_at), (blocks,), jnp.float32, low / len(pieces), high / len(pieces))
        gain = gain * jnp.repeat(jnp.exp(steps), extent[axis_at] // blocks).reshape((-1,) + (1,) * (len(extent) - 1 - axis_at))
    return gain


def deal_out(rng, own, number, rows, number_of, top, most, skew):
    ranking = jax.random.permutation(rng, number_of)
    crowded, usual = load_shares(number_of, rows * top, most, skew, True), load_shares(number_of, rows * top, most, skew, False)
    places = jnp.arange(number_of)

    def named(tallies, offset_by):
        used = int((tallies > 0).sum())
        fixed = max(1, used // 4)
        moved = fixed + (places - fixed + offset_by * (used - fixed)) % max(1, number_of - fixed)
        return jnp.zeros((number_of,), jnp.int32).at[ranking[jnp.where(places < fixed, places, moved)]].set(jnp.asarray(tallies, jnp.int32))

    tallies = jnp.where(number % 4 == 0, named(crowded, number // 4), named(usual, number - number // 4 - 1))
    mixed = jax.random.permutation(jax.random.fold_in(own, 3), number_of)
    donor, taker = mixed[0:number_of // 2 * 2:2], mixed[1:number_of // 2 * 2:2]
    margin = jnp.minimum(tallies[donor] - 1, most - tallies[taker]) // 2
    margin = jnp.where((donor == ranking[0]) | (taker == ranking[0]) | (tallies[taker] == 0), 0, jnp.maximum(margin, 0))
    moved = jax.random.randint(jax.random.fold_in(own, 4), (number_of // 2,), 0, 1 << 20) % (margin + 1)
    tallies = tallies.at[donor].add(-moved).at[taker].add(moved)
    labels = jnp.searchsorted(jnp.cumsum(tallies), jnp.arange(rows * top), side="right").astype(jnp.int32)
    table = labels.reshape(top, rows).T
    table = table[jax.random.permutation(jax.random.fold_in(own, 1), rows)]
    offset_by = jax.random.randint(jax.random.fold_in(own, 2), (rows, 1), 0, top)
    return jnp.take_along_axis(table, (jnp.arange(top)[None, :] + offset_by) % top, axis=1)


def load_shares(amount, total, reach, skew, full):
    loads = [(1 << 20) // math.isqrt(standing ** skew) + 1 for standing in range(1, amount + 1)]
    largest = reach if full else min(reach, max(-(-total // amount), total * loads[0] // sum(loads)))
    least = 1 if total - largest >= amount - 1 else 0
    counts, rest = [largest] + [least] * (amount - 1), total - largest - least * (amount - 1)
    while rest > 0:
        free = [i for i in range(1, amount) if counts[i] < largest] or [i for i in range(1, amount) if counts[i] < reach]
        pool, remaining = sum([loads[i] for i in free]), rest
        for i in free:
            addition = min(reach - counts[i], max(1, remaining * loads[i] // pool), rest)
            counts[i] = counts[i] + addition
            rest = rest - addition
    return np.array(counts)


def gaussian(rng, extent, width, limit, pieces=(), kind=jnp.bfloat16):
    entries = jax.random.normal(rng, extent, jnp.float32) * width
    if len(pieces) > 0:
        entries = levels(rng, extent, pieces, -0.22, 0.18) * entries
    return jnp.clip(entries, min=-limit, max=limit).astype(kind)


def setup_inputs(seed: int = 0) -> dict:
    key_of = jax.random.split(jax.random.key(seed), 9)
    model = gaussian(key_of[0], (B, NRA, NDEC), 1.0, 6.0, ((1, 8), (2, 16)), jnp.float32)
    observed = gaussian(key_of[1], (EXPOSURES, C * C), 1.0, 6.0, ((0, 128),), jnp.float32)
    inv_var = jnp.clip(jnp.exp(math.log(10.0) - 4.6051702 * jax.random.uniform(key_of[2], (EXPOSURES, C * C), jnp.float32) ** levels(key_of[2], (EXPOSURES, C * C), ((0, 128),), -0.2, 0.2)), 0.1, 10.0)
    psf = gaussian(key_of[3], (EXPOSURES, K * K), (K * K) ** -0.5, 0.09375, ((0, 128),), jnp.float32)
    target_dec_keys = jax.random.split(jax.random.fold_in(key_of[4], 1), EXPOSURES // E_DEV)
    target_dec_turns = jax.random.permutation(jax.random.fold_in(key_of[4], 3), EXPOSURES // E_DEV)
    target_dec = jax.vmap(lambda own, number: deal_out(jax.random.fold_in(key_of[4], 2), own, number, E_DEV, N_DEC, 1, CAP, 2))(target_dec_keys, target_dec_turns).reshape((EXPOSURES, 1))
    band = with_ends(jax.random.randint(key_of[5], (EXPOSURES,), 0, B), jax.random.fold_in(key_of[5], 1), 0, B - 1).astype(jnp.int32)
    offset_ra = with_ends(jax.random.randint(key_of[6], (EXPOSURES,), 0, TRA + 2 * H - P_SIZE + 1), jax.random.fold_in(key_of[6], 1), 0, TRA + 2 * H - P_SIZE).astype(jnp.int32)
    offset_dec = with_ends(jax.random.randint(key_of[7], (EXPOSURES,), 0, TDEC + 2 * H - P_SIZE + 1), jax.random.fold_in(key_of[7], 1), 0, TDEC + 2 * H - P_SIZE).astype(jnp.int32)
    return {"model": model, "observed": observed, "inv_var": inv_var, "psf": psf, "target_dec": target_dec, "band": band, "offset_ra": offset_ra, "offset_dec": offset_dec}


def reference(model, observed, inv_var, psf, target_dec, band, offset_ra, offset_dec):
    count = observed.shape[0]
    padded = jnp.pad(model, ((0, 0), (H, H), (H, H)))
    rows = jnp.arange(count, dtype=jnp.int32)
    ra_index = rows // (N_DEC * E_DEV)
    start_ra = (ra_index * TRA + offset_ra).astype(jnp.int32)
    start_dec = (target_dec[:, 0] * TDEC + offset_dec).astype(jnp.int32)

    def visit(gradpad, item):
        which, first_ra, first_dec, seen, weight, kernel = item
        patch = lax.dynamic_slice(padded, (which, first_ra, first_dec), (1, P_SIZE, P_SIZE))[0]
        kernel_pad = jnp.pad(kernel.reshape(K, K), ((0, P_SIZE - K), (0, P_SIZE - K)))
        khat = jnp.fft.fft2(kernel_pad)
        predicted = jnp.real(jnp.fft.ifft2(jnp.fft.fft2(patch) * khat)).astype(jnp.float32)[K - 1:, K - 1:]
        resid = weight.reshape(C, C) * (predicted - seen.reshape(C, C))
        resid_pad = jnp.pad(resid, ((K - 1, 0), (K - 1, 0)))
        back = jnp.real(jnp.fft.ifft2(jnp.fft.fft2(resid_pad) * jnp.conj(khat))).astype(jnp.float32)
        current = lax.dynamic_slice(gradpad, (which, first_ra, first_dec), (1, P_SIZE, P_SIZE))
        gradpad = lax.dynamic_update_slice(gradpad, current + back[None], (which, first_ra, first_dec))
        return gradpad, resid.reshape(C * C)

    gradpad, residual = lax.scan(visit, jnp.zeros_like(padded), (band, start_ra, start_dec, observed, inv_var, psf))
    return residual, gradpad[:, H:-H, H:-H]
```

```python
import functools
import math

import jax
import jax.numpy as jnp
import ml_dtypes
import numpy as np
from jax import lax
from jax.experimental import pallas as pl
from jax.experimental.pallas import tpu as pltpu
from jax.sharding import PartitionSpec as P

K = 63
C = 66
CAP = 4
N = 128
PAIRS = 33
PAD = 40
PSF_ROWS = 32
OBS_AT = 32
VAR_AT = 72
SLOT_ROWS = 112
EDGE = 64
SIDE = 128
LIMIT = 60 * 1024 * 1024
MESH = pl.DeviceIdType.MESH
F32 = jnp.float32
BF16 = jnp.bfloat16


def np_split(table):
    high = table.astype(np.float32).astype(ml_dtypes.bfloat16)
    low = (table - high.astype(np.float64)).astype(np.float32).astype(ml_dtypes.bfloat16)
    return high, low


def make_tables():
    theta = 2.0 * math.pi * (np.arange(64) + 0.5) / N

    def to_freq(columns):
        angle = np.asarray(columns)[:, None] * theta[None, :]
        return np.concatenate([np.cos(angle), -np.sin(angle)], axis=1)

    def rows_cs(out_index, in_index, sign):
        angle = 2.0 * math.pi * ((out_index[:, None] * in_index[None, :]) % N) / N
        return np.cos(angle), sign * np.sin(angle)

    full = np.arange(N)
    zero = np.zeros((N, N))
    zero16 = zero.astype(ml_dtypes.bfloat16)

    def wide(table):
        high, low = np_split(table)
        return np.block([[high, low], [high, zero16]])

    patch_cols = wide(to_freq(full))
    psf_cols = np.zeros((N, 2 * N))
    psf_cols[:K, :N] = to_freq(np.arange(K))
    psf_cols[K : 2 * K, N:] = to_freq(np.arange(K))
    psf_h, psf_l = np_split(psf_cols)
    psf_cols = np.concatenate([psf_h, psf_h, psf_l], axis=0)

    def left(out_index, in_index, sign, keep_in=None, keep_out=None):
        cosine, sine = rows_cs(out_index, in_index, sign)
        table = np.concatenate([cosine, sine], axis=1)
        if keep_in is not None:
            table = table * np.concatenate([keep_in, keep_in])[None, :]
        if keep_out is not None:
            table = table * keep_out[:, None]
        return np.concatenate(np_split(table), axis=0)

    patch_rows = left(full, full, 1.0)
    psf_index = np.concatenate([2 * np.arange(32), 2 * np.arange(32) + 1])
    psf_rows = left(full, psf_index, 1.0, keep_in=(psf_index < K).astype(np.float64))
    within = (np.arange(PAD) < PAIRS).astype(np.float64)
    inner_keep = np.concatenate([within, within])
    inner_index = np.concatenate([K - 1 + 2 * np.arange(PAD), K + 2 * np.arange(PAD)])
    pred_rows = left(inner_index, full, -1.0, keep_out=inner_keep)
    res_rows = left(full, inner_index, 1.0, keep_in=inner_keep)
    back_rows = left(full, full, -1.0)
    scale = 2.0 / (N * N)
    inner_cols = K - 1 + np.arange(C)
    pred_cols = np.zeros((2 * N, 2 * N))
    pred_cols[:N, :C] = scale * to_freq(inner_cols).T
    pred_cols[N:, C : 2 * C] = scale * to_freq(inner_cols).T
    pred_cols = np.concatenate(np_split(pred_cols), axis=0)
    res_cols = np.zeros((2 * N, 2 * N))
    res_cols[:C, :N] = to_freq(inner_cols)
    res_cols[C : 2 * C, N:] = to_freq(inner_cols)
    res_cols = np.concatenate(np_split(res_cols), axis=0)
    back_cols = wide(scale * to_freq(full).T)
    psf_rows = np.concatenate([np.concatenate([psf_rows[:N], psf_rows[:N]], axis=1),
                               np.concatenate([psf_rows[N:], np.zeros_like(psf_rows[N:])], axis=1)], axis=0)
    return (patch_cols, patch_rows, psf_cols, psf_rows, pred_rows, pred_cols, res_cols, res_rows,
            back_rows, back_cols)


def split(x):
    high = x.astype(BF16)
    return high, (x - high.astype(F32)).astype(BF16)


def dot(a, b):
    return jnp.dot(a, b, preferred_element_type=F32)


def right_wide(x, table_ref):
    high, low = split(x)
    both = dot(jnp.concatenate([high, low], axis=1), table_ref[...])
    return both[:, :N] + both[:, N:]


def right_three(x, table_ref):
    high, low = split(x)
    depth = x.shape[1]
    return (dot(high, table_ref[:depth, :]) + dot(low, table_ref[:depth, :])
            + dot(high, table_ref[depth:, :]))


def left_three(table_ref, x):
    rows = table_ref.shape[0] // 2
    high, low = split(x)
    both = dot(table_ref[...], high)
    return both[:rows] + both[rows:] + dot(table_ref[:rows, :], low)


def turned(y, sign):
    return pltpu.roll(y, 64, 1) * sign


def stacked(parts, sign):
    return jnp.concatenate(
        [jnp.concatenate([y, turned(y, sign)], axis=0) for y in parts], axis=1)


def exposure_kernel(first, meta_ref, slots_ref, ext_ref, *refs):
    if first:
        acc_in_ref = None
    else:
        acc_in_ref, refs = refs[0], refs[1:]
    (patch_cols, patch_rows, psf_cols, psf_rows, pred_rows, pred_cols, res_cols, res_rows,
     back_rows, back_cols, resid_ref, acc_ref) = refs
    step = pl.program_id(0)

    @pl.when(step == 0)
    def _():
        if first:
            acc_ref[...] = jnp.zeros_like(acc_ref)
        else:
            acc_ref[...] = acc_in_ref[...]

    lane = lax.broadcasted_iota(jnp.int32, (1, N), 1)
    sign = jnp.where(lane < 64, 1.0, -1.0).astype(F32)
    low_half = lane < 64

    places = []
    patches = []
    for e in range(2):
        code = jnp.maximum(meta_ref[step * 2 + e] - 1, 0)
        which = lax.shift_right_logical(code, 16)
        row = lax.bitwise_and(lax.shift_right_logical(code, 8), 255) + (EDGE - K + 1)
        column = lax.bitwise_and(code, 255) + (SIDE - K + 1)
        row_at = pl.multiple_of(lax.shift_left(lax.shift_right_logical(row, 3), 3), 8)
        col_at = pl.multiple_of(lax.shift_left(lax.shift_right_logical(column, 7), 7), 128)
        down = row - row_at
        over = column - col_at
        places.append((which, row_at, col_at, down, over))
        window = ext_ref[which, pl.ds(row_at, N + 8), pl.ds(col_at, 2 * N)]
        window = pltpu.roll(window, lax.bitwise_and(2 * N - over, 2 * N - 1), 1)[:, :N]
        window = pltpu.roll(window, jnp.where(down == 0, 0, N + 8 - down), 0)[:N]
        patches.append(window)

    y = right_wide(jnp.concatenate(patches, axis=0), patch_cols)
    z = left_three(patch_rows, stacked([y[:N], y[N:]], sign))

    pairs = []
    for e in range(2):
        x = slots_ref[e, :PSF_ROWS, :]
        both = jnp.concatenate([pltpu.roll(x, 1, 0), x], axis=1)
        pairs.append(pltpu.roll(both, N, 1, stride=2, stride_axis=0)[:, :N])
    high, low = split(jnp.concatenate(pairs, axis=0))
    y = dot(jnp.concatenate([high, low], axis=1), psf_cols[: 2 * N, :]) + dot(high, psf_cols[2 * N :, :])
    y = stacked([jnp.concatenate([y[32 * e : 32 * e + 32, :N], y[32 * e : 32 * e + 32, N:]], axis=0)
                 for e in range(2)], sign)
    high, low = split(y)
    khat = (dot(psf_rows[:N, :], jnp.concatenate([high, low], axis=0))
            + dot(psf_rows[N:, :N], high))

    kernels = []
    spec = []
    for e in range(2):
        k = khat[:, e * N : e * N + N]
        rk = pltpu.roll(k, 64, 1)
        k_re = jnp.where(low_half, k, rk)
        k_im = jnp.where(low_half, -rk, k)
        kernels.append((k_re, k_im))
        p = z[:, e * N : e * N + N]
        rp = pltpu.roll(p, 64, 1)
        spec.append(jnp.concatenate(
            [p * k_re + rp * k_im, (rp * k_re - p * k_im) * sign], axis=0))
    u = left_three(pred_rows, jnp.concatenate(spec, axis=1))
    u = jnp.concatenate(
        [jnp.concatenate([u[:PAD, e * N : e * N + N], u[PAD:, e * N : e * N + N]], axis=1)
         for e in range(2)], axis=0)
    predicted = right_three(u, pred_cols)

    number = lax.broadcasted_iota(jnp.int32, (PAD, 1), 0)
    last = number == PAIRS - 1
    turn = lax.bitwise_and(lane + 4 * number, N - 1)
    pairs = []
    for e in range(2):
        image = pltpu.roll(predicted[e * PAD : e * PAD + PAD], 0, 1, stride=4, stride_axis=0)
        front, rear = image[:, :N], image[:, N:]
        flat = (jnp.where(last, 0.0, front) + pltpu.roll(rear, 1, 0)
                + pltpu.roll(jnp.where(last, front, 0.0), 2, 0))
        resid = slots_ref[e, VAR_AT : VAR_AT + PAD, :] * (flat - slots_ref[e, OBS_AT : OBS_AT + PAD, :])
        resid_ref[e] = resid
        front = jnp.take_along_axis(resid, turn, axis=1, mode="promise_in_bounds")
        rear = jnp.take_along_axis(pltpu.roll(resid, PAD - 1, 0), turn, axis=1, mode="promise_in_bounds")
        pairs.append(jnp.concatenate(
            [jnp.where(lane + 4 * number < N, front, rear),
             jnp.where(last, pltpu.roll(resid, PAD - 2, 0), rear)], axis=1))
    v = right_three(jnp.concatenate(pairs, axis=0), res_cols)
    v = [jnp.concatenate([v[e * PAD : e * PAD + PAD, :N], v[e * PAD : e * PAD + PAD, N:]], axis=0)
         for e in range(2)]
    r = left_three(res_rows, stacked(v, sign))
    spec = []
    for e in range(2):
        k_re, k_im = kernels[e]
        p = r[:, e * N : e * N + N]
        rp = pltpu.roll(p, 64, 1)
        spec.append(jnp.concatenate(
            [p * k_re - rp * k_im, (rp * k_re + p * k_im) * sign], axis=0))
    u = left_three(back_rows, jnp.concatenate(spec, axis=1))
    back = right_wide(jnp.concatenate([u[:, :N], u[:, N:]], axis=0), back_cols)
    for e in range(2):
        which, row_at, col_at, down, over = places[e]
        image = jnp.concatenate([back[e * N : e * N + N], jnp.zeros((8, N), F32)], axis=0)
        image = pltpu.roll(image, down, 0)
        image = jnp.concatenate([image, jnp.zeros_like(image)], axis=1)
        image = pltpu.roll(image, over, 1)
        acc_ref[which, pl.ds(row_at, N + 8), pl.ds(col_at, 2 * N)] += image


def whole(shape):
    return pl.BlockSpec(shape, lambda i, meta: (0,) * len(shape), pipeline_mode=pl.Buffered(1))


def run_exposures(meta, slots, ext, acc, tables):
    number = slots.shape[0]
    first = acc is None
    operands = [slots, ext] + ([] if first else [acc]) + list(tables)
    in_specs = [pl.BlockSpec((2, SLOT_ROWS, N), lambda i, meta: (i, 0, 0))]
    in_specs += [whole(o.shape) for o in operands[1:]]
    return pl.pallas_call(
        functools.partial(exposure_kernel, first),
        grid_spec=pltpu.PrefetchScalarGridSpec(
            num_scalar_prefetch=1,
            grid=(number // 2,),
            in_specs=in_specs,
            out_specs=[
                pl.BlockSpec((2, PAD, N), lambda i, meta: (i, 0, 0)),
                whole(ext.shape),
            ],
        ),
        out_shape=[
            jax.ShapeDtypeStruct((number, PAD, N), F32),
            jax.ShapeDtypeStruct(ext.shape, F32),
        ],
        compiler_params=pltpu.CompilerParams(vmem_limit_bytes=LIMIT),
        cost_estimate=pl.CostEstimate(flops=number * 200_000_000, bytes_accessed=12_000_000, transcendentals=0),
    )(meta, *operands)


def three(x):
    high = x.astype(BF16)
    rest = x - high.astype(F32)
    middle = rest.astype(BF16)
    return jnp.concatenate([high, middle, (rest - middle.astype(F32)).astype(BF16)], axis=0)


def prepare_kernel(n_dec, column_ref, row_ref, psf_ref, obs_ref, var_ref, out_ref):
    column, row = column_ref[...], row_ref[...]
    count = row.shape[1]
    slots = CAP * n_dec
    earlier = lax.broadcasted_iota(jnp.int32, (count, count), 0) < lax.broadcasted_iota(
        jnp.int32, (count, count), 1)
    rank = jnp.sum(jnp.where(jnp.logical_and(column == row, earlier), 1, 0), axis=0, keepdims=True)
    place = rank * n_dec + row
    chosen = (lax.broadcasted_iota(jnp.int32, (slots, count), 0) == place).astype(F32).astype(BF16)
    chosen = jnp.concatenate([chosen] * 3, axis=1)
    for ref, base, rows in ((psf_ref, 0, 32), (obs_ref, OBS_AT, PAD), (var_ref, VAR_AT, PAD)):
        width = ref.shape[1]
        for start in range(0, rows, 4):
            end = min((start + 4) * N, width)
            if start * N < width:
                x = ref[:, start * N : end]
                y = dot(chosen, three(x))
                if end < (start + 4) * N:
                    y = jnp.concatenate([y, jnp.zeros((slots, (start + 4) * N - end), F32)], axis=1)
            else:
                y = jnp.zeros((slots, 4 * N), F32)
            for t in range(4):
                out_ref[pl.ds(base + start + t, slots, stride=SLOT_ROWS), :] = y[:, t * N : t * N + N]


def prepare(column, row, psf, obs, var, n_dec):
    return pl.pallas_call(
        functools.partial(prepare_kernel, n_dec),
        out_shape=jax.ShapeDtypeStruct((CAP * n_dec * SLOT_ROWS, N), F32),
        compiler_params=pltpu.CompilerParams(vmem_limit_bytes=LIMIT),
    )(column, row, psf, obs, var)


def finish_kernel(n_dec, column_ref, row_ref, in_ref, out_ref):
    column, row = column_ref[...], row_ref[...]
    count = row.shape[1]
    slots = CAP * n_dec
    earlier = lax.broadcasted_iota(jnp.int32, (count, count), 1) < lax.broadcasted_iota(
        jnp.int32, (count, count), 0)
    rank = jnp.sum(jnp.where(jnp.logical_and(column == row, earlier), 1, 0), axis=1, keepdims=True)
    place = rank * n_dec + column
    chosen = (lax.broadcasted_iota(jnp.int32, (count, slots), 1) == place).astype(F32).astype(BF16)
    chosen = jnp.concatenate([chosen] * 3, axis=1)
    width = out_ref.shape[1]
    for start in range(0, PAD, 4):
        if start * N >= width:
            break
        x = jnp.concatenate(
            [in_ref[pl.ds(start + t, slots, stride=PAD), :] for t in range(4)], axis=1)
        y = dot(chosen, three(x))
        end = min((start + 4) * N, width)
        out_ref[:, start * N : end] = y[:, : end - start * N]


def finish(column, row, landed, n_dec):
    return pl.pallas_call(
        functools.partial(finish_kernel, n_dec),
        out_shape=jax.ShapeDtypeStruct((row.shape[1], C * C), F32),
        compiler_params=pltpu.CompilerParams(vmem_limit_bytes=LIMIT),
    )(column, row, landed)


def neighbours(n_ra, n_dec):
    ra, dec = lax.axis_index("ra"), lax.axis_index("dec")
    up, down = lax.rem(ra + 1, n_ra), lax.rem(ra + n_ra - 1, n_ra)
    right, left = lax.rem(dec + 1, n_dec), lax.rem(dec + n_dec - 1, n_dec)
    return ra, dec, up, down, right, left


def greet(ra, dec, up, down, right, left):
    barrier = pltpu.get_barrier_semaphore()
    for other in ((up, dec), (down, dec), (ra, right), (ra, left),
                  (up, right), (up, left), (down, right), (down, left)):
        pl.semaphore_signal(barrier, inc=1, device_id=other, device_id_type=MESH)
    pl.semaphore_wait(barrier, 8)


def halo_kernel(n_ra, n_dec, model_ref, ext_ref, to_right, to_left, from_left, from_right, corners,
                send, recv):
    ra, dec, up, down, right, left = neighbours(n_ra, n_dec)
    greet(ra, dec, up, down, right, left)
    tra, tdec = model_ref.shape[1], model_ref.shape[2]
    top, side_at = EDGE + tra, SIDE + tdec
    low_half = lax.broadcasted_iota(jnp.int32, (1, 1, N), 2) < 64

    def copy(index, src, dst, other):
        return pltpu.make_async_remote_copy(
            src_ref=src, dst_ref=dst, send_sem=send.at[index], recv_sem=recv.at[index],
            device_id=other, device_id_type=MESH)

    copies = [
        copy(0, model_ref.at[:, tra - EDGE :, :], ext_ref.at[:, :EDGE, SIDE:side_at], (up, dec)),
        copy(1, model_ref.at[:, :EDGE, :], ext_ref.at[:, top:, SIDE:side_at], (down, dec)),
    ]
    for c in copies:
        c.start()
    for q in range(3):
        to_right[q] = jnp.where(
            low_half[0], pltpu.roll(model_ref[2 * q + 1, :, tdec - N :], 64, 1), model_ref[2 * q, :, tdec - N :])
    more = [
        copy(2, to_right, from_left, (ra, right)),
        copy(4, to_right.at[:, tra - EDGE :, :], corners.at[0], (up, right)),
        copy(5, to_right.at[:, :EDGE, :], corners.at[1], (down, right)),
    ]
    for c in more:
        c.start()
    copies += more
    for q in range(3):
        to_left[q] = jnp.where(
            low_half[0], model_ref[2 * q, :, :N], pltpu.roll(model_ref[2 * q + 1, :, :N], 64, 1))
    more = [
        copy(3, to_left, from_right, (ra, left)),
        copy(6, to_left.at[:, tra - EDGE :, :], corners.at[2], (up, left)),
        copy(7, to_left.at[:, :EDGE, :], corners.at[3], (down, left)),
    ]
    for c in more:
        c.start()
    copies += more
    ext_ref[:, EDGE:top, SIDE:side_at] = model_ref[...]
    for c in copies:
        c.wait()
    zero = jnp.zeros((), F32)
    one = jnp.ones((), F32)
    in_left = jnp.where(dec > 0, one, zero)
    in_right = jnp.where(dec < n_dec - 1, one, zero)
    in_low = jnp.where(ra > 0, one, zero)
    in_high = jnp.where(ra < n_ra - 1, one, zero)

    @pl.when(ra == 0)
    def _():
        ext_ref[:, :EDGE, SIDE:side_at] = jnp.zeros((ext_ref.shape[0], EDGE, tdec), F32)

    @pl.when(ra == n_ra - 1)
    def _():
        ext_ref[:, top:, SIDE:side_at] = jnp.zeros((ext_ref.shape[0], EDGE, tdec), F32)

    for q in range(3):
        for src, rows, col, scale in (
            (from_left.at[q], slice(EDGE, top), slice(0, SIDE), in_left),
            (from_right.at[q], slice(EDGE, top), slice(side_at, side_at + SIDE), in_right),
            (corners.at[0, q], slice(0, EDGE), slice(0, SIDE), in_low * in_left),
            (corners.at[1, q], slice(top, top + EDGE), slice(0, SIDE), in_high * in_left),
            (corners.at[2, q], slice(0, EDGE), slice(side_at, side_at + SIDE), in_low * in_right),
            (corners.at[3, q], slice(top, top + EDGE), slice(side_at, side_at + SIDE), in_high * in_right),
        ):
            value = src[...] * scale
            ext_ref[2 * q, rows, col] = value
            ext_ref[2 * q + 1, rows, col] = pltpu.roll(value, 64, 1)


def halo(model, n_ra, n_dec):
    bands, tra, tdec = model.shape
    strip = pltpu.VMEM((3, tra, N), F32)
    return pl.pallas_call(
        functools.partial(halo_kernel, n_ra, n_dec),
        out_shape=jax.ShapeDtypeStruct((bands, tra + 2 * EDGE, tdec + 2 * SIDE), F32),
        in_specs=[pl.BlockSpec(memory_space=pltpu.VMEM)],
        out_specs=pl.BlockSpec(memory_space=pltpu.VMEM),
        scratch_shapes=[strip, strip, strip, strip, pltpu.VMEM((4, 3, EDGE, N), F32),
                        pltpu.SemaphoreType.DMA((8,)), pltpu.SemaphoreType.DMA((8,))],
        compiler_params=pltpu.CompilerParams(
            collective_id=0, has_side_effects=True, vmem_limit_bytes=LIMIT),
        cost_estimate=pl.CostEstimate(flops=0, bytes_accessed=40_000_000, transcendentals=0),
    )(model)


def fold_kernel(n_ra, n_dec, acc_ref, out_ref, to_right, to_left, from_left, from_right, out_corners,
                corners, from_up, from_down, send, recv):
    ra, dec, up, down, right, left = neighbours(n_ra, n_dec)
    greet(ra, dec, up, down, right, left)
    tra, tdec = out_ref.shape[1], out_ref.shape[2]
    top, side_at = EDGE + tra, SIDE + tdec
    low_half = lax.broadcasted_iota(jnp.int32, (1, N), 1) < 64

    def copy(index, src, dst, other):
        return pltpu.make_async_remote_copy(
            src_ref=src, dst_ref=dst, send_sem=send.at[index], recv_sem=recv.at[index],
            device_id=other, device_id_type=MESH)

    copies = [
        copy(0, acc_ref.at[:, :EDGE, SIDE:side_at], from_up, (down, dec)),
        copy(1, acc_ref.at[:, top:, SIDE:side_at], from_down, (up, dec)),
    ]
    for c in copies:
        c.start()

    def pack_left(q, rows):
        return jnp.where(low_half, pltpu.roll(acc_ref[2 * q + 1, rows, :SIDE], 64, 1), acc_ref[2 * q, rows, :SIDE])

    def pack_right(q, rows):
        return jnp.where(low_half, acc_ref[2 * q, rows, side_at:], pltpu.roll(acc_ref[2 * q + 1, rows, side_at:], 64, 1))

    middle, lower, upper = slice(EDGE, top), slice(0, EDGE), slice(top, top + EDGE)
    for q in range(3):
        to_left[q] = pack_left(q, middle)
    more = [copy(2, to_left, from_right, (ra, left))]
    more[0].start()
    copies += more
    for q in range(3):
        to_right[q] = pack_right(q, middle)
    more = [copy(3, to_right, from_left, (ra, right))]
    more[0].start()
    copies += more
    for q in range(3):
        out_corners[0, q] = pack_left(q, lower)
        out_corners[1, q] = pack_left(q, upper)
        out_corners[2, q] = pack_right(q, lower)
        out_corners[3, q] = pack_right(q, upper)
    more = [
        copy(4, out_corners.at[0], corners.at[0], (down, left)),
        copy(5, out_corners.at[1], corners.at[1], (up, left)),
        copy(6, out_corners.at[2], corners.at[2], (down, right)),
        copy(7, out_corners.at[3], corners.at[3], (up, right)),
    ]
    for c in more:
        c.start()
    copies += more
    out_ref[...] = acc_ref[:, EDGE:top, SIDE:side_at]
    for c in copies:
        c.wait()
    zero = jnp.zeros((), F32)
    one = jnp.ones((), F32)
    in_left = jnp.where(dec > 0, one, zero)
    in_right = jnp.where(dec < n_dec - 1, one, zero)
    in_low = jnp.where(ra > 0, one, zero)
    in_high = jnp.where(ra < n_ra - 1, one, zero)
    out_ref[:, tra - EDGE :, :] += from_up[...] * in_high
    out_ref[:, :EDGE, :] += from_down[...] * in_low
    every, low_rows, high_rows = slice(0, tra), slice(0, EDGE), slice(tra - EDGE, tra)
    for q in range(3):
        for src, rows, scale, at_right in (
            (from_right.at[q], every, in_right, True),
            (from_left.at[q], every, in_left, False),
            (corners.at[0, q], high_rows, in_high * in_right, True),
            (corners.at[1, q], low_rows, in_low * in_right, True),
            (corners.at[2, q], high_rows, in_high * in_left, False),
            (corners.at[3, q], low_rows, in_low * in_left, False),
        ):
            value = src[...] * scale
            other = pltpu.roll(value, 64, 1)
            if at_right:
                cols, keep = slice(tdec - N, tdec), jnp.logical_not(low_half)
            else:
                cols, keep = slice(0, N), low_half
            out_ref[2 * q, rows, cols] += jnp.where(keep, value, 0.0)
            out_ref[2 * q + 1, rows, cols] += jnp.where(keep, other, 0.0)


def fold(acc, n_ra, n_dec):
    bands, tra, tdec = acc.shape[0], acc.shape[1] - 2 * EDGE, acc.shape[2] - 2 * SIDE
    strip = pltpu.VMEM((3, tra, N), F32)
    corner = pltpu.VMEM((4, 3, EDGE, N), F32)
    band = pltpu.VMEM((bands, EDGE, tdec), F32)
    return pl.pallas_call(
        functools.partial(fold_kernel, n_ra, n_dec),
        out_shape=jax.ShapeDtypeStruct((bands, tra, tdec), F32),
        in_specs=[pl.BlockSpec(memory_space=pltpu.VMEM)],
        out_specs=pl.BlockSpec(memory_space=pltpu.VMEM),
        scratch_shapes=[strip, strip, strip, strip, corner, corner, band, band,
                        pltpu.SemaphoreType.DMA((8,)), pltpu.SemaphoreType.DMA((8,))],
        compiler_params=pltpu.CompilerParams(
            collective_id=1, has_side_effects=True, vmem_limit_bytes=LIMIT),
        cost_estimate=pl.CostEstimate(flops=0, bytes_accessed=40_000_000, transcendentals=0),
    )(acc)


def body(model, observed, inv_var, psf, target_dec, band, offset_ra, offset_dec):
    n_ra, n_dec = lax.axis_size("ra"), lax.axis_size("dec")
    own = lax.axis_index("dec")
    e_dev = observed.shape[0]
    targets = target_dec[:, 0].reshape(n_dec, e_dev)
    row = lax.dynamic_slice_in_dim(targets, own, 1, 0)
    column = lax.dynamic_slice_in_dim(target_dec, own * e_dev, e_dev, 0)
    slots = prepare(column, row, psf, observed, inv_var, n_dec)
    slots = slots.reshape(CAP, n_dec, SLOT_ROWS, N)
    here = targets == own
    order = jnp.arange(e_dev, dtype=jnp.int32)
    rank = jnp.sum(jnp.where(here[:, None, :] & (order[None, :] < order[:, None])[None], 1, 0), axis=2)
    code = ((band * 256 + offset_ra) * 256 + offset_dec + 1).reshape(n_dec, e_dev)
    meta = jnp.sum(
        jnp.where(here[None] & (rank[None] == jnp.arange(CAP, dtype=jnp.int32)[:, None, None]), code[None], 0),
        axis=2)
    arrived = [lax.all_to_all(slots[s], "dec", 0, 0, tiled=True) for s in range(CAP)]
    ext = halo(model, n_ra, n_dec)
    tables = [jnp.asarray(t) for t in make_tables()]
    acc = None
    landed = []
    for s in range(CAP):
        resid, acc = run_exposures(meta[s], arrived[s], ext, acc, tables)
        landed.append(lax.all_to_all(resid, "dec", 0, 0, tiled=True))
    gradient = fold(acc, n_ra, n_dec)
    landed = jnp.concatenate(landed, axis=0).reshape(CAP * n_dec * PAD, N)
    residual = finish(column, row, landed, n_dec)
    return residual, gradient


def solution(mesh):
    placed = (
        P(None, "ra", "dec"),
        P(("ra", "dec"), None),
        P(("ra", "dec"), None),
        P(("ra", "dec"), None),
        P("ra", None),
        P("ra"),
        P("ra"),
        P("ra"),
    )
    return jax.shard_map(
        body,
        mesh=mesh,
        in_specs=placed,
        out_specs=(P(("ra", "dec"), None), P(None, "ra", "dec")),
        check_vma=False,
    )
```

```python
import functools
import math

import jax
import jax.numpy as jnp
import ml_dtypes
import numpy as np
from jax import lax
from jax.experimental import pallas as pl
from jax.experimental.pallas import tpu as pltpu
from jax.sharding import PartitionSpec as P

K = 63
C = 66
CAP = 4
GROUP = 8
N = 128
PAIRS = 33
PAD = 40
PSF_ROWS = 32
OBS_AT = 32
VAR_AT = 72
SLOT_ROWS = 112
EDGE = 64
SIDE = 128
LIMIT = 60 * 1024 * 1024
MESH = pl.DeviceIdType.MESH
F32 = jnp.float32
BF16 = jnp.bfloat16


def np_split(table):
    high = table.astype(np.float32).astype(ml_dtypes.bfloat16)
    low = (table - high.astype(np.float64)).astype(np.float32).astype(ml_dtypes.bfloat16)
    return high, low


def make_tables():
    theta = 2.0 * math.pi * (np.arange(64) + 0.5) / N

    def to_freq(columns):
        angle = np.asarray(columns)[:, None] * theta[None, :]
        return np.concatenate([np.cos(angle), -np.sin(angle)], axis=1)

    def rows_cs(out_index, in_index, sign):
        angle = 2.0 * math.pi * ((out_index[:, None] * in_index[None, :]) % N) / N
        return np.cos(angle), sign * np.sin(angle)

    full = np.arange(N)
    zero = np.zeros((N, N))
    zero16 = zero.astype(ml_dtypes.bfloat16)

    def wide(table):
        high, low = np_split(table)
        return np.block([[high, low], [high, zero16]])

    patch_cols = wide(to_freq(full))
    psf_cols = np.zeros((N, 2 * N))
    psf_cols[:K, :N] = to_freq(np.arange(K))
    psf_cols[K : 2 * K, N:] = to_freq(np.arange(K))
    psf_h, psf_l = np_split(psf_cols)
    psf_cols = np.concatenate([psf_h, psf_h, psf_l], axis=0)

    def left(out_index, in_index, sign, keep_in=None, keep_out=None):
        cosine, sine = rows_cs(out_index, in_index, sign)
        table = np.concatenate([cosine, sine], axis=1)
        if keep_in is not None:
            table = table * np.concatenate([keep_in, keep_in])[None, :]
        if keep_out is not None:
            table = table * keep_out[:, None]
        return np.concatenate(np_split(table), axis=0)

    patch_rows = left(full, full, 1.0)
    psf_index = np.concatenate([2 * np.arange(32), 2 * np.arange(32) + 1])
    psf_rows = left(full, psf_index, 1.0, keep_in=(psf_index < K).astype(np.float64))
    within = (np.arange(PAD) < PAIRS).astype(np.float64)
    inner_keep = np.concatenate([within, within])
    inner_index = np.concatenate([K - 1 + 2 * np.arange(PAD), K + 2 * np.arange(PAD)])
    pred_rows = left(inner_index, full, -1.0, keep_out=inner_keep)
    res_rows = left(full, inner_index, 1.0, keep_in=inner_keep)
    back_rows = left(full, full, -1.0)
    scale = 2.0 / (N * N)
    inner_cols = K - 1 + np.arange(C)
    pred_cols = np.zeros((2 * N, 2 * N))
    pred_cols[:N, :C] = scale * to_freq(inner_cols).T
    pred_cols[N:, C : 2 * C] = scale * to_freq(inner_cols).T
    pred_cols = np.concatenate(np_split(pred_cols), axis=0)
    res_cols = np.zeros((2 * N, 2 * N))
    res_cols[:C, :N] = to_freq(inner_cols)
    res_cols[C : 2 * C, N:] = to_freq(inner_cols)
    res_cols = np.concatenate(np_split(res_cols), axis=0)
    back_cols = wide(scale * to_freq(full).T)
    psf_rows = np.concatenate([np.concatenate([psf_rows[:N], psf_rows[:N]], axis=1),
                               np.concatenate([psf_rows[N:], np.zeros_like(psf_rows[N:])], axis=1)], axis=0)
    return (patch_cols, patch_rows, psf_cols, psf_rows, pred_rows, pred_cols, res_cols, res_rows,
            back_rows, back_cols)


def split(x):
    high = x.astype(BF16)
    return high, (x - high.astype(F32)).astype(BF16)


def dot(a, b):
    return jnp.dot(a, b, preferred_element_type=F32)


def right_wide(x, table_ref):
    high, low = split(x)
    both = dot(jnp.concatenate([high, low], axis=1), table_ref[...])
    return both[:, :N] + both[:, N:]


def right_three(x, table_ref):
    high, low = split(x)
    depth = x.shape[1]
    return (dot(high, table_ref[:depth, :]) + dot(low, table_ref[:depth, :])
            + dot(high, table_ref[depth:, :]))


def left_three(table_ref, x):
    rows = table_ref.shape[0] // 2
    high, low = split(x)
    both = dot(table_ref[...], high)
    return both[:rows] + both[rows:] + dot(table_ref[:rows, :], low)


def turned(y, sign):
    return pltpu.roll(y, 64, 1) * sign


def stacked(parts, sign):
    return jnp.concatenate(
        [jnp.concatenate([y, turned(y, sign)], axis=0) for y in parts], axis=1)


def exposure_kernel(first, meta_ref, slots_ref, ext_ref, *refs):
    if first:
        acc_in_ref = None
    else:
        acc_in_ref, refs = refs[0], refs[1:]
    (patch_cols, patch_rows, psf_cols, psf_rows, pred_rows, pred_cols, res_cols, res_rows,
     back_rows, back_cols, resid_ref, acc_ref) = refs
    step = pl.program_id(0)

    @pl.when(step == 0)
    def _():
        if first:
            acc_ref[...] = jnp.zeros_like(acc_ref)
        else:
            acc_ref[...] = acc_in_ref[...]

    lane = lax.broadcasted_iota(jnp.int32, (1, N), 1)
    sign = jnp.where(lane < 64, 1.0, -1.0).astype(F32)
    low_half = lane < 64

    places = []
    patches = []
    for e in range(GROUP):
        code = jnp.maximum(meta_ref[step * GROUP + e] - 1, 0)
        which = lax.shift_right_logical(code, 16)
        row = lax.bitwise_and(lax.shift_right_logical(code, 8), 255) + (EDGE - K + 1)
        column = lax.bitwise_and(code, 255) + (SIDE - K + 1)
        row_at = pl.multiple_of(lax.shift_left(lax.shift_right_logical(row, 3), 3), 8)
        col_at = pl.multiple_of(lax.shift_left(lax.shift_right_logical(column, 7), 7), 128)
        down = row - row_at
        over = column - col_at
        places.append((which, row_at, col_at, down, over))
        window = ext_ref[which, pl.ds(row_at, N + 8), pl.ds(col_at, 2 * N)]
        window = pltpu.roll(window, lax.bitwise_and(2 * N - over, 2 * N - 1), 1)[:, :N]
        window = pltpu.roll(window, jnp.where(down == 0, 0, N + 8 - down), 0)[:N]
        patches.append(window)

    y = right_wide(jnp.concatenate(patches, axis=0), patch_cols)
    z = left_three(patch_rows, stacked([y[e * N : e * N + N] for e in range(GROUP)], sign))

    pairs = []
    for e in range(GROUP):
        x = slots_ref[e, :PSF_ROWS, :]
        both = jnp.concatenate([pltpu.roll(x, 1, 0), x], axis=1)
        pairs.append(pltpu.roll(both, N, 1, stride=2, stride_axis=0)[:, :N])
    high, low = split(jnp.concatenate(pairs, axis=0))
    y = dot(jnp.concatenate([high, low], axis=1), psf_cols[: 2 * N, :]) + dot(high, psf_cols[2 * N :, :])
    y = stacked([jnp.concatenate([y[32 * e : 32 * e + 32, :N], y[32 * e : 32 * e + 32, N:]], axis=0)
                 for e in range(GROUP)], sign)
    high, low = split(y)
    khat = (dot(psf_rows[:N, :], jnp.concatenate([high, low], axis=0))
            + dot(psf_rows[N:, :N], high))

    kernels = []
    spec = []
    for e in range(GROUP):
        k = khat[:, e * N : e * N + N]
        rk = pltpu.roll(k, 64, 1)
        k_re = jnp.where(low_half, k, rk)
        k_im = jnp.where(low_half, -rk, k)
        kernels.append((k_re, k_im))
        p = z[:, e * N : e * N + N]
        rp = pltpu.roll(p, 64, 1)
        spec.append(jnp.concatenate(
            [p * k_re + rp * k_im, (rp * k_re - p * k_im) * sign], axis=0))
    u = left_three(pred_rows, jnp.concatenate(spec, axis=1))
    u = jnp.concatenate(
        [jnp.concatenate([u[:PAD, e * N : e * N + N], u[PAD:, e * N : e * N + N]], axis=1)
         for e in range(GROUP)], axis=0)
    predicted = right_three(u, pred_cols)

    number = lax.broadcasted_iota(jnp.int32, (PAD, 1), 0)
    last = number == PAIRS - 1
    turn = lax.bitwise_and(lane + 4 * number, N - 1)
    pairs = []
    for e in range(GROUP):
        image = pltpu.roll(predicted[e * PAD : e * PAD + PAD], 0, 1, stride=4, stride_axis=0)
        front, rear = image[:, :N], image[:, N:]
        flat = (jnp.where(last, 0.0, front) + pltpu.roll(rear, 1, 0)
                + pltpu.roll(jnp.where(last, front, 0.0), 2, 0))
        resid = slots_ref[e, VAR_AT : VAR_AT + PAD, :] * (flat - slots_ref[e, OBS_AT : OBS_AT + PAD, :])
        resid_ref[e] = resid
        front = jnp.take_along_axis(resid, turn, axis=1, mode="promise_in_bounds")
        rear = jnp.take_along_axis(pltpu.roll(resid, PAD - 1, 0), turn, axis=1, mode="promise_in_bounds")
        pairs.append(jnp.concatenate(
            [jnp.where(lane + 4 * number < N, front, rear),
             jnp.where(last, pltpu.roll(resid, PAD - 2, 0), rear)], axis=1))
    v = right_three(jnp.concatenate(pairs, axis=0), res_cols)
    v = [jnp.concatenate([v[e * PAD : e * PAD + PAD, :N], v[e * PAD : e * PAD + PAD, N:]], axis=0)
         for e in range(GROUP)]
    r = left_three(res_rows, stacked(v, sign))
    spec = []
    for e in range(GROUP):
        k_re, k_im = kernels[e]
        p = r[:, e * N : e * N + N]
        rp = pltpu.roll(p, 64, 1)
        spec.append(jnp.concatenate(
            [p * k_re - rp * k_im, (rp * k_re + p * k_im) * sign], axis=0))
    u = left_three(back_rows, jnp.concatenate(spec, axis=1))
    back = right_wide(jnp.concatenate([u[:, e * N : e * N + N] for e in range(GROUP)], axis=0), back_cols)
    for e in range(GROUP):
        which, row_at, col_at, down, over = places[e]
        image = jnp.concatenate([back[e * N : e * N + N], jnp.zeros((8, N), F32)], axis=0)
        image = pltpu.roll(image, down, 0)
        image = jnp.concatenate([image, jnp.zeros_like(image)], axis=1)
        image = pltpu.roll(image, over, 1)
        acc_ref[which, pl.ds(row_at, N + 8), pl.ds(col_at, 2 * N)] += image


def whole(shape):
    return pl.BlockSpec(shape, lambda i, meta: (0,) * len(shape), pipeline_mode=pl.Buffered(1))


def run_exposures(meta, slots, ext, acc, tables):
    number = slots.shape[0]
    first = acc is None
    operands = [slots, ext] + ([] if first else [acc]) + list(tables)
    in_specs = [pl.BlockSpec((GROUP, SLOT_ROWS, N), lambda i, meta: (i, 0, 0))]
    in_specs += [whole(o.shape) for o in operands[1:]]
    return pl.pallas_call(
        functools.partial(exposure_kernel, first),
        grid_spec=pltpu.PrefetchScalarGridSpec(
            num_scalar_prefetch=1,
            grid=(number // GROUP,),
            in_specs=in_specs,
            out_specs=[
                pl.BlockSpec((GROUP, PAD, N), lambda i, meta: (i, 0, 0)),
                whole(ext.shape),
            ],
        ),
        out_shape=[
            jax.ShapeDtypeStruct((number, PAD, N), F32),
            jax.ShapeDtypeStruct(ext.shape, F32),
        ],
        compiler_params=pltpu.CompilerParams(vmem_limit_bytes=LIMIT),
        cost_estimate=pl.CostEstimate(flops=number * 200_000_000, bytes_accessed=12_000_000, transcendentals=0),
    )(meta, *operands)


def three(x):
    high = x.astype(BF16)
    rest = x - high.astype(F32)
    middle = rest.astype(BF16)
    return jnp.concatenate([high, middle, (rest - middle.astype(F32)).astype(BF16)], axis=0)


def own_places(packed_ref, own):
    row = lax.shift_right_logical(packed_ref[pl.ds(own, 1), :], 19)
    count = row.shape[1]
    first = lax.broadcasted_iota(jnp.int32, (count, count), 0)
    second = lax.broadcasted_iota(jnp.int32, (count, count), 1)
    column = jnp.sum(jnp.where(first == second, row, 0), axis=1, keepdims=True)
    return row, column, first, second


def places_of_tile(packed_ref, own):
    packed = packed_ref[...]
    count = packed.shape[1]
    here = lax.shift_right_logical(packed, 19) == own
    code = lax.bitwise_and(packed, (1 << 19) - 1) + 1
    first = lax.broadcasted_iota(jnp.int32, (count, count), 0)
    second = lax.broadcasted_iota(jnp.int32, (count, count), 1)
    earlier = (first < second).astype(F32).astype(BF16)
    rank = dot(here.astype(F32).astype(BF16), earlier)
    return jnp.concatenate(
        [jnp.sum(jnp.where(jnp.logical_and(here, rank == float(s)), code, 0), axis=1, keepdims=True)
         for s in range(CAP)], axis=1)


def neighbours(n_ra, n_dec):
    ra, dec = lax.axis_index("ra"), lax.axis_index("dec")
    up, down = lax.rem(ra + 1, n_ra), lax.rem(ra + n_ra - 1, n_ra)
    right, left = lax.rem(dec + 1, n_dec), lax.rem(dec + n_dec - 1, n_dec)
    return ra, dec, up, down, right, left


def greet(n_dec, ra, dec, up, down, right, left):
    barrier = pltpu.get_barrier_semaphore()
    for other in ((up, dec), (down, dec), (up, right), (up, left), (down, right), (down, left)):
        pl.semaphore_signal(barrier, inc=1, device_id=other, device_id_type=MESH)
    for d in range(1, n_dec):
        pl.semaphore_signal(barrier, inc=1, device_id=(ra, lax.rem(dec + d, n_dec)), device_id_type=MESH)
    pl.semaphore_wait(barrier, n_dec + 5)


def edges(n_ra, n_dec, ra, dec):
    zero, one = jnp.zeros((), F32), jnp.ones((), F32)
    return (jnp.where(ra > 0, one, zero), jnp.where(ra < n_ra - 1, one, zero),
            jnp.where(dec > 0, one, zero), jnp.where(dec < n_dec - 1, one, zero))


def sender(send, recv):
    def copy(index, src, dst, other):
        return pltpu.make_async_remote_copy(
            src_ref=src, dst_ref=dst, send_sem=send.at[index], recv_sem=recv.at[index],
            device_id=other, device_id_type=MESH)
    return copy


def far_first(n_dec):
    return sorted(range(1, n_dec), key=lambda d: -(min(d // 4, 4 - d // 4) + min(d % 4, 4 - d % 4)))


def exchange_kernel(n_ra, n_dec, packed_ref, psf_ref, obs_ref, var_ref, model_ref,
                    meta_ref, slots_ref, ext_ref,
                    leaving, to_right, to_left, from_left, from_right, corners, send, recv, send_slot, recv_slot):
    ra, dec, up, down, right, left = neighbours(n_ra, n_dec)
    greet(n_dec, ra, dec, up, down, right, left)
    tra, tdec = model_ref.shape[1], model_ref.shape[2]
    top, side_at = EDGE + tra, SIDE + tdec
    low_half = lax.broadcasted_iota(jnp.int32, (1, N), 1) < 64
    copy = sender(send, recv)
    copies = [
        copy(0, model_ref.at[:, tra - EDGE :, :], ext_ref.at[:, :EDGE, SIDE:side_at], (up, dec)),
        copy(1, model_ref.at[:, :EDGE, :], ext_ref.at[:, top:, SIDE:side_at], (down, dec)),
    ]
    for c in copies:
        c.start()
    for q in range(3):
        to_right[q] = jnp.where(
            low_half, pltpu.roll(model_ref[2 * q + 1, :, tdec - N :], 64, 1), model_ref[2 * q, :, tdec - N :])
    more = [
        copy(2, to_right, from_left, (ra, right)),
        copy(4, to_right.at[:, tra - EDGE :, :], corners.at[0], (up, right)),
        copy(5, to_right.at[:, :EDGE, :], corners.at[1], (down, right)),
    ]
    for c in more:
        c.start()
    copies += more
    for q in range(3):
        to_left[q] = jnp.where(
            low_half, model_ref[2 * q, :, :N], pltpu.roll(model_ref[2 * q + 1, :, :N], 64, 1))
    more = [
        copy(3, to_left, from_right, (ra, left)),
        copy(6, to_left.at[:, tra - EDGE :, :], corners.at[2], (up, left)),
        copy(7, to_left.at[:, :EDGE, :], corners.at[3], (down, left)),
    ]
    for c in more:
        c.start()
    copies += more

    row, column, first, second = own_places(packed_ref, dec)
    count = row.shape[1]
    slots = CAP * n_dec
    rank = jnp.sum(jnp.where(jnp.logical_and(column == row, first < second), 1, 0), axis=0, keepdims=True)
    place = row * CAP + rank
    chosen = (lax.broadcasted_iota(jnp.int32, (slots, count), 0) == place).astype(F32).astype(BF16)
    chosen = jnp.concatenate([chosen] * 3, axis=1)
    for ref, base, rows in ((psf_ref, 0, PSF_ROWS), (obs_ref, OBS_AT, PAD), (var_ref, VAR_AT, PAD)):
        width = ref.shape[1]
        for start in range(0, rows, 4):
            end = min((start + 4) * N, width)
            if start * N < width:
                y = dot(chosen, three(ref[:, start * N : end]))
                if end < (start + 4) * N:
                    y = jnp.concatenate([y, jnp.zeros((slots, (start + 4) * N - end), F32)], axis=1)
            else:
                y = jnp.zeros((slots, 4 * N), F32)
            for t in range(4):
                leaving[pl.ds(base + start + t, slots, stride=SLOT_ROWS), :] = y[:, t * N : t * N + N]
    size = CAP * SLOT_ROWS
    slot_copy = sender(send_slot, recv_slot)
    moves = []
    for d in far_first(n_dec):
        other = lax.rem(dec + d, n_dec)
        moves.append(slot_copy(
            d, leaving.at[pl.ds(pl.multiple_of(other * size, 8), size), :],
            slots_ref.at[pl.ds(pl.multiple_of(dec * size, 8), size), :], (ra, other)))
        moves[-1].start()
    here = pl.ds(pl.multiple_of(dec * size, 8), size)
    slots_ref[here, :] = leaving[here, :]
    ext_ref[:, EDGE:top, SIDE:side_at] = model_ref[...]
    meta_ref[...] = places_of_tile(packed_ref, dec)
    for c in copies:
        c.wait()
    in_low, in_high, in_left, in_right = edges(n_ra, n_dec, ra, dec)

    @pl.when(ra == 0)
    def _():
        ext_ref[:, :EDGE, SIDE:side_at] = jnp.zeros((ext_ref.shape[0], EDGE, tdec), F32)

    @pl.when(ra == n_ra - 1)
    def _():
        ext_ref[:, top:, SIDE:side_at] = jnp.zeros((ext_ref.shape[0], EDGE, tdec), F32)

    for q in range(3):
        for src, rows, col, scale in (
            (from_left.at[q], slice(EDGE, top), slice(0, SIDE), in_left),
            (from_right.at[q], slice(EDGE, top), slice(side_at, side_at + SIDE), in_right),
            (corners.at[0, q], slice(0, EDGE), slice(0, SIDE), in_low * in_left),
            (corners.at[1, q], slice(top, top + EDGE), slice(0, SIDE), in_high * in_left),
            (corners.at[2, q], slice(0, EDGE), slice(side_at, side_at + SIDE), in_low * in_right),
            (corners.at[3, q], slice(top, top + EDGE), slice(side_at, side_at + SIDE), in_high * in_right),
        ):
            value = src[...] * scale
            ext_ref[2 * q, rows, col] = value
            ext_ref[2 * q + 1, rows, col] = pltpu.roll(value, 64, 1)
    for c in moves:
        c.wait()


def vmem(count):
    return [pl.BlockSpec(memory_space=pltpu.VMEM)] * count


def exchange(packed, psf, obs, var, model, n_ra, n_dec):
    bands, tra, tdec = model.shape
    strip = pltpu.VMEM((3, tra, N), F32)
    size = n_dec * CAP * SLOT_ROWS
    return pl.pallas_call(
        functools.partial(exchange_kernel, n_ra, n_dec),
        out_shape=[
            jax.ShapeDtypeStruct((n_dec, CAP), jnp.int32),
            jax.ShapeDtypeStruct((size, N), F32),
            jax.ShapeDtypeStruct((bands, tra + 2 * EDGE, tdec + 2 * SIDE), F32),
        ],
        in_specs=vmem(5),
        out_specs=vmem(3),
        scratch_shapes=[pltpu.VMEM((size, N), F32), strip, strip, strip, strip, pltpu.VMEM((4, 3, EDGE, N), F32),
                        pltpu.SemaphoreType.DMA((8,)), pltpu.SemaphoreType.DMA((8,)),
                        pltpu.SemaphoreType.DMA((n_dec,)), pltpu.SemaphoreType.DMA((n_dec,))],
        compiler_params=pltpu.CompilerParams(
            collective_id=0, has_side_effects=True, vmem_limit_bytes=LIMIT),
        cost_estimate=pl.CostEstimate(flops=0, bytes_accessed=40_000_000, transcendentals=0),
    )(packed, psf, obs, var, model)


def return_kernel(n_ra, n_dec, packed_ref, resid_ref, acc_ref, residual_ref, out_ref, landed, to_right, to_left,
                  from_left, from_right, out_corners, corners, from_up, from_down, send, recv, send_slot, recv_slot):
    ra, dec, up, down, right, left = neighbours(n_ra, n_dec)
    greet(n_dec, ra, dec, up, down, right, left)
    tra, tdec = out_ref.shape[1], out_ref.shape[2]
    top, side_at = EDGE + tra, SIDE + tdec
    low_half = lax.broadcasted_iota(jnp.int32, (1, N), 1) < 64
    copy = sender(send, recv)
    copies = [
        copy(0, acc_ref.at[:, :EDGE, SIDE:side_at], from_up, (down, dec)),
        copy(1, acc_ref.at[:, top:, SIDE:side_at], from_down, (up, dec)),
    ]
    for c in copies:
        c.start()

    def pack_left(q, rows):
        return jnp.where(low_half, pltpu.roll(acc_ref[2 * q + 1, rows, :SIDE], 64, 1), acc_ref[2 * q, rows, :SIDE])

    def pack_right(q, rows):
        return jnp.where(low_half, acc_ref[2 * q, rows, side_at:], pltpu.roll(acc_ref[2 * q + 1, rows, side_at:], 64, 1))

    middle, lower, upper = slice(EDGE, top), slice(0, EDGE), slice(top, top + EDGE)
    for q in range(3):
        to_left[q] = pack_left(q, middle)
    more = [copy(2, to_left, from_right, (ra, left))]
    more[0].start()
    copies += more
    for q in range(3):
        to_right[q] = pack_right(q, middle)
    more = [copy(3, to_right, from_left, (ra, right))]
    more[0].start()
    copies += more
    for q in range(3):
        out_corners[0, q] = pack_left(q, lower)
        out_corners[1, q] = pack_left(q, upper)
        out_corners[2, q] = pack_right(q, lower)
        out_corners[3, q] = pack_right(q, upper)
    more = [
        copy(4, out_corners.at[0], corners.at[0], (down, left)),
        copy(5, out_corners.at[1], corners.at[1], (up, left)),
        copy(6, out_corners.at[2], corners.at[2], (down, right)),
        copy(7, out_corners.at[3], corners.at[3], (up, right)),
    ]
    for c in more:
        c.start()
    copies += more
    size = CAP * PAD
    slot_copy = sender(send_slot, recv_slot)
    moves = []
    here = pl.ds(pl.multiple_of(dec * size, 8), size)
    for d in far_first(n_dec):
        other = lax.rem(dec + d, n_dec)
        moves.append(slot_copy(
            d, resid_ref.at[pl.ds(pl.multiple_of(other * size, 8), size), :], landed.at[here, :], (ra, other)))
        moves[-1].start()
    landed[here, :] = resid_ref[here, :]
    out_ref[...] = acc_ref[:, EDGE:top, SIDE:side_at]
    for c in copies:
        c.wait()
    in_low, in_high, in_left, in_right = edges(n_ra, n_dec, ra, dec)
    out_ref[:, tra - EDGE :, :] += from_up[...] * in_high
    out_ref[:, :EDGE, :] += from_down[...] * in_low
    every, low_rows, high_rows = slice(0, tra), slice(0, EDGE), slice(tra - EDGE, tra)
    for q in range(3):
        for src, rows, scale, at_right in (
            (from_right.at[q], every, in_right, True),
            (from_left.at[q], every, in_left, False),
            (corners.at[0, q], high_rows, in_high * in_right, True),
            (corners.at[1, q], low_rows, in_low * in_right, True),
            (corners.at[2, q], high_rows, in_high * in_left, False),
            (corners.at[3, q], low_rows, in_low * in_left, False),
        ):
            value = src[...] * scale
            other = pltpu.roll(value, 64, 1)
            if at_right:
                cols, keep = slice(tdec - N, tdec), jnp.logical_not(low_half)
            else:
                cols, keep = slice(0, N), low_half
            out_ref[2 * q, rows, cols] += jnp.where(keep, value, 0.0)
            out_ref[2 * q + 1, rows, cols] += jnp.where(keep, other, 0.0)
    for c in moves:
        c.wait()
    row, column, first, second = own_places(packed_ref, dec)
    count = row.shape[1]
    slots = CAP * n_dec
    rank = jnp.sum(jnp.where(jnp.logical_and(column == row, second < first), 1, 0), axis=1, keepdims=True)
    place = column * CAP + rank
    chosen = (lax.broadcasted_iota(jnp.int32, (count, slots), 1) == place).astype(F32).astype(BF16)
    chosen = jnp.concatenate([chosen] * 3, axis=1)
    width = residual_ref.shape[1]
    for start in range(0, PAD, 4):
        if start * N >= width:
            break
        x = jnp.concatenate(
            [landed[pl.ds(start + t, slots, stride=PAD), :] for t in range(4)], axis=1)
        y = dot(chosen, three(x))
        end = min((start + 4) * N, width)
        residual_ref[:, start * N : end] = y[:, : end - start * N]


def give_back(packed, resid, acc, n_ra, n_dec):
    bands, tra, tdec = acc.shape[0], acc.shape[1] - 2 * EDGE, acc.shape[2] - 2 * SIDE
    strip = pltpu.VMEM((3, tra, N), F32)
    corner = pltpu.VMEM((4, 3, EDGE, N), F32)
    band = pltpu.VMEM((bands, EDGE, tdec), F32)
    size = n_dec * CAP * PAD
    return pl.pallas_call(
        functools.partial(return_kernel, n_ra, n_dec),
        out_shape=[jax.ShapeDtypeStruct((packed.shape[1], C * C), F32),
                   jax.ShapeDtypeStruct((bands, tra, tdec), F32)],
        in_specs=vmem(3),
        out_specs=vmem(2),
        scratch_shapes=[pltpu.VMEM((size, N), F32), strip, strip, strip, strip, corner, corner, band, band,
                        pltpu.SemaphoreType.DMA((8,)), pltpu.SemaphoreType.DMA((8,)),
                        pltpu.SemaphoreType.DMA((n_dec,)), pltpu.SemaphoreType.DMA((n_dec,))],
        compiler_params=pltpu.CompilerParams(
            collective_id=1, has_side_effects=True, vmem_limit_bytes=LIMIT),
        cost_estimate=pl.CostEstimate(flops=0, bytes_accessed=40_000_000, transcendentals=0),
    )(packed, resid, acc)


def body(model, observed, inv_var, psf, target_dec, band, offset_ra, offset_dec):
    n_ra, n_dec = lax.axis_size("ra"), lax.axis_size("dec")
    e_dev = observed.shape[0]
    packed = (((target_dec[:, 0] * 8 + band) * 256 + offset_ra) * 256 + offset_dec).reshape(n_dec, e_dev)
    meta, slots, ext = exchange(packed, psf, observed, inv_var, model, n_ra, n_dec)
    tables = [jnp.asarray(t) for t in make_tables()]
    resid, acc = run_exposures(meta.reshape(-1), slots.reshape(n_dec * CAP, SLOT_ROWS, N), ext, None, tables)
    residual, gradient = give_back(packed, resid.reshape(n_dec * CAP * PAD, N), acc, n_ra, n_dec)
    return residual, gradient


def solution(mesh):
    placed = (
        P(None, "ra", "dec"),
        P(("ra", "dec"), None),
        P(("ra", "dec"), None),
        P(("ra", "dec"), None),
        P("ra", None),
        P("ra"),
        P("ra"),
        P("ra"),
    )
    return jax.shard_map(
        body,
        mesh=mesh,
        in_specs=placed,
        out_specs=(P(("ra", "dec"), None), P(None, "ra", "dec")),
        check_vma=False,
    )
```

```python
import functools
import math

import jax
import jax.numpy as jnp
import ml_dtypes
import numpy as np
from jax import lax
from jax.experimental import pallas as pl
from jax.experimental.pallas import tpu as pltpu
from jax.sharding import PartitionSpec as P

K = 63
C = 66
CAP = 4
GROUP = 8
N = 128
PAIRS = 33
PAD = 40
PSF_ROWS = 32
EDGE = 64
SIDE = 128
LIMIT = 60 * 1024 * 1024
MESH = pl.DeviceIdType.MESH
F32 = jnp.float32
BF16 = jnp.bfloat16


def np_split(table):
    high = table.astype(np.float32).astype(ml_dtypes.bfloat16)
    low = (table - high.astype(np.float64)).astype(np.float32).astype(ml_dtypes.bfloat16)
    return high, low


def make_tables():
    theta = 2.0 * math.pi * (np.arange(64) + 0.5) / N

    def to_freq(columns):
        angle = np.asarray(columns)[:, None] * theta[None, :]
        return np.concatenate([np.cos(angle), -np.sin(angle)], axis=1)

    def rows_cs(out_index, in_index, sign):
        angle = 2.0 * math.pi * ((out_index[:, None] * in_index[None, :]) % N) / N
        return np.cos(angle), sign * np.sin(angle)

    full = np.arange(N)
    zero = np.zeros((N, N))
    zero16 = zero.astype(ml_dtypes.bfloat16)

    def wide(table):
        high, low = np_split(table)
        return np.block([[high, low], [high, zero16]])

    patch_cols = wide(to_freq(full))
    psf_cols = np.zeros((N, 2 * N))
    psf_cols[:K, :N] = to_freq(np.arange(K))
    psf_cols[K : 2 * K, N:] = to_freq(np.arange(K))
    psf_h, psf_l = np_split(psf_cols)
    psf_cols = np.concatenate([psf_h, psf_h, psf_l], axis=0)

    def left(out_index, in_index, sign, keep_in=None, keep_out=None):
        cosine, sine = rows_cs(out_index, in_index, sign)
        table = np.concatenate([cosine, sine], axis=1)
        if keep_in is not None:
            table = table * np.concatenate([keep_in, keep_in])[None, :]
        if keep_out is not None:
            table = table * keep_out[:, None]
        return np.concatenate(np_split(table), axis=0)

    patch_rows = left(full, full, 1.0)
    psf_index = np.concatenate([2 * np.arange(32), 2 * np.arange(32) + 1])
    psf_rows = left(full, psf_index, 1.0, keep_in=(psf_index < K).astype(np.float64))
    within = (np.arange(PAD) < PAIRS).astype(np.float64)
    inner_keep = np.concatenate([within, within])
    inner_index = np.concatenate([K - 1 + 2 * np.arange(PAD), K + 2 * np.arange(PAD)])
    pred_rows = left(inner_index, full, -1.0, keep_out=inner_keep)
    res_rows = left(full, inner_index, 1.0, keep_in=inner_keep)
    back_rows = left(full, full, -1.0)
    scale = 2.0 / (N * N)
    inner_cols = K - 1 + np.arange(C)
    pred_cols = np.zeros((2 * N, 2 * N))
    pred_cols[:N, :C] = scale * to_freq(inner_cols).T
    pred_cols[N:, C : 2 * C] = scale * to_freq(inner_cols).T
    pred_cols = np.concatenate(np_split(pred_cols), axis=0)
    res_cols = np.zeros((2 * N, 2 * N))
    res_cols[:C, :N] = to_freq(inner_cols)
    res_cols[C : 2 * C, N:] = to_freq(inner_cols)
    res_cols = np.concatenate(np_split(res_cols), axis=0)
    back_cols = wide(scale * to_freq(full).T)
    psf_rows = np.concatenate([np.concatenate([psf_rows[:N], psf_rows[:N]], axis=1),
                               np.concatenate([psf_rows[N:], np.zeros_like(psf_rows[N:])], axis=1)], axis=0)
    return (patch_cols, patch_rows, psf_cols, psf_rows, pred_rows, pred_cols, res_cols, res_rows,
            back_rows, back_cols)


def split(x):
    high = x.astype(BF16)
    return high, (x - high.astype(F32)).astype(BF16)


def dot(a, b):
    return jnp.dot(a, b, preferred_element_type=F32)


def right_wide(x, table_ref):
    high, low = split(x)
    both = dot(jnp.concatenate([high, low], axis=1), table_ref[...])
    return both[:, :N] + both[:, N:]


def right_three(x, table_ref):
    high, low = split(x)
    depth = x.shape[1]
    return (dot(high, table_ref[:depth, :]) + dot(low, table_ref[:depth, :])
            + dot(high, table_ref[depth:, :]))


def left_three(table_ref, x):
    rows = table_ref.shape[0] // 2
    high, low = split(x)
    both = dot(table_ref[...], high)
    return both[:rows] + both[rows:] + dot(table_ref[:rows, :], low)


def turned(y, sign):
    return pltpu.roll(y, 64, 1) * sign


def stacked(parts, sign):
    return jnp.concatenate(
        [jnp.concatenate([y, turned(y, sign)], axis=0) for y in parts], axis=1)


def lanes():
    lane = lax.broadcasted_iota(jnp.int32, (1, N), 1)
    return lane, jnp.where(lane < 64, 1.0, -1.0).astype(F32), lane < 64


def place_of(code):
    code = jnp.maximum(code - 1, 0)
    which = lax.shift_right_logical(code, 16)
    row = lax.bitwise_and(lax.shift_right_logical(code, 8), 255) + (EDGE - K + 1)
    column = lax.bitwise_and(code, 255) + (SIDE - K + 1)
    row_at = pl.multiple_of(lax.shift_left(lax.shift_right_logical(row, 3), 3), 8)
    col_at = pl.multiple_of(lax.shift_left(lax.shift_right_logical(column, 7), 7), 128)
    return which, row_at, col_at, row - row_at, column - col_at


def halves(k, low_half):
    rk = pltpu.roll(k, 64, 1)
    return jnp.where(low_half, k, rk), jnp.where(low_half, -rk, k)


def predict(patches, psfs, tables):
    patch_cols, patch_rows, psf_cols, psf_rows, pred_rows, pred_cols = tables
    count = len(patches)
    lane, sign, low_half = lanes()
    y = right_wide(jnp.concatenate(patches, axis=0), patch_cols)
    z = left_three(patch_rows, stacked([y[e * N : e * N + N] for e in range(count)], sign))
    pairs = []
    for x in psfs:
        both = jnp.concatenate([pltpu.roll(x, 1, 0), x], axis=1)
        pairs.append(pltpu.roll(both, N, 1, stride=2, stride_axis=0)[:, :N])
    high, low = split(jnp.concatenate(pairs, axis=0))
    y = dot(jnp.concatenate([high, low], axis=1), psf_cols[: 2 * N, :]) + dot(high, psf_cols[2 * N :, :])
    y = stacked([jnp.concatenate([y[32 * e : 32 * e + 32, :N], y[32 * e : 32 * e + 32, N:]], axis=0)
                 for e in range(count)], sign)
    high, low = split(y)
    khat = (dot(psf_rows[:N, :], jnp.concatenate([high, low], axis=0))
            + dot(psf_rows[N:, :N], high))
    khat = [khat[:, e * N : e * N + N] for e in range(count)]
    spec = []
    for e in range(count):
        k_re, k_im = halves(khat[e], low_half)
        p = z[:, e * N : e * N + N]
        rp = pltpu.roll(p, 64, 1)
        spec.append(jnp.concatenate(
            [p * k_re + rp * k_im, (rp * k_re - p * k_im) * sign], axis=0))
    u = left_three(pred_rows, jnp.concatenate(spec, axis=1))
    u = jnp.concatenate(
        [jnp.concatenate([u[:PAD, e * N : e * N + N], u[PAD:, e * N : e * N + N]], axis=1)
         for e in range(count)], axis=0)
    predicted = right_three(u, pred_cols)
    last = lax.broadcasted_iota(jnp.int32, (PAD, 1), 0) == PAIRS - 1
    flat = []
    for e in range(count):
        image = pltpu.roll(predicted[e * PAD : e * PAD + PAD], 0, 1, stride=4, stride_axis=0)
        front, rear = image[:, :N], image[:, N:]
        flat.append(jnp.where(last, 0.0, front) + pltpu.roll(rear, 1, 0)
                    + pltpu.roll(jnp.where(last, front, 0.0), 2, 0))
    return khat, flat


def adjoint(resids, khat, tables):
    res_cols, res_rows, back_rows, back_cols = tables
    count = len(resids)
    lane, sign, low_half = lanes()
    number = lax.broadcasted_iota(jnp.int32, (PAD, 1), 0)
    last = number == PAIRS - 1
    turn = lax.bitwise_and(lane + 4 * number, N - 1)
    pairs = []
    for resid in resids:
        front = jnp.take_along_axis(resid, turn, axis=1, mode="promise_in_bounds")
        rear = jnp.take_along_axis(pltpu.roll(resid, PAD - 1, 0), turn, axis=1, mode="promise_in_bounds")
        pairs.append(jnp.concatenate(
            [jnp.where(lane + 4 * number < N, front, rear),
             jnp.where(last, pltpu.roll(resid, PAD - 2, 0), rear)], axis=1))
    v = right_three(jnp.concatenate(pairs, axis=0), res_cols)
    v = [jnp.concatenate([v[e * PAD : e * PAD + PAD, :N], v[e * PAD : e * PAD + PAD, N:]], axis=0)
         for e in range(count)]
    r = left_three(res_rows, stacked(v, sign))
    spec = []
    for e in range(count):
        k_re, k_im = halves(khat[e], low_half)
        p = r[:, e * N : e * N + N]
        rp = pltpu.roll(p, 64, 1)
        spec.append(jnp.concatenate(
            [p * k_re - rp * k_im, (rp * k_re + p * k_im) * sign], axis=0))
    u = left_three(back_rows, jnp.concatenate(spec, axis=1))
    back = right_wide(jnp.concatenate([u[:, e * N : e * N + N] for e in range(count)], axis=0), back_cols)
    return [back[e * N : e * N + N] for e in range(count)]


def three(x):
    high = x.astype(BF16)
    rest = x - high.astype(F32)
    middle = rest.astype(BF16)
    return jnp.concatenate([high, middle, (rest - middle.astype(F32)).astype(BF16)], axis=0)


def own_places(packed_ref, own):
    row = lax.shift_right_logical(packed_ref[pl.ds(own, 1), :], 19)
    count = row.shape[1]
    first = lax.broadcasted_iota(jnp.int32, (count, count), 0)
    second = lax.broadcasted_iota(jnp.int32, (count, count), 1)
    column = jnp.sum(jnp.where(first == second, row, 0), axis=1, keepdims=True)
    return row, column, first, second


def places_of_tile(packed_ref, own):
    packed = packed_ref[...]
    count = packed.shape[1]
    here = lax.shift_right_logical(packed, 19) == own
    code = lax.bitwise_and(packed, (1 << 19) - 1) + 1
    first = lax.broadcasted_iota(jnp.int32, (count, count), 0)
    second = lax.broadcasted_iota(jnp.int32, (count, count), 1)
    earlier = (first < second).astype(F32).astype(BF16)
    rank = dot(here.astype(F32).astype(BF16), earlier)
    return jnp.concatenate(
        [jnp.sum(jnp.where(jnp.logical_and(here, rank == float(s)), code, 0), axis=1, keepdims=True)
         for s in range(CAP)], axis=1)


def neighbours(n_ra, n_dec):
    ra, dec = lax.axis_index("ra"), lax.axis_index("dec")
    up, down = lax.rem(ra + 1, n_ra), lax.rem(ra + n_ra - 1, n_ra)
    right, left = lax.rem(dec + 1, n_dec), lax.rem(dec + n_dec - 1, n_dec)
    return ra, dec, up, down, right, left


def greet(n_dec, ra, dec, up, down, right, left):
    barrier = pltpu.get_barrier_semaphore()
    for other in ((up, dec), (down, dec), (up, right), (up, left), (down, right), (down, left)):
        pl.semaphore_signal(barrier, inc=1, device_id=other, device_id_type=MESH)
    for d in range(1, n_dec):
        pl.semaphore_signal(barrier, inc=1, device_id=(ra, lax.rem(dec + d, n_dec)), device_id_type=MESH)
    pl.semaphore_wait(barrier, n_dec + 5)


def greet_near(ra, dec, up, down, right, left):
    barrier = pltpu.get_barrier_semaphore()
    for other in ((up, dec), (down, dec), (ra, right), (ra, left),
                  (up, right), (up, left), (down, right), (down, left)):
        pl.semaphore_signal(barrier, inc=1, device_id=other, device_id_type=MESH)
    pl.semaphore_wait(barrier, 8)


def edges(n_ra, n_dec, ra, dec):
    zero, one = jnp.zeros((), F32), jnp.ones((), F32)
    return (jnp.where(ra > 0, one, zero), jnp.where(ra < n_ra - 1, one, zero),
            jnp.where(dec > 0, one, zero), jnp.where(dec < n_dec - 1, one, zero))


def sender(send, recv):
    def copy(index, src, dst, other):
        return pltpu.make_async_remote_copy(
            src_ref=src, dst_ref=dst, send_sem=send.at[index], recv_sem=recv.at[index],
            device_id=other, device_id_type=MESH)
    return copy


def rows_of(index, size):
    return pl.ds(pl.multiple_of(index * size, 8), size)


def slot_chooser(packed_ref, dec, n_dec):
    row, column, first, second = own_places(packed_ref, dec)
    count = row.shape[1]
    slots = CAP * n_dec
    rank = jnp.sum(jnp.where(jnp.logical_and(column == row, first < second), 1, 0), axis=0, keepdims=True)
    place = row * CAP + rank
    chosen = (lax.broadcasted_iota(jnp.int32, (slots, count), 0) == place).astype(F32).astype(BF16)
    return jnp.concatenate([chosen] * 3, axis=1)


def to_slots(chosen, ref, out_ref, rows):
    width, slots = ref.shape[1], chosen.shape[0]
    for start in range(0, rows, 4):
        end = min((start + 4) * N, width)
        if start * N < width:
            y = dot(chosen, three(ref[:, start * N : end]))
            if end < (start + 4) * N:
                y = jnp.concatenate([y, jnp.zeros((slots, (start + 4) * N - end), F32)], axis=1)
        else:
            y = jnp.zeros((slots, 4 * N), F32)
        for t in range(4):
            out_ref[pl.ds(start + t, slots, stride=rows), :] = y[:, t * N : t * N + N]


def exchange_kernel(n_ra, n_dec, packed_ref, psf_ref, model_ref, psf_in, ext_ref,
                    to_right, to_left, from_left, from_right, corners, psf_out, send, recv, send_psf, recv_psf):
    ra, dec, up, down, right, left = neighbours(n_ra, n_dec)
    greet(n_dec, ra, dec, up, down, right, left)
    tra, tdec = model_ref.shape[1], model_ref.shape[2]
    top = EDGE + tra
    low_half = lax.broadcasted_iota(jnp.int32, (1, N), 1) < 64
    copy = sender(send, recv)
    copies = [
        copy(8 * t, model_ref.at[:, tra - EDGE :, t * N : t * N + N], ext_ref.at[:, 1 + t, :EDGE, :], (up, dec))
        for t in range(2)
    ] + [
        copy(1 + 8 * t, model_ref.at[:, :EDGE, t * N : t * N + N], ext_ref.at[:, 1 + t, top:, :], (down, dec))
        for t in range(2)
    ]
    for c in copies:
        c.start()
    for q in range(3):
        to_right[q] = jnp.where(
            low_half, pltpu.roll(model_ref[2 * q + 1, :, tdec - N :], 64, 1), model_ref[2 * q, :, tdec - N :])
    more = [
        copy(2, to_right, from_left, (ra, right)),
        copy(4, to_right.at[:, tra - EDGE :, :], corners.at[0], (up, right)),
        copy(5, to_right.at[:, :EDGE, :], corners.at[1], (down, right)),
    ]
    for c in more:
        c.start()
    copies += more
    for q in range(3):
        to_left[q] = jnp.where(
            low_half, model_ref[2 * q, :, :N], pltpu.roll(model_ref[2 * q + 1, :, :N], 64, 1))
    more = [
        copy(3, to_left, from_right, (ra, left)),
        copy(6, to_left.at[:, tra - EDGE :, :], corners.at[2], (up, left)),
        copy(7, to_left.at[:, :EDGE, :], corners.at[3], (down, left)),
    ]
    for c in more:
        c.start()
    copies += more

    def psf_move(d):
        tile = lax.rem(dec + d, n_dec)
        return sender(send_psf, recv_psf)(
            d, psf_out.at[rows_of(tile, CAP * PSF_ROWS), :], psf_in.at[rows_of(dec, CAP * PSF_ROWS), :], (ra, tile))

    to_slots(slot_chooser(packed_ref, dec, n_dec), psf_ref, psf_out, PSF_ROWS)

    def start_psf(d, carry):
        psf_move(d).start()
        return carry

    lax.fori_loop(1, n_dec, start_psf, 0)
    psf_in[rows_of(dec, CAP * PSF_ROWS), :] = psf_out[rows_of(dec, CAP * PSF_ROWS), :]
    for t in range(2):
        ext_ref[:, 1 + t, EDGE:top, :] = model_ref[:, :, t * N : t * N + N]
    for c in copies:
        c.wait()
    in_low, in_high, in_left, in_right = edges(n_ra, n_dec, ra, dec)

    @pl.when(ra == 0)
    def _():
        ext_ref[:, 1:3, :EDGE, :] = jnp.zeros((ext_ref.shape[0], 2, EDGE, N), F32)

    @pl.when(ra == n_ra - 1)
    def _():
        ext_ref[:, 1:3, top:, :] = jnp.zeros((ext_ref.shape[0], 2, EDGE, N), F32)

    for q in range(3):
        for src, rows, col, scale in (
            (from_left.at[q], slice(EDGE, top), 0, in_left),
            (from_right.at[q], slice(EDGE, top), 3, in_right),
            (corners.at[0, q], slice(0, EDGE), 0, in_low * in_left),
            (corners.at[1, q], slice(top, top + EDGE), 0, in_high * in_left),
            (corners.at[2, q], slice(0, EDGE), 3, in_low * in_right),
            (corners.at[3, q], slice(top, top + EDGE), 3, in_high * in_right),
        ):
            value = src[...] * scale
            ext_ref[2 * q, col, rows, :] = value
            ext_ref[2 * q + 1, col, rows, :] = pltpu.roll(value, 64, 1)

    def end_psf(d, carry):
        psf_move(d).wait()
        return carry

    lax.fori_loop(1, n_dec, end_psf, 0)


def photometry_kernel(n_ra, n_dec, packed_ref, obs_ref, var_ref, psf_in, patch_ref, *refs):
    tables, refs = refs[:10], refs[10:]
    (back_ref, residual_ref, obs_slots, var_slots, pred_out, pred_in, resid_in, khat_ref,
     send_pred, recv_pred, send_res, recv_res) = refs
    ra, dec = lax.axis_index("ra"), lax.axis_index("dec")
    barrier = pltpu.get_barrier_semaphore()
    for d in range(1, n_dec):
        pl.semaphore_signal(barrier, inc=1, device_id=(ra, lax.rem(dec + d, n_dec)), device_id_type=MESH)
    chosen = slot_chooser(packed_ref, dec, n_dec)
    to_slots(chosen, obs_ref, obs_slots, PAD)
    to_slots(chosen, var_ref, var_slots, PAD)
    pl.semaphore_wait(barrier, n_dec - 1)

    def pred_move(d):
        owner = lax.rem(dec + n_dec - d, n_dec)
        return sender(send_pred, recv_pred)(
            d, pred_out.at[rows_of(owner, CAP * PAD), :], pred_in.at[rows_of(dec, CAP * PAD), :], (ra, owner))

    def res_move(d):
        tile = lax.rem(dec + d, n_dec)
        return sender(send_res, recv_res)(
            d, residual_ref.at[rows_of(tile, CAP * PAD), :], resid_in.at[rows_of(dec, CAP * PAD), :], (ra, tile))

    per = GROUP // CAP
    steps = n_dec // per

    def each(j, move, what):
        for i in range(per):
            d = j * per + i
            if i == 0:
                @pl.when(j > 0)
                def _():
                    what(move(d))
            else:
                what(move(d))

    def owned(j):
        return [(lax.rem(dec + 2 * n_dec - (j * per + e // CAP), n_dec), e % CAP) for e in range(GROUP)]

    def step(j, carry):
        @pl.when(j < steps)
        def _():
            which = owned(j)
            khat, flat = predict(
                [patch_ref[o * CAP + s] for o, s in which],
                [psf_in[rows_of(o * CAP + s, PSF_ROWS), :] for o, s in which],
                tables[:6])
            for (o, s), k, f in zip(which, khat, flat):
                khat_ref[o * CAP + s] = k
                pred_out[rows_of(o * CAP + s, PAD), :] = f
            each(j, pred_move, lambda c: c.start())

        @pl.when(jnp.logical_and(j > 0, j <= steps))
        def _():
            each(j - 1, pred_move, lambda c: c.wait_recv())

            @pl.when(j == 1)
            def _():
                pred_in[rows_of(dec, CAP * PAD), :] = pred_out[rows_of(dec, CAP * PAD), :]

            for i in range(per):
                tile = rows_of(lax.rem(dec + (j - 1) * per + i, n_dec), CAP * PAD)
                residual_ref[tile, :] = var_slots[tile, :] * (pred_in[tile, :] - obs_slots[tile, :])
            each(j - 1, res_move, lambda c: c.start())

            @pl.when(j == 1)
            def _():
                resid_in[rows_of(dec, CAP * PAD), :] = residual_ref[rows_of(dec, CAP * PAD), :]

        @pl.when(j > 1)
        def _():
            each(j - 2, res_move, lambda c: c.wait_recv())
            which = owned(j - 2)
            back = adjoint(
                [resid_in[rows_of(o * CAP + s, PAD), :] for o, s in which],
                [khat_ref[o * CAP + s] for o, s in which], tables[6:])
            for (o, s), image in zip(which, back):
                back_ref[o * CAP + s] = image

        return carry

    lax.fori_loop(0, steps + 2, step, 0)

    def end(d, carry):
        pred_move(d).wait_send()
        res_move(d).wait_send()
        return carry

    lax.fori_loop(1, n_dec, end, 0)


def vmem(count):
    return [pl.BlockSpec(memory_space=pltpu.VMEM)] * count


def exchange(packed, psf, model, n_ra, n_dec):
    bands, tra, tdec = model.shape
    strip = pltpu.VMEM((3, tra, N), F32)
    size = n_dec * CAP * PSF_ROWS
    several, many = pltpu.SemaphoreType.DMA((10,)), pltpu.SemaphoreType.DMA((n_dec,))
    return pl.pallas_call(
        functools.partial(exchange_kernel, n_ra, n_dec),
        out_shape=[
            jax.ShapeDtypeStruct((size, N), F32),
            jax.ShapeDtypeStruct((bands, (tdec + 2 * SIDE) // N, tra + 2 * EDGE, N), F32),
        ],
        in_specs=vmem(3),
        out_specs=vmem(2),
        scratch_shapes=[strip, strip, strip, strip, pltpu.VMEM((4, 3, EDGE, N), F32), pltpu.VMEM((size, N), F32),
                        several, several, many, many],
        compiler_params=pltpu.CompilerParams(
            collective_id=2, has_side_effects=True, vmem_limit_bytes=LIMIT),
        cost_estimate=pl.CostEstimate(flops=0, bytes_accessed=40_000_000, transcendentals=0),
    )(packed, psf, model)


def cut_kernel(meta_ref, ext_ref, patch_ref):
    step = pl.program_id(0)
    for e in range(GROUP):
        which, row_at, col_at, down, over = place_of(meta_ref[step * (GROUP // CAP) + e // CAP, e % CAP])
        at = lax.shift_right_logical(col_at, 7)
        rows = pl.ds(row_at + down, N)
        window = jnp.concatenate([ext_ref[which, at, rows, :], ext_ref[which, at + 1, rows, :]], axis=1)
        patch_ref[e] = pltpu.roll(window, lax.bitwise_and(2 * N - over, 2 * N - 1), 1)[:, :N]


def cut(meta, ext):
    slots = meta.shape[0] * CAP
    return pl.pallas_call(
        cut_kernel,
        grid_spec=pltpu.PrefetchScalarGridSpec(
            num_scalar_prefetch=1,
            grid=(slots // GROUP,),
            in_specs=[pl.BlockSpec(ext.shape, lambda i, meta: (0, 0, 0, 0), pipeline_mode=pl.Buffered(1))],
            out_specs=pl.BlockSpec((GROUP, N, N), lambda i, meta: (i, 0, 0)),
        ),
        out_shape=jax.ShapeDtypeStruct((slots, N, N), F32),
        compiler_params=pltpu.CompilerParams(vmem_limit_bytes=LIMIT),
    )(meta, ext)


def photometry(packed, obs, var, psfs, patches, n_ra, n_dec):
    slots = n_dec * CAP
    image = pltpu.VMEM((slots * PAD, N), F32)
    many = pltpu.SemaphoreType.DMA((n_dec,))
    tables = [jnp.asarray(t) for t in make_tables()]
    return pl.pallas_call(
        functools.partial(photometry_kernel, n_ra, n_dec),
        out_shape=[
            jax.ShapeDtypeStruct((slots, N, N), F32),
            jax.ShapeDtypeStruct((slots * PAD, N), F32),
        ],
        in_specs=vmem(5 + len(tables)),
        out_specs=vmem(2),
        scratch_shapes=[image, image, image, image, image, pltpu.VMEM((slots, N, N), F32), many, many, many, many],
        compiler_params=pltpu.CompilerParams(
            collective_id=0, has_side_effects=True, vmem_limit_bytes=LIMIT),
        cost_estimate=pl.CostEstimate(flops=0, bytes_accessed=40_000_000, transcendentals=0),
    )(packed, obs, var, psfs, patches, *tables)


def meta_kernel(packed_ref, meta_ref):
    meta_ref[...] = places_of_tile(packed_ref, lax.axis_index("dec"))


def tile_meta(packed):
    return pl.pallas_call(
        meta_kernel, out_shape=jax.ShapeDtypeStruct((packed.shape[0], CAP), jnp.int32))(packed)


def scatter_kernel(n_dec, meta_ref, packed_ref, slots_ref, back_ref, residual_ref, acc_ref):
    step = pl.program_id(0)

    @pl.when(step == 0)
    def _():
        acc_ref[...] = jnp.zeros_like(acc_ref)
        row, column, first, second = own_places(packed_ref, lax.axis_index("dec"))
        count = row.shape[1]
        slots = CAP * n_dec
        rank = jnp.sum(jnp.where(jnp.logical_and(column == row, second < first), 1, 0), axis=1, keepdims=True)
        place = column * CAP + rank
        chosen = (lax.broadcasted_iota(jnp.int32, (count, slots), 1) == place).astype(F32).astype(BF16)
        chosen = jnp.concatenate([chosen] * 3, axis=1)
        width = residual_ref.shape[1]
        for start in range(0, PAD, 4):
            if start * N >= width:
                break
            x = jnp.concatenate(
                [slots_ref[pl.ds(start + t, slots, stride=PAD), :] for t in range(4)], axis=1)
            y = dot(chosen, three(x))
            end = min((start + 4) * N, width)
            residual_ref[:, start * N : end] = y[:, : end - start * N]

    for e in range(GROUP):
        which, row_at, col_at, down, over = place_of(meta_ref[step * (GROUP // CAP) + e // CAP, e % CAP])
        image = jnp.concatenate([back_ref[e], jnp.zeros((8, N), F32)], axis=0)
        image = pltpu.roll(image, down, 0)
        image = jnp.concatenate([image, jnp.zeros_like(image)], axis=1)
        image = pltpu.roll(image, over, 1)
        acc_ref[which, pl.ds(row_at, N + 8), pl.ds(col_at, 2 * N)] += image


def scatter(meta, packed, residual, back, shape, n_dec):
    def whole(block):
        return pl.BlockSpec(block, lambda i, meta: (0,) * len(block), pipeline_mode=pl.Buffered(1))

    bands, tra, tdec = shape
    wide = (bands, tra + 2 * EDGE, tdec + 2 * SIDE)
    out = (packed.shape[1], C * C)
    return pl.pallas_call(
        functools.partial(scatter_kernel, n_dec),
        grid_spec=pltpu.PrefetchScalarGridSpec(
            num_scalar_prefetch=1,
            grid=(back.shape[0] // GROUP,),
            in_specs=[whole(packed.shape), whole(residual.shape), pl.BlockSpec((GROUP, N, N), lambda i, meta: (i, 0, 0))],
            out_specs=[whole(out), whole(wide)],
        ),
        out_shape=[jax.ShapeDtypeStruct(out, F32), jax.ShapeDtypeStruct(wide, F32)],
        compiler_params=pltpu.CompilerParams(vmem_limit_bytes=LIMIT),
    )(meta, packed, residual, back)


def fold_kernel(n_ra, n_dec, acc_ref, out_ref, to_right, to_left, from_left, from_right, out_corners, corners,
                from_up, from_down, send, recv):
    ra, dec, up, down, right, left = neighbours(n_ra, n_dec)
    greet_near(ra, dec, up, down, right, left)
    tra, tdec = out_ref.shape[1], out_ref.shape[2]
    top, side_at = EDGE + tra, SIDE + tdec
    low_half = lax.broadcasted_iota(jnp.int32, (1, N), 1) < 64
    copy = sender(send, recv)
    copies = [
        copy(0, acc_ref.at[:, :EDGE, SIDE:side_at], from_up, (down, dec)),
        copy(1, acc_ref.at[:, top:, SIDE:side_at], from_down, (up, dec)),
    ]
    for c in copies:
        c.start()

    def pack_left(q, rows):
        return jnp.where(low_half, pltpu.roll(acc_ref[2 * q + 1, rows, :SIDE], 64, 1), acc_ref[2 * q, rows, :SIDE])

    def pack_right(q, rows):
        return jnp.where(low_half, acc_ref[2 * q, rows, side_at:], pltpu.roll(acc_ref[2 * q + 1, rows, side_at:], 64, 1))

    middle, lower, upper = slice(EDGE, top), slice(0, EDGE), slice(top, top + EDGE)
    for q in range(3):
        to_left[q] = pack_left(q, middle)
    more = [copy(2, to_left, from_right, (ra, left))]
    more[0].start()
    copies += more
    for q in range(3):
        to_right[q] = pack_right(q, middle)
    more = [copy(3, to_right, from_left, (ra, right))]
    more[0].start()
    copies += more
    for q in range(3):
        out_corners[0, q] = pack_left(q, lower)
        out_corners[1, q] = pack_left(q, upper)
        out_corners[2, q] = pack_right(q, lower)
        out_corners[3, q] = pack_right(q, upper)
    more = [
        copy(4, out_corners.at[0], corners.at[0], (down, left)),
        copy(5, out_corners.at[1], corners.at[1], (up, left)),
        copy(6, out_corners.at[2], corners.at[2], (down, right)),
        copy(7, out_corners.at[3], corners.at[3], (up, right)),
    ]
    for c in more:
        c.start()
    copies += more
    out_ref[...] = acc_ref[:, EDGE:top, SIDE:side_at]
    for c in copies:
        c.wait()
    in_low, in_high, in_left, in_right = edges(n_ra, n_dec, ra, dec)
    out_ref[:, tra - EDGE :, :] += from_up[...] * in_high
    out_ref[:, :EDGE, :] += from_down[...] * in_low
    every, low_rows, high_rows = slice(0, tra), slice(0, EDGE), slice(tra - EDGE, tra)
    for q in range(3):
        for src, rows, scale, at_right in (
            (from_right.at[q], every, in_right, True),
            (from_left.at[q], every, in_left, False),
            (corners.at[0, q], high_rows, in_high * in_right, True),
            (corners.at[1, q], low_rows, in_low * in_right, True),
            (corners.at[2, q], high_rows, in_high * in_left, False),
            (corners.at[3, q], low_rows, in_low * in_left, False),
        ):
            value = src[...] * scale
            other = pltpu.roll(value, 64, 1)
            if at_right:
                cols, keep = slice(tdec - N, tdec), jnp.logical_not(low_half)
            else:
                cols, keep = slice(0, N), low_half
            out_ref[2 * q, rows, cols] += jnp.where(keep, value, 0.0)
            out_ref[2 * q + 1, rows, cols] += jnp.where(keep, other, 0.0)


def fold(acc, n_ra, n_dec):
    bands, tra, tdec = acc.shape[0], acc.shape[1] - 2 * EDGE, acc.shape[2] - 2 * SIDE
    strip = pltpu.VMEM((3, tra, N), F32)
    corner = pltpu.VMEM((4, 3, EDGE, N), F32)
    band = pltpu.VMEM((bands, EDGE, tdec), F32)
    return pl.pallas_call(
        functools.partial(fold_kernel, n_ra, n_dec),
        out_shape=jax.ShapeDtypeStruct((bands, tra, tdec), F32),
        in_specs=vmem(1),
        out_specs=pl.BlockSpec(memory_space=pltpu.VMEM),
        scratch_shapes=[strip, strip, strip, strip, corner, corner, band, band,
                        pltpu.SemaphoreType.DMA((8,)), pltpu.SemaphoreType.DMA((8,))],
        compiler_params=pltpu.CompilerParams(
            collective_id=1, has_side_effects=True, vmem_limit_bytes=LIMIT),
        cost_estimate=pl.CostEstimate(flops=0, bytes_accessed=40_000_000, transcendentals=0),
    )(acc)


def body(model, observed, inv_var, psf, target_dec, band, offset_ra, offset_dec):
    n_ra, n_dec = lax.axis_size("ra"), lax.axis_size("dec")
    e_dev = observed.shape[0]
    packed = (((target_dec[:, 0] * 8 + band) * 256 + offset_ra) * 256 + offset_dec).reshape(n_dec, e_dev)
    meta = tile_meta(packed)
    psfs, ext = exchange(packed, psf, model, n_ra, n_dec)
    patches = cut(meta, ext)
    back, slots = photometry(packed, observed, inv_var, psfs, patches, n_ra, n_dec)
    residual, acc = scatter(meta, packed, slots, back, model.shape, n_dec)
    return residual, fold(acc, n_ra, n_dec)


def solution(mesh):
    placed = (
        P(None, "ra", "dec"),
        P(("ra", "dec"), None),
        P(("ra", "dec"), None),
        P(("ra", "dec"), None),
        P("ra", None),
        P("ra"),
        P("ra"),
        P("ra"),
    )
    return jax.shard_map(
        body,
        mesh=mesh,
        in_specs=placed,
        out_specs=(P(("ra", "dec"), None), P(None, "ra", "dec")),
        check_vma=False,
    )
```

```python
import functools
import math

import jax
import jax.numpy as jnp
import ml_dtypes
import numpy as np
from jax import lax
from jax.experimental import pallas as pl
from jax.experimental.pallas import tpu as pltpu
from jax.sharding import PartitionSpec as P

K = 63
C = 66
CAP = 4
GROUP = 16
RING = 4
PEERS = (
    ((2, 1), (2, 3), (1, 2), (3, 2)),
    ((1, 1), (3, 3), (1, 3), (3, 1)),
    ((2, 0), (0, 2), (2, 2), (0, 0)),
    ((1, 0), (3, 0), (0, 1), (0, 3)),
)
N = 128
PAIRS = 33
PAD = 40
PSF_ROWS = 32
EDGE = 64
SIDE = 128
LIMIT = 60 * 1024 * 1024
MESH = pl.DeviceIdType.MESH
F32 = jnp.float32
BF16 = jnp.bfloat16


def np_split(table):
    high = table.astype(np.float32).astype(ml_dtypes.bfloat16)
    low = (table - high.astype(np.float64)).astype(np.float32).astype(ml_dtypes.bfloat16)
    return high, low


def make_tables():
    theta = 2.0 * math.pi * (np.arange(64) + 0.5) / N

    def to_freq(columns):
        angle = np.asarray(columns)[:, None] * theta[None, :]
        return np.concatenate([np.cos(angle), -np.sin(angle)], axis=1)

    def rows_cs(out_index, in_index, sign):
        angle = 2.0 * math.pi * ((out_index[:, None] * in_index[None, :]) % N) / N
        return np.cos(angle), sign * np.sin(angle)

    full = np.arange(N)
    zero = np.zeros((N, N))
    zero16 = zero.astype(ml_dtypes.bfloat16)

    def wide(table):
        high, low = np_split(table)
        return np.block([[high, low], [high, zero16]])

    patch_cols = wide(to_freq(full))
    psf_cols = np.zeros((N, 2 * N))
    psf_cols[:K, :N] = to_freq(np.arange(K))
    psf_cols[K : 2 * K, N:] = to_freq(np.arange(K))
    psf_h, psf_l = np_split(psf_cols)
    psf_cols = np.concatenate([psf_h, psf_h, psf_l], axis=0)

    def left(out_index, in_index, sign, keep_in=None, keep_out=None):
        cosine, sine = rows_cs(out_index, in_index, sign)
        table = np.concatenate([cosine, sine], axis=1)
        if keep_in is not None:
            table = table * np.concatenate([keep_in, keep_in])[None, :]
        if keep_out is not None:
            table = table * keep_out[:, None]
        return np.concatenate(np_split(table), axis=0)

    patch_rows = left(full, full, 1.0)
    psf_index = np.concatenate([2 * np.arange(32), 2 * np.arange(32) + 1])
    psf_rows = left(full, psf_index, 1.0, keep_in=(psf_index < K).astype(np.float64))
    within = (np.arange(PAD) < PAIRS).astype(np.float64)
    inner_keep = np.concatenate([within, within])
    inner_index = np.concatenate([K - 1 + 2 * np.arange(PAD), K + 2 * np.arange(PAD)])
    pred_rows = left(inner_index, full, -1.0, keep_out=inner_keep)
    res_rows = left(full, inner_index, 1.0, keep_in=inner_keep)
    back_rows = left(full, full, -1.0)
    scale = 2.0 / (N * N)
    inner_cols = K - 1 + np.arange(C)
    pred_cols = np.zeros((2 * N, 2 * N))
    pred_cols[:N, :C] = scale * to_freq(inner_cols).T
    pred_cols[N:, C : 2 * C] = scale * to_freq(inner_cols).T
    pred_cols = np.concatenate(np_split(pred_cols), axis=0)
    res_cols = np.zeros((2 * N, 2 * N))
    res_cols[:C, :N] = to_freq(inner_cols)
    res_cols[C : 2 * C, N:] = to_freq(inner_cols)
    res_cols = np.concatenate(np_split(res_cols), axis=0)
    back_cols = wide(scale * to_freq(full).T)
    psf_rows = np.concatenate([np.concatenate([psf_rows[:N], psf_rows[:N]], axis=1),
                               np.concatenate([psf_rows[N:], np.zeros_like(psf_rows[N:])], axis=1)], axis=0)
    return (patch_cols, patch_rows, psf_cols, psf_rows, pred_rows, pred_cols, res_cols, res_rows,
            back_rows, back_cols)


def split(x):
    high = x.astype(BF16)
    return high, (x - high.astype(F32)).astype(BF16)


def dot(a, b):
    return jnp.dot(a, b, preferred_element_type=F32)


def right_wide(x, table_ref):
    high, low = split(x)
    both = dot(jnp.concatenate([high, low], axis=1), table_ref[...])
    return both[:, :N] + both[:, N:]


def right_three(x, table_ref):
    high, low = split(x)
    depth = x.shape[1]
    return (dot(high, table_ref[:depth, :]) + dot(low, table_ref[:depth, :])
            + dot(high, table_ref[depth:, :]))


def left_three(table_ref, x):
    rows = table_ref.shape[0] // 2
    high, low = split(x)
    both = dot(table_ref[...], high)
    return both[:rows] + both[rows:] + dot(table_ref[:rows, :], low)


def turned(y, sign):
    return pltpu.roll(y, 64, 1) * sign


def stacked(parts, sign):
    return jnp.concatenate(
        [jnp.concatenate([y, turned(y, sign)], axis=0) for y in parts], axis=1)


def lanes():
    lane = lax.broadcasted_iota(jnp.int32, (1, N), 1)
    return lane, jnp.where(lane < 64, 1.0, -1.0).astype(F32), lane < 64


def place_of(code):
    code = jnp.maximum(code - 1, 0)
    which = lax.shift_right_logical(code, 16)
    row = lax.bitwise_and(lax.shift_right_logical(code, 8), 255) + (EDGE - K + 1)
    column = lax.bitwise_and(code, 255) + (SIDE - K + 1)
    row_at = pl.multiple_of(lax.shift_left(lax.shift_right_logical(row, 3), 3), 8)
    col_at = pl.multiple_of(lax.shift_left(lax.shift_right_logical(column, 7), 7), 128)
    return which, row_at, col_at, row - row_at, column - col_at


def halves(k, low_half):
    rk = pltpu.roll(k, 64, 1)
    return jnp.where(low_half, k, rk), jnp.where(low_half, -rk, k)


def predict(patches, psfs, tables):
    patch_cols, patch_rows, psf_cols, psf_rows, pred_rows, pred_cols = tables
    count = len(patches)
    lane, sign, low_half = lanes()
    y = right_wide(jnp.concatenate(patches, axis=0), patch_cols)
    z = left_three(patch_rows, stacked([y[e * N : e * N + N] for e in range(count)], sign))
    pairs = []
    for x in psfs:
        both = jnp.concatenate([pltpu.roll(x, 1, 0), x], axis=1)
        pairs.append(pltpu.roll(both, N, 1, stride=2, stride_axis=0)[:, :N])
    high, low = split(jnp.concatenate(pairs, axis=0))
    y = dot(jnp.concatenate([high, low], axis=1), psf_cols[: 2 * N, :]) + dot(high, psf_cols[2 * N :, :])
    y = stacked([jnp.concatenate([y[32 * e : 32 * e + 32, :N], y[32 * e : 32 * e + 32, N:]], axis=0)
                 for e in range(count)], sign)
    high, low = split(y)
    khat = (dot(psf_rows[:N, :], jnp.concatenate([high, low], axis=0))
            + dot(psf_rows[N:, :N], high))
    khat = [khat[:, e * N : e * N + N] for e in range(count)]
    spec = []
    for e in range(count):
        k_re, k_im = halves(khat[e], low_half)
        p = z[:, e * N : e * N + N]
        rp = pltpu.roll(p, 64, 1)
        spec.append(jnp.concatenate(
            [p * k_re + rp * k_im, (rp * k_re - p * k_im) * sign], axis=0))
    u = left_three(pred_rows, jnp.concatenate(spec, axis=1))
    u = jnp.concatenate(
        [jnp.concatenate([u[:PAD, e * N : e * N + N], u[PAD:, e * N : e * N + N]], axis=1)
         for e in range(count)], axis=0)
    predicted = right_three(u, pred_cols)
    last = lax.broadcasted_iota(jnp.int32, (PAD, 1), 0) == PAIRS - 1
    flat = []
    for e in range(count):
        image = pltpu.roll(predicted[e * PAD : e * PAD + PAD], 0, 1, stride=4, stride_axis=0)
        front, rear = image[:, :N], image[:, N:]
        flat.append(jnp.where(last, 0.0, front) + pltpu.roll(rear, 1, 0)
                    + pltpu.roll(jnp.where(last, front, 0.0), 2, 0))
    return khat, flat


def adjoint(resids, khat, tables):
    res_cols, res_rows, back_rows, back_cols = tables
    count = len(resids)
    lane, sign, low_half = lanes()
    number = lax.broadcasted_iota(jnp.int32, (PAD, 1), 0)
    last = number == PAIRS - 1
    turn = lax.bitwise_and(lane + 4 * number, N - 1)
    pairs = []
    for resid in resids:
        front = jnp.take_along_axis(resid, turn, axis=1, mode="promise_in_bounds")
        rear = jnp.take_along_axis(pltpu.roll(resid, PAD - 1, 0), turn, axis=1, mode="promise_in_bounds")
        pairs.append(jnp.concatenate(
            [jnp.where(lane + 4 * number < N, front, rear),
             jnp.where(last, pltpu.roll(resid, PAD - 2, 0), rear)], axis=1))
    v = right_three(jnp.concatenate(pairs, axis=0), res_cols)
    v = [jnp.concatenate([v[e * PAD : e * PAD + PAD, :N], v[e * PAD : e * PAD + PAD, N:]], axis=0)
         for e in range(count)]
    r = left_three(res_rows, stacked(v, sign))
    spec = []
    for e in range(count):
        k_re, k_im = halves(khat[e], low_half)
        p = r[:, e * N : e * N + N]
        rp = pltpu.roll(p, 64, 1)
        spec.append(jnp.concatenate(
            [p * k_re - rp * k_im, (rp * k_re + p * k_im) * sign], axis=0))
    u = left_three(back_rows, jnp.concatenate(spec, axis=1))
    back = right_wide(jnp.concatenate([u[:, e * N : e * N + N] for e in range(count)], axis=0), back_cols)
    return [back[e * N : e * N + N] for e in range(count)]


def three(x):
    high = x.astype(BF16)
    rest = x - high.astype(F32)
    middle = rest.astype(BF16)
    return jnp.concatenate([high, middle, (rest - middle.astype(F32)).astype(BF16)], axis=0)


def own_places(packed_ref, own):
    row = lax.shift_right_logical(packed_ref[pl.ds(own, 1), :], 19)
    count = row.shape[1]
    first = lax.broadcasted_iota(jnp.int32, (count, count), 0)
    second = lax.broadcasted_iota(jnp.int32, (count, count), 1)
    column = jnp.sum(jnp.where(first == second, row, 0), axis=1, keepdims=True)
    return row, column, first, second


def places_of_tile(packed_ref, own):
    packed = packed_ref[...]
    count = packed.shape[1]
    here = lax.shift_right_logical(packed, 19) == own
    code = lax.bitwise_and(packed, (1 << 19) - 1) + 1
    first = lax.broadcasted_iota(jnp.int32, (count, count), 0)
    second = lax.broadcasted_iota(jnp.int32, (count, count), 1)
    earlier = (first < second).astype(F32).astype(BF16)
    rank = dot(here.astype(F32).astype(BF16), earlier)
    return jnp.concatenate(
        [jnp.sum(jnp.where(jnp.logical_and(here, rank == float(s)), code, 0), axis=1, keepdims=True)
         for s in range(CAP)], axis=1)


def neighbours(n_ra, n_dec):
    ra, dec = lax.axis_index("ra"), lax.axis_index("dec")
    up, down = lax.rem(ra + 1, n_ra), lax.rem(ra + n_ra - 1, n_ra)
    right, left = lax.rem(dec + 1, n_dec), lax.rem(dec + n_dec - 1, n_dec)
    return ra, dec, up, down, right, left


def signal_all(devices):
    for device in devices:
        pl.semaphore_signal(pltpu.get_barrier_semaphore(), inc=1, device_id=device, device_id_type=MESH)


def wait_all(devices):
    pl.semaphore_wait(pltpu.get_barrier_semaphore(), len(devices))


def moved(dec, shift, n_dec, sign):
    rings = n_dec // RING
    outer = lax.rem(dec // RING + rings + sign * shift[0], rings)
    inner = lax.rem(lax.rem(dec, RING) + RING + sign * shift[1], RING)
    return outer * RING + inner


def shifts():
    return [(j * len(PEERS[j]) + i, shift) for j in range(len(PEERS)) for i, shift in enumerate(PEERS[j])
            if shift != (0, 0)]


def edges(n_ra, n_dec, ra, dec):
    zero, one = jnp.zeros((), F32), jnp.ones((), F32)
    return (jnp.where(ra > 0, one, zero), jnp.where(ra < n_ra - 1, one, zero),
            jnp.where(dec > 0, one, zero), jnp.where(dec < n_dec - 1, one, zero))


def sender(send, recv):
    def copy(index, src, dst, other):
        return pltpu.make_async_remote_copy(
            src_ref=src, dst_ref=dst, send_sem=send.at[index], recv_sem=recv.at[index],
            device_id=other, device_id_type=MESH)
    return copy


def rows_of(index, size):
    return pl.ds(pl.multiple_of(index * size, 8), size)


def slot_chooser(packed_ref, dec, n_dec):
    row, column, first, second = own_places(packed_ref, dec)
    count = row.shape[1]
    slots = CAP * n_dec
    rank = jnp.sum(jnp.where(jnp.logical_and(column == row, first < second), 1, 0), axis=0, keepdims=True)
    place = row * CAP + rank
    chosen = (lax.broadcasted_iota(jnp.int32, (slots, count), 0) == place).astype(F32).astype(BF16)
    return jnp.concatenate([chosen] * 3, axis=1)


def to_slots(chosen, ref, out_ref, rows):
    width, slots = ref.shape[1], chosen.shape[0]
    for start in range(0, rows, 4):
        end = min((start + 4) * N, width)
        if start * N < width:
            y = dot(chosen, three(ref[:, start * N : end]))
            if end < (start + 4) * N:
                y = jnp.concatenate([y, jnp.zeros((slots, (start + 4) * N - end), F32)], axis=1)
        else:
            y = jnp.zeros((slots, 4 * N), F32)
        for t in range(4):
            out_ref[pl.ds(start + t, slots, stride=rows), :] = y[:, t * N : t * N + N]


def exchange_kernel(n_ra, n_dec, packed_ref, psf_ref, model_ref, psf_in, ext_ref,
                    to_right, to_left, from_left, from_right, corners, psf_out, send, recv, send_psf, recv_psf):
    ra, dec, up, down, right, left = neighbours(n_ra, n_dec)
    peers = [(ra, moved(dec, shift, n_dec, 1)) for _, shift in shifts()] + [(up, dec), (down, dec)]
    signal_all(peers)
    tra, tdec = model_ref.shape[1], model_ref.shape[2]
    top = EDGE + tra
    low_half = lax.broadcasted_iota(jnp.int32, (1, N), 1) < 64
    copy = sender(send, recv)
    for q in range(3):
        to_right[q] = jnp.where(
            low_half, pltpu.roll(model_ref[2 * q + 1, :, tdec - N :], 64, 1), model_ref[2 * q, :, tdec - N :])
        to_left[q] = jnp.where(
            low_half, model_ref[2 * q, :, :N], pltpu.roll(model_ref[2 * q + 1, :, :N], 64, 1))
    wait_all(peers)
    sides = [copy(0, to_right, from_left, (ra, right)), copy(1, to_left, from_right, (ra, left))]
    for c in sides:
        c.start()
    copies = []
    for t in range(2):
        cols = slice(t * N, t * N + N)
        copies += [copy(2 + t, model_ref.at[:, tra - EDGE :, cols], ext_ref.at[:, 1 + t, :EDGE, :], (up, dec)),
                   copy(4 + t, model_ref.at[:, :EDGE, cols], ext_ref.at[:, 1 + t, top:, :], (down, dec))]
    for c in copies:
        c.start()
    to_slots(slot_chooser(packed_ref, dec, n_dec), psf_ref, psf_out, PSF_ROWS)
    moves = []
    here = rows_of(dec, CAP * PSF_ROWS)
    for d, shift in shifts():
        tile = moved(dec, shift, n_dec, 1)
        moves.append(sender(send_psf, recv_psf)(
            d, psf_out.at[rows_of(tile, CAP * PSF_ROWS), :], psf_in.at[here, :], (ra, tile)))
        moves[-1].start()
    psf_in[here, :] = psf_out[here, :]
    for t in range(2):
        ext_ref[:, 1 + t, EDGE:top, :] = model_ref[:, :, t * N : t * N + N]
    for c in sides:
        c.wait_recv()
    more = [
        copy(6, from_left.at[:, tra - EDGE :, :], corners.at[0], (up, dec)),
        copy(7, from_left.at[:, :EDGE, :], corners.at[1], (down, dec)),
        copy(8, from_right.at[:, tra - EDGE :, :], corners.at[2], (up, dec)),
        copy(9, from_right.at[:, :EDGE, :], corners.at[3], (down, dec)),
    ]
    for c in more:
        c.start()
    in_low, in_high, in_left, in_right = edges(n_ra, n_dec, ra, dec)

    def place(pieces):
        for src, q, col, rows, scale in pieces:
            value = src[...] * scale
            ext_ref[2 * q, col, rows, :] = value
            ext_ref[2 * q + 1, col, rows, :] = pltpu.roll(value, 64, 1)

    middle, low, high = slice(EDGE, top), slice(0, EDGE), slice(top, top + EDGE)
    place([(from_left.at[q], q, 0, middle, in_left) for q in range(3)]
          + [(from_right.at[q], q, 3, middle, in_right) for q in range(3)])
    for c in copies + more:
        c.wait()

    @pl.when(ra == 0)
    def _():
        ext_ref[:, 1:3, :EDGE, :] = jnp.zeros((ext_ref.shape[0], 2, EDGE, N), F32)

    @pl.when(ra == n_ra - 1)
    def _():
        ext_ref[:, 1:3, top:, :] = jnp.zeros((ext_ref.shape[0], 2, EDGE, N), F32)

    for q in range(3):
        place([(corners.at[0, q], q, 0, low, in_low * in_left), (corners.at[1, q], q, 0, high, in_high * in_left),
               (corners.at[2, q], q, 3, low, in_low * in_right), (corners.at[3, q], q, 3, high, in_high * in_right)])
    for c in sides:
        c.wait_send()
    for c in moves:
        c.wait()


def photometry_kernel(n_ra, n_dec, packed_ref, obs_ref, var_ref, psf_in, patch_ref, *refs):
    tables, refs = refs[:10], refs[10:]
    (back_ref, residual_ref, obs_slots, var_slots, pred_out, pred_in, resid_in, khat_ref,
     send_pred, recv_pred, send_res, recv_res) = refs
    ra, dec = lax.axis_index("ra"), lax.axis_index("dec")
    peers = [(ra, moved(dec, shift, n_dec, 1)) for _, shift in shifts()]
    signal_all(peers)
    own = rows_of(dec, CAP * PAD)
    steps = len(PEERS)
    pred_moves, res_moves = {}, {}
    for d, shift in shifts():
        owner, tile = moved(dec, shift, n_dec, -1), moved(dec, shift, n_dec, 1)
        pred_moves[shift] = sender(send_pred, recv_pred)(
            d, pred_out.at[rows_of(owner, CAP * PAD), :], pred_in.at[own, :], (ra, owner))
        res_moves[shift] = sender(send_res, recv_res)(
            d, residual_ref.at[rows_of(tile, CAP * PAD), :], resid_in.at[own, :], (ra, tile))

    def owned(j):
        return [(moved(dec, PEERS[j][e // CAP], n_dec, -1), e % CAP) for e in range(GROUP)]

    for j in range(steps + 2):
        if j < steps:
            which = owned(j)
            khat, flat = predict(
                [patch_ref[o * CAP + s] for o, s in which],
                [psf_in[rows_of(o * CAP + s, PSF_ROWS), :] for o, s in which],
                tables[:6])
            for (o, s), k, f in zip(which, khat, flat):
                khat_ref[o * CAP + s] = k
                pred_out[rows_of(o * CAP + s, PAD), :] = f
            if j == 0:
                wait_all(peers)
            for shift in PEERS[j]:
                if shift in pred_moves:
                    pred_moves[shift].start()
            if j == 0:
                chosen = slot_chooser(packed_ref, dec, n_dec)
                to_slots(chosen, obs_ref, obs_slots, PAD)
                to_slots(chosen, var_ref, var_slots, PAD)
        if 1 <= j <= steps:
            for shift in PEERS[j - 1]:
                tile = rows_of(moved(dec, shift, n_dec, 1), CAP * PAD)
                if shift in pred_moves:
                    pred_moves[shift].wait_recv()
                    residual_ref[tile, :] = var_slots[tile, :] * (pred_in[tile, :] - obs_slots[tile, :])
                    res_moves[shift].start()
                else:
                    resid = var_slots[own, :] * (pred_out[own, :] - obs_slots[own, :])
                    residual_ref[own, :] = resid
                    resid_in[own, :] = resid
        if j >= 2:
            for shift in PEERS[j - 2]:
                if shift in res_moves:
                    res_moves[shift].wait_recv()
            which = owned(j - 2)
            back = adjoint(
                [resid_in[rows_of(o * CAP + s, PAD), :] for o, s in which],
                [khat_ref[o * CAP + s] for o, s in which], tables[6:])
            for (o, s), image in zip(which, back):
                back_ref[o * CAP + s] = image
    for shift in pred_moves:
        pred_moves[shift].wait_send()
        res_moves[shift].wait_send()


def vmem(count):
    return [pl.BlockSpec(memory_space=pltpu.VMEM)] * count


def exchange(packed, psf, model, n_ra, n_dec):
    bands, tra, tdec = model.shape
    strip = pltpu.VMEM((3, tra, N), F32)
    size = n_dec * CAP * PSF_ROWS
    several, many = pltpu.SemaphoreType.DMA((10,)), pltpu.SemaphoreType.DMA((n_dec,))
    return pl.pallas_call(
        functools.partial(exchange_kernel, n_ra, n_dec),
        out_shape=[
            jax.ShapeDtypeStruct((size, N), F32),
            jax.ShapeDtypeStruct((bands, (tdec + 2 * SIDE) // N, tra + 2 * EDGE, N), F32),
        ],
        in_specs=vmem(3),
        out_specs=vmem(2),
        scratch_shapes=[strip, strip, strip, strip, pltpu.VMEM((4, 3, EDGE, N), F32), pltpu.VMEM((size, N), F32),
                        several, several, many, many],
        compiler_params=pltpu.CompilerParams(
            collective_id=2, has_side_effects=True, vmem_limit_bytes=LIMIT),
        cost_estimate=pl.CostEstimate(flops=0, bytes_accessed=40_000_000, transcendentals=0),
    )(packed, psf, model)


def cut_kernel(meta_ref, ext_ref, patch_ref):
    step = pl.program_id(0)
    for e in range(GROUP):
        which, row_at, col_at, down, over = place_of(meta_ref[step * (GROUP // CAP) + e // CAP, e % CAP])
        at = lax.shift_right_logical(col_at, 7)
        rows = pl.ds(row_at + down, N)
        window = jnp.concatenate([ext_ref[which, at, rows, :], ext_ref[which, at + 1, rows, :]], axis=1)
        patch_ref[e] = pltpu.roll(window, lax.bitwise_and(2 * N - over, 2 * N - 1), 1)[:, :N]


def cut(meta, ext):
    slots = meta.shape[0] * CAP
    return pl.pallas_call(
        cut_kernel,
        grid_spec=pltpu.PrefetchScalarGridSpec(
            num_scalar_prefetch=1,
            grid=(slots // GROUP,),
            in_specs=[pl.BlockSpec(ext.shape, lambda i, meta: (0, 0, 0, 0), pipeline_mode=pl.Buffered(1))],
            out_specs=pl.BlockSpec((GROUP, N, N), lambda i, meta: (i, 0, 0)),
        ),
        out_shape=jax.ShapeDtypeStruct((slots, N, N), F32),
        compiler_params=pltpu.CompilerParams(vmem_limit_bytes=LIMIT),
    )(meta, ext)


def photometry(packed, obs, var, psfs, patches, n_ra, n_dec):
    slots = n_dec * CAP
    image = pltpu.VMEM((slots * PAD, N), F32)
    many = pltpu.SemaphoreType.DMA((n_dec,))
    tables = [jnp.asarray(t) for t in make_tables()]
    return pl.pallas_call(
        functools.partial(photometry_kernel, n_ra, n_dec),
        out_shape=[
            jax.ShapeDtypeStruct((slots, N, N), F32),
            jax.ShapeDtypeStruct((slots * PAD, N), F32),
        ],
        in_specs=vmem(5 + len(tables)),
        out_specs=vmem(2),
        scratch_shapes=[image, image, image, image, image, pltpu.VMEM((slots, N, N), F32), many, many, many, many],
        compiler_params=pltpu.CompilerParams(
            collective_id=0, has_side_effects=True, vmem_limit_bytes=LIMIT),
        cost_estimate=pl.CostEstimate(flops=0, bytes_accessed=40_000_000, transcendentals=0),
    )(packed, obs, var, psfs, patches, *tables)


def meta_kernel(packed_ref, meta_ref):
    meta_ref[...] = places_of_tile(packed_ref, lax.axis_index("dec"))


def tile_meta(packed):
    return pl.pallas_call(
        meta_kernel, out_shape=jax.ShapeDtypeStruct((packed.shape[0], CAP), jnp.int32))(packed)


def scatter_kernel(n_dec, meta_ref, packed_ref, slots_ref, back_ref, residual_ref, acc_ref):
    step = pl.program_id(0)

    @pl.when(step == 0)
    def _():
        acc_ref[...] = jnp.zeros_like(acc_ref)
        row, column, first, second = own_places(packed_ref, lax.axis_index("dec"))
        count = row.shape[1]
        slots = CAP * n_dec
        rank = jnp.sum(jnp.where(jnp.logical_and(column == row, second < first), 1, 0), axis=1, keepdims=True)
        place = column * CAP + rank
        chosen = (lax.broadcasted_iota(jnp.int32, (count, slots), 1) == place).astype(F32).astype(BF16)
        chosen = jnp.concatenate([chosen] * 3, axis=1)
        width = residual_ref.shape[1]
        for start in range(0, PAD, 4):
            if start * N >= width:
                break
            x = jnp.concatenate(
                [slots_ref[pl.ds(start + t, slots, stride=PAD), :] for t in range(4)], axis=1)
            y = dot(chosen, three(x))
            end = min((start + 4) * N, width)
            residual_ref[:, start * N : end] = y[:, : end - start * N]

    for e in range(GROUP):
        which, row_at, col_at, down, over = place_of(meta_ref[step * (GROUP // CAP) + e // CAP, e % CAP])
        image = jnp.concatenate([back_ref[e], jnp.zeros((8, N), F32)], axis=0)
        image = pltpu.roll(image, down, 0)
        image = jnp.concatenate([image, jnp.zeros_like(image)], axis=1)
        image = pltpu.roll(image, over, 1)
        acc_ref[which, pl.ds(row_at, N + 8), pl.ds(col_at, 2 * N)] += image


def scatter(meta, packed, residual, back, shape, n_dec):
    def whole(block):
        return pl.BlockSpec(block, lambda i, meta: (0,) * len(block), pipeline_mode=pl.Buffered(1))

    bands, tra, tdec = shape
    wide = (bands, tra + 2 * EDGE, tdec + 2 * SIDE)
    out = (packed.shape[1], C * C)
    return pl.pallas_call(
        functools.partial(scatter_kernel, n_dec),
        grid_spec=pltpu.PrefetchScalarGridSpec(
            num_scalar_prefetch=1,
            grid=(back.shape[0] // GROUP,),
            in_specs=[whole(packed.shape), whole(residual.shape), pl.BlockSpec((GROUP, N, N), lambda i, meta: (i, 0, 0))],
            out_specs=[whole(out), whole(wide)],
        ),
        out_shape=[jax.ShapeDtypeStruct(out, F32), jax.ShapeDtypeStruct(wide, F32)],
        compiler_params=pltpu.CompilerParams(vmem_limit_bytes=LIMIT),
    )(meta, packed, residual, back)


def fold_kernel(n_ra, n_dec, acc_ref, out_ref, to_right, to_left, from_left, from_right, out_corners, corners,
                from_up, from_down, send, recv):
    ra, dec, up, down, right, left = neighbours(n_ra, n_dec)
    peers = [(up, dec), (down, dec), (ra, right), (ra, left)]
    signal_all(peers)
    tra, tdec = out_ref.shape[1], out_ref.shape[2]
    top, side_at = EDGE + tra, SIDE + tdec
    low_half = lax.broadcasted_iota(jnp.int32, (1, N), 1) < 64
    copy = sender(send, recv)

    def pack_left(q, rows):
        return jnp.where(low_half, pltpu.roll(acc_ref[2 * q + 1, rows, :SIDE], 64, 1), acc_ref[2 * q, rows, :SIDE])

    def pack_right(q, rows):
        return jnp.where(low_half, acc_ref[2 * q, rows, side_at:], pltpu.roll(acc_ref[2 * q + 1, rows, side_at:], 64, 1))

    middle, lower, upper = slice(EDGE, top), slice(0, EDGE), slice(top, top + EDGE)
    for q in range(3):
        out_corners[0, q] = pack_left(q, lower)
        out_corners[1, q] = pack_left(q, upper)
        out_corners[2, q] = pack_right(q, lower)
        out_corners[3, q] = pack_right(q, upper)
        to_left[q] = pack_left(q, middle)
        to_right[q] = pack_right(q, middle)
    wait_all(peers)
    inner, low_rows, high_rows = slice(EDGE, tra - EDGE), slice(0, EDGE), slice(tra - EDGE, tra)
    turns = [copy(i, out_corners.at[i], corners.at[i], (down if i % 2 == 0 else up, dec)) for i in range(4)]
    copies = [
        copy(4, to_left.at[:, inner, :], from_right.at[:, inner, :], (ra, left)),
        copy(5, to_right.at[:, inner, :], from_left.at[:, inner, :], (ra, right)),
        copy(6, acc_ref.at[:, lower, SIDE:side_at], from_up, (down, dec)),
        copy(7, acc_ref.at[:, upper, SIDE:side_at], from_down, (up, dec)),
    ]
    for c in turns + copies:
        c.start()
    in_low, in_high, in_left, in_right = edges(n_ra, n_dec, ra, dec)
    for c in turns:
        c.wait_recv()
    to_left[:, high_rows, :] += corners[0] * in_high
    to_right[:, high_rows, :] += corners[2] * in_high
    more = [
        copy(8, to_left.at[:, high_rows, :], from_right.at[:, high_rows, :], (ra, left)),
        copy(9, to_right.at[:, high_rows, :], from_left.at[:, high_rows, :], (ra, right)),
    ]
    for c in more:
        c.start()
    to_left[:, low_rows, :] += corners[1] * in_low
    to_right[:, low_rows, :] += corners[3] * in_low
    more += [
        copy(10, to_left.at[:, low_rows, :], from_right.at[:, low_rows, :], (ra, left)),
        copy(11, to_right.at[:, low_rows, :], from_left.at[:, low_rows, :], (ra, right)),
    ]
    for c in more[2:]:
        c.start()
    out_ref[...] = acc_ref[:, middle, SIDE:side_at]
    for c in turns:
        c.wait_send()
    for c in copies[2:]:
        c.wait()
    out_ref[:, high_rows, :] += from_up[...] * in_high
    out_ref[:, low_rows, :] += from_down[...] * in_low
    for c in copies[:2] + more:
        c.wait()
    for q in range(3):
        for src, scale, at_right in ((from_right.at[q], in_right, True), (from_left.at[q], in_left, False)):
            value = src[...] * scale
            other = pltpu.roll(value, 64, 1)
            if at_right:
                cols, keep = slice(tdec - N, tdec), jnp.logical_not(low_half)
            else:
                cols, keep = slice(0, N), low_half
            out_ref[2 * q, :, cols] += jnp.where(keep, value, 0.0)
            out_ref[2 * q + 1, :, cols] += jnp.where(keep, other, 0.0)


def fold(acc, n_ra, n_dec):
    bands, tra, tdec = acc.shape[0], acc.shape[1] - 2 * EDGE, acc.shape[2] - 2 * SIDE
    strip = pltpu.VMEM((3, tra, N), F32)
    corner = pltpu.VMEM((4, 3, EDGE, N), F32)
    band = pltpu.VMEM((bands, EDGE, tdec), F32)
    return pl.pallas_call(
        functools.partial(fold_kernel, n_ra, n_dec),
        out_shape=jax.ShapeDtypeStruct((bands, tra, tdec), F32),
        in_specs=vmem(1),
        out_specs=pl.BlockSpec(memory_space=pltpu.VMEM),
        scratch_shapes=[strip, strip, strip, strip, corner, corner, band, band,
                        pltpu.SemaphoreType.DMA((12,)), pltpu.SemaphoreType.DMA((12,))],
        compiler_params=pltpu.CompilerParams(
            collective_id=1, has_side_effects=True, vmem_limit_bytes=LIMIT),
        cost_estimate=pl.CostEstimate(flops=0, bytes_accessed=40_000_000, transcendentals=0),
    )(acc)


def body(model, observed, inv_var, psf, target_dec, band, offset_ra, offset_dec):
    n_ra, n_dec = lax.axis_size("ra"), lax.axis_size("dec")
    e_dev = observed.shape[0]
    packed = (((target_dec[:, 0] * 8 + band) * 256 + offset_ra) * 256 + offset_dec).reshape(n_dec, e_dev)
    meta = tile_meta(packed)
    psfs, ext = exchange(packed, psf, model, n_ra, n_dec)
    patches = cut(meta, ext)
    back, slots = photometry(packed, observed, inv_var, psfs, patches, n_ra, n_dec)
    residual, acc = scatter(meta, packed, slots, back, model.shape, n_dec)
    return residual, fold(acc, n_ra, n_dec)


def solution(mesh):
    placed = (
        P(None, "ra", "dec"),
        P(("ra", "dec"), None),
        P(("ra", "dec"), None),
        P(("ra", "dec"), None),
        P("ra", None),
        P("ra"),
        P("ra"),
        P("ra"),
    )
    return jax.shard_map(
        body,
        mesh=mesh,
        in_specs=placed,
        out_specs=(P(("ra", "dec"), None), P(None, "ra", "dec")),
        check_vma=False,
    )
```

```python
import functools
import math

import jax
import jax.numpy as jnp
import ml_dtypes
import numpy as np
from jax import lax
from jax.experimental import pallas as pl
from jax.experimental.pallas import tpu as pltpu
from jax.sharding import PartitionSpec as P

K = 63
C = 66
CAP = 4
GROUP = 16
RING = 4
PEERS = (
    ((2, 1), (2, 3), (1, 2), (3, 2)),
    ((1, 1), (3, 3), (1, 3), (3, 1)),
    ((2, 0), (0, 2), (2, 2), (0, 0)),
    ((1, 0), (3, 0), (0, 1), (0, 3)),
)
N = 128
PAIRS = 33
PAD = 40
PSF_ROWS = 32
EDGE = 64
SIDE = 128
LIMIT = 60 * 1024 * 1024
MESH = pl.DeviceIdType.MESH
F32 = jnp.float32
BF16 = jnp.bfloat16


def np_split(table):
    high = table.astype(np.float32).astype(ml_dtypes.bfloat16)
    low = (table - high.astype(np.float64)).astype(np.float32).astype(ml_dtypes.bfloat16)
    return high, low


def make_tables():
    theta = 2.0 * math.pi * (np.arange(64) + 0.5) / N

    def to_freq(columns):
        angle = np.asarray(columns)[:, None] * theta[None, :]
        return np.concatenate([np.cos(angle), -np.sin(angle)], axis=1)

    def rows_cs(out_index, in_index, sign):
        angle = 2.0 * math.pi * ((out_index[:, None] * in_index[None, :]) % N) / N
        return np.cos(angle), sign * np.sin(angle)

    full = np.arange(N)
    zero = np.zeros((N, N))
    zero16 = zero.astype(ml_dtypes.bfloat16)

    def wide(table):
        high, low = np_split(table)
        return np.block([[high, low], [high, zero16]])

    patch_cols = wide(to_freq(full))
    psf_cols = np.zeros((N, 2 * N))
    psf_cols[:K, :N] = to_freq(np.arange(K))
    psf_cols[K : 2 * K, N:] = to_freq(np.arange(K))
    psf_h, psf_l = np_split(psf_cols)
    psf_cols = np.concatenate([psf_h, psf_h, psf_l], axis=0)

    def left(out_index, in_index, sign, keep_in=None, keep_out=None):
        cosine, sine = rows_cs(out_index, in_index, sign)
        table = np.concatenate([cosine, sine], axis=1)
        if keep_in is not None:
            table = table * np.concatenate([keep_in, keep_in])[None, :]
        if keep_out is not None:
            table = table * keep_out[:, None]
        return np.concatenate(np_split(table), axis=0)

    patch_rows = left(full, full, 1.0)
    psf_index = np.concatenate([2 * np.arange(32), 2 * np.arange(32) + 1])
    psf_rows = left(full, psf_index, 1.0, keep_in=(psf_index < K).astype(np.float64))
    within = (np.arange(PAD) < PAIRS).astype(np.float64)
    inner_keep = np.concatenate([within, within])
    inner_index = np.concatenate([K - 1 + 2 * np.arange(PAD), K + 2 * np.arange(PAD)])
    pred_rows = left(inner_index, full, -1.0, keep_out=inner_keep)
    res_rows = left(full, inner_index, 1.0, keep_in=inner_keep)
    back_rows = left(full, full, -1.0)
    scale = 2.0 / (N * N)
    inner_cols = K - 1 + np.arange(C)
    pred_cols = np.zeros((2 * N, 2 * N))
    pred_cols[:N, :C] = scale * to_freq(inner_cols).T
    pred_cols[N:, C : 2 * C] = scale * to_freq(inner_cols).T
    pred_cols = np.concatenate(np_split(pred_cols), axis=0)
    res_cols = np.zeros((2 * N, 2 * N))
    res_cols[:C, :N] = to_freq(inner_cols)
    res_cols[C : 2 * C, N:] = to_freq(inner_cols)
    res_cols = np.concatenate(np_split(res_cols), axis=0)
    back_cols = wide(scale * to_freq(full).T)
    psf_rows = np.concatenate([np.concatenate([psf_rows[:N], psf_rows[:N]], axis=1),
                               np.concatenate([psf_rows[N:], np.zeros_like(psf_rows[N:])], axis=1)], axis=0)
    return (patch_cols, patch_rows, psf_cols, psf_rows, pred_rows, pred_cols, res_cols, res_rows,
            back_rows, back_cols)


def split(x):
    high = x.astype(BF16)
    return high, (x - high.astype(F32)).astype(BF16)


def dot(a, b):
    return jnp.dot(a, b, preferred_element_type=F32)


def right_wide(x, table_ref):
    high, low = split(x)
    both = dot(jnp.concatenate([high, low], axis=1), table_ref[...])
    return both[:, :N] + both[:, N:]


def right_three(x, table_ref):
    high, low = split(x)
    depth = x.shape[1]
    return (dot(high, table_ref[:depth, :]) + dot(low, table_ref[:depth, :])
            + dot(high, table_ref[depth:, :]))


def left_three(table_ref, x):
    rows = table_ref.shape[0] // 2
    high, low = split(x)
    both = dot(table_ref[...], high)
    return both[:rows] + both[rows:] + dot(table_ref[:rows, :], low)


def turned(y, sign):
    return pltpu.roll(y, 64, 1) * sign


def stacked(parts, sign):
    return jnp.concatenate(
        [jnp.concatenate([y, turned(y, sign)], axis=0) for y in parts], axis=1)


def lanes():
    lane = lax.broadcasted_iota(jnp.int32, (1, N), 1)
    return lane, jnp.where(lane < 64, 1.0, -1.0).astype(F32), lane < 64


def place_of(code):
    code = jnp.maximum(code - 1, 0)
    which = lax.shift_right_logical(code, 16)
    row = lax.bitwise_and(lax.shift_right_logical(code, 8), 255) + (EDGE - K + 1)
    column = lax.bitwise_and(code, 255) + (SIDE - K + 1)
    return which, lax.shift_right_logical(column, 7), row, lax.bitwise_and(column, N - 1)


def cut(code, ext_ref):
    which, at, row, over = place_of(code)
    rows = pl.ds(row, N)
    window = jnp.concatenate([ext_ref[which, at, rows, :], ext_ref[which, at + 1, rows, :]], axis=1)
    return pltpu.roll(window, lax.bitwise_and(2 * N - over, 2 * N - 1), 1)[:, :N]


def halves(k, low_half):
    rk = pltpu.roll(k, 64, 1)
    return jnp.where(low_half, k, rk), jnp.where(low_half, -rk, k)


def predict(patches, psfs, tables):
    patch_cols, patch_rows, psf_cols, psf_rows, pred_rows, pred_cols = tables
    count = len(patches)
    lane, sign, low_half = lanes()
    y = right_wide(jnp.concatenate(patches, axis=0), patch_cols)
    z = left_three(patch_rows, stacked([y[e * N : e * N + N] for e in range(count)], sign))
    pairs = []
    for x in psfs:
        both = jnp.concatenate([pltpu.roll(x, 1, 0), x], axis=1)
        pairs.append(pltpu.roll(both, N, 1, stride=2, stride_axis=0)[:, :N])
    high, low = split(jnp.concatenate(pairs, axis=0))
    y = dot(jnp.concatenate([high, low], axis=1), psf_cols[: 2 * N, :]) + dot(high, psf_cols[2 * N :, :])
    y = stacked([jnp.concatenate([y[32 * e : 32 * e + 32, :N], y[32 * e : 32 * e + 32, N:]], axis=0)
                 for e in range(count)], sign)
    high, low = split(y)
    khat = (dot(psf_rows[:N, :], jnp.concatenate([high, low], axis=0))
            + dot(psf_rows[N:, :N], high))
    khat = [khat[:, e * N : e * N + N] for e in range(count)]
    spec = []
    for e in range(count):
        k_re, k_im = halves(khat[e], low_half)
        p = z[:, e * N : e * N + N]
        rp = pltpu.roll(p, 64, 1)
        spec.append(jnp.concatenate(
            [p * k_re + rp * k_im, (rp * k_re - p * k_im) * sign], axis=0))
    u = left_three(pred_rows, jnp.concatenate(spec, axis=1))
    u = jnp.concatenate(
        [jnp.concatenate([u[:PAD, e * N : e * N + N], u[PAD:, e * N : e * N + N]], axis=1)
         for e in range(count)], axis=0)
    predicted = right_three(u, pred_cols)
    last = lax.broadcasted_iota(jnp.int32, (PAD, 1), 0) == PAIRS - 1
    flat = []
    for e in range(count):
        image = pltpu.roll(predicted[e * PAD : e * PAD + PAD], 0, 1, stride=4, stride_axis=0)
        front, rear = image[:, :N], image[:, N:]
        flat.append(jnp.where(last, 0.0, front) + pltpu.roll(rear, 1, 0)
                    + pltpu.roll(jnp.where(last, front, 0.0), 2, 0))
    return khat, flat


def adjoint(resids, khat, tables):
    res_cols, res_rows, back_rows, back_cols = tables
    count = len(resids)
    lane, sign, low_half = lanes()
    number = lax.broadcasted_iota(jnp.int32, (PAD, 1), 0)
    last = number == PAIRS - 1
    turn = lax.bitwise_and(lane + 4 * number, N - 1)
    pairs = []
    for resid in resids:
        front = jnp.take_along_axis(resid, turn, axis=1, mode="promise_in_bounds")
        rear = jnp.take_along_axis(pltpu.roll(resid, PAD - 1, 0), turn, axis=1, mode="promise_in_bounds")
        pairs.append(jnp.concatenate(
            [jnp.where(lane + 4 * number < N, front, rear),
             jnp.where(last, pltpu.roll(resid, PAD - 2, 0), rear)], axis=1))
    v = right_three(jnp.concatenate(pairs, axis=0), res_cols)
    v = [jnp.concatenate([v[e * PAD : e * PAD + PAD, :N], v[e * PAD : e * PAD + PAD, N:]], axis=0)
         for e in range(count)]
    r = left_three(res_rows, stacked(v, sign))
    spec = []
    for e in range(count):
        k_re, k_im = halves(khat[e], low_half)
        p = r[:, e * N : e * N + N]
        rp = pltpu.roll(p, 64, 1)
        spec.append(jnp.concatenate(
            [p * k_re - rp * k_im, (rp * k_re + p * k_im) * sign], axis=0))
    u = left_three(back_rows, jnp.concatenate(spec, axis=1))
    back = right_wide(jnp.concatenate([u[:, e * N : e * N + N] for e in range(count)], axis=0), back_cols)
    return [back[e * N : e * N + N] for e in range(count)]


def three(x):
    high = x.astype(BF16)
    rest = x - high.astype(F32)
    middle = rest.astype(BF16)
    return jnp.concatenate([high, middle, (rest - middle.astype(F32)).astype(BF16)], axis=0)


def own_places(packed_ref, own):
    row = lax.shift_right_logical(packed_ref[pl.ds(own, 1), :], 19)
    count = row.shape[1]
    first = lax.broadcasted_iota(jnp.int32, (count, count), 0)
    second = lax.broadcasted_iota(jnp.int32, (count, count), 1)
    column = jnp.sum(jnp.where(first == second, row, 0), axis=1, keepdims=True)
    return row, column, first, second


def places_of_tile(packed_ref, own):
    packed = packed_ref[...]
    count = packed.shape[1]
    here = lax.shift_right_logical(packed, 19) == own
    code = lax.bitwise_and(packed, (1 << 19) - 1) + 1
    first = lax.broadcasted_iota(jnp.int32, (count, count), 0)
    second = lax.broadcasted_iota(jnp.int32, (count, count), 1)
    earlier = (first < second).astype(F32).astype(BF16)
    rank = dot(here.astype(F32).astype(BF16), earlier)
    return jnp.concatenate(
        [jnp.sum(jnp.where(jnp.logical_and(here, rank == float(s)), code, 0), axis=1, keepdims=True)
         for s in range(CAP)], axis=1)


def neighbours(n_ra, n_dec):
    ra, dec = lax.axis_index("ra"), lax.axis_index("dec")
    up, down = lax.rem(ra + 1, n_ra), lax.rem(ra + n_ra - 1, n_ra)
    right, left = lax.rem(dec + 1, n_dec), lax.rem(dec + n_dec - 1, n_dec)
    return ra, dec, up, down, right, left


def signal_all(devices):
    for device in devices:
        pl.semaphore_signal(pltpu.get_barrier_semaphore(), inc=1, device_id=device, device_id_type=MESH)


def wait_all(devices):
    pl.semaphore_wait(pltpu.get_barrier_semaphore(), len(devices))


def moved(dec, shift, n_dec, sign):
    rings = n_dec // RING
    outer = lax.rem(dec // RING + rings + sign * shift[0], rings)
    inner = lax.rem(lax.rem(dec, RING) + RING + sign * shift[1], RING)
    return outer * RING + inner


def shifts():
    return [(j * len(PEERS[j]) + i, shift) for j in range(len(PEERS)) for i, shift in enumerate(PEERS[j])
            if shift != (0, 0)]


def edges(n_ra, n_dec, ra, dec):
    zero, one = jnp.zeros((), F32), jnp.ones((), F32)
    return (jnp.where(ra > 0, one, zero), jnp.where(ra < n_ra - 1, one, zero),
            jnp.where(dec > 0, one, zero), jnp.where(dec < n_dec - 1, one, zero))


def sender(send, recv):
    def copy(index, src, dst, other):
        return pltpu.make_async_remote_copy(
            src_ref=src, dst_ref=dst, send_sem=send.at[index], recv_sem=recv.at[index],
            device_id=other, device_id_type=MESH)
    return copy


def rows_of(index, size):
    return pl.ds(pl.multiple_of(index * size, 8), size)


def slot_chooser(packed_ref, dec, n_dec):
    row, column, first, second = own_places(packed_ref, dec)
    count = row.shape[1]
    slots = CAP * n_dec
    rank = jnp.sum(jnp.where(jnp.logical_and(column == row, first < second), 1, 0), axis=0, keepdims=True)
    place = row * CAP + rank
    chosen = (lax.broadcasted_iota(jnp.int32, (slots, count), 0) == place).astype(F32).astype(BF16)
    return jnp.concatenate([chosen] * 3, axis=1)


def to_slots(chosen, ref, out_ref, rows):
    width, slots = ref.shape[1], chosen.shape[0]
    for start in range(0, rows, 4):
        end = min((start + 4) * N, width)
        if start * N < width:
            y = dot(chosen, three(ref[:, start * N : end]))
            if end < (start + 4) * N:
                y = jnp.concatenate([y, jnp.zeros((slots, (start + 4) * N - end), F32)], axis=1)
        else:
            y = jnp.zeros((slots, 4 * N), F32)
        for t in range(4):
            out_ref[pl.ds(start + t, slots, stride=rows), :] = y[:, t * N : t * N + N]


def photometry_kernel(n_ra, n_dec, meta_ref, packed_ref, psf_ref, obs_ref, var_ref, model_ref, *refs):
    tables, refs = refs[:10], refs[10:]
    (back_ref, residual_ref, ext_ref, to_right, to_left, from_left, from_right, corners, psf_out, psf_in,
     obs_slots, var_slots, pred_out, pred_in, resid_in, khat_ref, send, recv, send_psf, recv_psf,
     send_pred, recv_pred, send_res, recv_res) = refs
    ra, dec, up, down, right, left = neighbours(n_ra, n_dec)
    peers = [(ra, moved(dec, shift, n_dec, 1)) for _, shift in shifts()] + [(up, dec), (down, dec)]
    signal_all(peers)
    tra, tdec = model_ref.shape[1], model_ref.shape[2]
    top = EDGE + tra
    low_half = lax.broadcasted_iota(jnp.int32, (1, N), 1) < 64
    copy = sender(send, recv)
    for q in range(3):
        to_right[q] = jnp.where(
            low_half, pltpu.roll(model_ref[2 * q + 1, :, tdec - N :], 64, 1), model_ref[2 * q, :, tdec - N :])
        to_left[q] = jnp.where(
            low_half, model_ref[2 * q, :, :N], pltpu.roll(model_ref[2 * q + 1, :, :N], 64, 1))
    wait_all(peers)
    sides = [copy(0, to_right, from_left, (ra, right)), copy(1, to_left, from_right, (ra, left))]
    for c in sides:
        c.start()
    copies = []
    for t in range(2):
        cols = slice(t * N, t * N + N)
        copies += [copy(2 + t, model_ref.at[:, tra - EDGE :, cols], ext_ref.at[:, 1 + t, :EDGE, :], (up, dec)),
                   copy(4 + t, model_ref.at[:, :EDGE, cols], ext_ref.at[:, 1 + t, top:, :], (down, dec))]
    for c in copies:
        c.start()
    chosen = slot_chooser(packed_ref, dec, n_dec)
    to_slots(chosen, psf_ref, psf_out, PSF_ROWS)
    moves = {}
    here = rows_of(dec, CAP * PSF_ROWS)
    for d, shift in shifts():
        tile = moved(dec, shift, n_dec, 1)
        moves[shift] = sender(send_psf, recv_psf)(
            d, psf_out.at[rows_of(tile, CAP * PSF_ROWS), :], psf_in.at[here, :], (ra, tile))
        moves[shift].start()
    psf_in[here, :] = psf_out[here, :]
    to_slots(chosen, obs_ref, obs_slots, PAD)
    to_slots(chosen, var_ref, var_slots, PAD)
    for t in range(2):
        ext_ref[:, 1 + t, EDGE:top, :] = model_ref[:, :, t * N : t * N + N]
    for c in sides:
        c.wait_recv()
    more = [
        copy(6, from_left.at[:, tra - EDGE :, :], corners.at[0], (up, dec)),
        copy(7, from_left.at[:, :EDGE, :], corners.at[1], (down, dec)),
        copy(8, from_right.at[:, tra - EDGE :, :], corners.at[2], (up, dec)),
        copy(9, from_right.at[:, :EDGE, :], corners.at[3], (down, dec)),
    ]
    for c in more:
        c.start()
    in_low, in_high, in_left, in_right = edges(n_ra, n_dec, ra, dec)

    def place(pieces):
        for src, q, col, rows, scale in pieces:
            value = src[...] * scale
            ext_ref[2 * q, col, rows, :] = value
            ext_ref[2 * q + 1, col, rows, :] = pltpu.roll(value, 64, 1)

    middle, low, high = slice(EDGE, top), slice(0, EDGE), slice(top, top + EDGE)
    place([(from_left.at[q], q, 0, middle, in_left) for q in range(3)]
          + [(from_right.at[q], q, 3, middle, in_right) for q in range(3)])
    for c in copies + more:
        c.wait()

    @pl.when(ra == 0)
    def _():
        ext_ref[:, 1:3, :EDGE, :] = jnp.zeros((ext_ref.shape[0], 2, EDGE, N), F32)

    @pl.when(ra == n_ra - 1)
    def _():
        ext_ref[:, 1:3, top:, :] = jnp.zeros((ext_ref.shape[0], 2, EDGE, N), F32)

    for q in range(3):
        place([(corners.at[0, q], q, 0, low, in_low * in_left), (corners.at[1, q], q, 0, high, in_high * in_left),
               (corners.at[2, q], q, 3, low, in_low * in_right), (corners.at[3, q], q, 3, high, in_high * in_right)])
    for c in sides:
        c.wait_send()

    own = rows_of(dec, CAP * PAD)
    steps = len(PEERS)
    pred_moves, res_moves = {}, {}
    for d, shift in shifts():
        owner, tile = moved(dec, shift, n_dec, -1), moved(dec, shift, n_dec, 1)
        pred_moves[shift] = sender(send_pred, recv_pred)(
            d, pred_out.at[rows_of(owner, CAP * PAD), :], pred_in.at[own, :], (ra, owner))
        res_moves[shift] = sender(send_res, recv_res)(
            d, residual_ref.at[rows_of(tile, CAP * PAD), :], resid_in.at[own, :], (ra, tile))

    def owned(j):
        return [(moved(dec, PEERS[j][e // CAP], n_dec, -1), e % CAP) for e in range(GROUP)]

    for j in range(steps + 2):
        if j < steps:
            for shift in PEERS[j]:
                if shift in moves:
                    moves[shift].wait_recv()
            which = owned(j)
            khat, flat = predict(
                [cut(meta_ref[o, s], ext_ref) for o, s in which],
                [psf_in[rows_of(o * CAP + s, PSF_ROWS), :] for o, s in which],
                tables[:6])
            for (o, s), k, f in zip(which, khat, flat):
                khat_ref[o * CAP + s] = k
                pred_out[rows_of(o * CAP + s, PAD), :] = f
            for shift in PEERS[j]:
                if shift in pred_moves:
                    pred_moves[shift].start()
        if 1 <= j <= steps:
            for shift in PEERS[j - 1]:
                tile = rows_of(moved(dec, shift, n_dec, 1), CAP * PAD)
                if shift in pred_moves:
                    pred_moves[shift].wait_recv()
                    residual_ref[tile, :] = var_slots[tile, :] * (pred_in[tile, :] - obs_slots[tile, :])
                    res_moves[shift].start()
                else:
                    resid = var_slots[own, :] * (pred_out[own, :] - obs_slots[own, :])
                    residual_ref[own, :] = resid
                    resid_in[own, :] = resid
        if j >= 2:
            for shift in PEERS[j - 2]:
                if shift in res_moves:
                    res_moves[shift].wait_recv()
            which = owned(j - 2)
            back = adjoint(
                [resid_in[rows_of(o * CAP + s, PAD), :] for o, s in which],
                [khat_ref[o * CAP + s] for o, s in which], tables[6:])
            for (o, s), image in zip(which, back):
                back_ref[o * CAP + s] = image
    for shift in pred_moves:
        moves[shift].wait_send()
        pred_moves[shift].wait_send()
        res_moves[shift].wait_send()


def vmem(count):
    return [pl.BlockSpec(memory_space=pltpu.VMEM)] * count


def photometry(meta, packed, psf, obs, var, model, n_ra, n_dec):
    bands, tra, tdec = model.shape
    strip = pltpu.VMEM((3, tra, N), F32)
    slots = n_dec * CAP
    image, small = pltpu.VMEM((slots * PAD, N), F32), pltpu.VMEM((slots * PSF_ROWS, N), F32)
    several, many = pltpu.SemaphoreType.DMA((10,)), pltpu.SemaphoreType.DMA((n_dec,))
    tables = [jnp.asarray(t) for t in make_tables()]
    return pl.pallas_call(
        functools.partial(photometry_kernel, n_ra, n_dec),
        out_shape=[
            jax.ShapeDtypeStruct((slots, N, N), F32),
            jax.ShapeDtypeStruct((slots * PAD, N), F32),
        ],
        in_specs=[pl.BlockSpec(memory_space=pltpu.SMEM)] + vmem(5 + len(tables)),
        out_specs=vmem(2),
        scratch_shapes=[pltpu.VMEM((bands, (tdec + 2 * SIDE) // N, tra + 2 * EDGE, N), F32),
                        strip, strip, strip, strip, pltpu.VMEM((4, 3, EDGE, N), F32), small, small,
                        image, image, image, image, image, pltpu.VMEM((slots, N, N), F32),
                        several, several, many, many, many, many, many, many],
        compiler_params=pltpu.CompilerParams(
            collective_id=0, has_side_effects=True, vmem_limit_bytes=LIMIT),
        cost_estimate=pl.CostEstimate(flops=0, bytes_accessed=40_000_000, transcendentals=0),
    )(meta, packed, psf, obs, var, model, *tables)


def meta_kernel(packed_ref, meta_ref):
    meta_ref[...] = places_of_tile(packed_ref, lax.axis_index("dec"))


def tile_meta(packed):
    return pl.pallas_call(
        meta_kernel, out_shape=jax.ShapeDtypeStruct((packed.shape[0], CAP), jnp.int32))(packed)


def scatter_kernel(n_dec, meta_ref, packed_ref, slots_ref, back_ref, residual_ref, acc_ref):
    step = pl.program_id(0)

    @pl.when(step == 0)
    def _():
        acc_ref[...] = jnp.zeros_like(acc_ref)
        row, column, first, second = own_places(packed_ref, lax.axis_index("dec"))
        count = row.shape[1]
        slots = CAP * n_dec
        rank = jnp.sum(jnp.where(jnp.logical_and(column == row, second < first), 1, 0), axis=1, keepdims=True)
        place = column * CAP + rank
        chosen = (lax.broadcasted_iota(jnp.int32, (count, slots), 1) == place).astype(F32).astype(BF16)
        chosen = jnp.concatenate([chosen] * 3, axis=1)
        width = residual_ref.shape[1]
        for start in range(0, PAD, 4):
            if start * N >= width:
                break
            x = jnp.concatenate(
                [slots_ref[pl.ds(start + t, slots, stride=PAD), :] for t in range(4)], axis=1)
            y = dot(chosen, three(x))
            end = min((start + 4) * N, width)
            residual_ref[:, start * N : end] = y[:, : end - start * N]

    for e in range(GROUP):
        which, at, row, over = place_of(meta_ref[step * (GROUP // CAP) + e // CAP, e % CAP])
        image = back_ref[e]
        image = pltpu.roll(jnp.concatenate([image, jnp.zeros_like(image)], axis=1), over, 1)
        rows = pl.ds(row, N)
        acc_ref[which, at, rows, :] += image[:, :N]
        acc_ref[which, at + 1, rows, :] += image[:, N:]


def scatter(meta, packed, residual, back, shape, n_dec):
    def whole(block):
        return pl.BlockSpec(block, lambda i, meta: (0,) * len(block), pipeline_mode=pl.Buffered(1))

    bands, tra, tdec = shape
    wide = (bands, (tdec + 2 * SIDE) // N, tra + 2 * EDGE, N)
    out = (packed.shape[1], C * C)
    return pl.pallas_call(
        functools.partial(scatter_kernel, n_dec),
        grid_spec=pltpu.PrefetchScalarGridSpec(
            num_scalar_prefetch=1,
            grid=(back.shape[0] // GROUP,),
            in_specs=[whole(packed.shape), whole(residual.shape), pl.BlockSpec((GROUP, N, N), lambda i, meta: (i, 0, 0))],
            out_specs=[whole(out), whole(wide)],
        ),
        out_shape=[jax.ShapeDtypeStruct(out, F32), jax.ShapeDtypeStruct(wide, F32)],
        compiler_params=pltpu.CompilerParams(vmem_limit_bytes=LIMIT),
    )(meta, packed, residual, back)


def fold_kernel(n_ra, n_dec, acc_ref, out_ref, to_right, to_left, from_left, from_right, out_corners, corners,
                from_up, from_down, send, recv):
    ra, dec, up, down, right, left = neighbours(n_ra, n_dec)
    peers = [(up, dec), (down, dec), (ra, right), (ra, left)]
    signal_all(peers)
    tra, tdec = out_ref.shape[1], out_ref.shape[2]
    top = EDGE + tra
    low_half = lax.broadcasted_iota(jnp.int32, (1, N), 1) < 64
    copy = sender(send, recv)

    def pack_left(q, rows):
        return jnp.where(low_half, pltpu.roll(acc_ref[2 * q + 1, 0, rows, :], 64, 1), acc_ref[2 * q, 0, rows, :])

    def pack_right(q, rows):
        return jnp.where(low_half, acc_ref[2 * q, 3, rows, :], pltpu.roll(acc_ref[2 * q + 1, 3, rows, :], 64, 1))

    middle, lower, upper = slice(EDGE, top), slice(0, EDGE), slice(top, top + EDGE)
    for q in range(3):
        out_corners[0, q] = pack_left(q, lower)
        out_corners[1, q] = pack_left(q, upper)
        out_corners[2, q] = pack_right(q, lower)
        out_corners[3, q] = pack_right(q, upper)
        to_left[q] = pack_left(q, middle)
        to_right[q] = pack_right(q, middle)
    wait_all(peers)
    inner, low_rows, high_rows = slice(EDGE, tra - EDGE), slice(0, EDGE), slice(tra - EDGE, tra)
    turns = [copy(i, out_corners.at[i], corners.at[i], (down if i % 2 == 0 else up, dec)) for i in range(4)]
    copies = [
        copy(4, to_left.at[:, inner, :], from_right.at[:, inner, :], (ra, left)),
        copy(5, to_right.at[:, inner, :], from_left.at[:, inner, :], (ra, right)),
        copy(6, acc_ref.at[:, 1:3, lower, :], from_up, (down, dec)),
        copy(7, acc_ref.at[:, 1:3, upper, :], from_down, (up, dec)),
    ]
    for c in turns + copies:
        c.start()
    in_low, in_high, in_left, in_right = edges(n_ra, n_dec, ra, dec)
    for c in turns:
        c.wait_recv()
    to_left[:, high_rows, :] += corners[0] * in_high
    to_right[:, high_rows, :] += corners[2] * in_high
    more = [
        copy(8, to_left.at[:, high_rows, :], from_right.at[:, high_rows, :], (ra, left)),
        copy(9, to_right.at[:, high_rows, :], from_left.at[:, high_rows, :], (ra, right)),
    ]
    for c in more:
        c.start()
    to_left[:, low_rows, :] += corners[1] * in_low
    to_right[:, low_rows, :] += corners[3] * in_low
    more += [
        copy(10, to_left.at[:, low_rows, :], from_right.at[:, low_rows, :], (ra, left)),
        copy(11, to_right.at[:, low_rows, :], from_left.at[:, low_rows, :], (ra, right)),
    ]
    for c in more[2:]:
        c.start()
    for t in range(2):
        out_ref[:, :, t * N : t * N + N] = acc_ref[:, 1 + t, middle, :]
    for c in turns:
        c.wait_send()
    for c in copies[2:]:
        c.wait()
    for t in range(2):
        cols = slice(t * N, t * N + N)
        out_ref[:, high_rows, cols] += from_up[:, t] * in_high
        out_ref[:, low_rows, cols] += from_down[:, t] * in_low
    for c in copies[:2] + more:
        c.wait()
    for q in range(3):
        for src, scale, at_right in ((from_right.at[q], in_right, True), (from_left.at[q], in_left, False)):
            value = src[...] * scale
            other = pltpu.roll(value, 64, 1)
            if at_right:
                cols, keep = slice(tdec - N, tdec), jnp.logical_not(low_half)
            else:
                cols, keep = slice(0, N), low_half
            out_ref[2 * q, :, cols] += jnp.where(keep, value, 0.0)
            out_ref[2 * q + 1, :, cols] += jnp.where(keep, other, 0.0)


def fold(acc, n_ra, n_dec):
    bands, tra, tdec = acc.shape[0], acc.shape[2] - 2 * EDGE, acc.shape[1] * N - 2 * SIDE
    strip = pltpu.VMEM((3, tra, N), F32)
    corner = pltpu.VMEM((4, 3, EDGE, N), F32)
    band = pltpu.VMEM((bands, 2, EDGE, N), F32)
    return pl.pallas_call(
        functools.partial(fold_kernel, n_ra, n_dec),
        out_shape=jax.ShapeDtypeStruct((bands, tra, tdec), F32),
        in_specs=vmem(1),
        out_specs=pl.BlockSpec(memory_space=pltpu.VMEM),
        scratch_shapes=[strip, strip, strip, strip, corner, corner, band, band,
                        pltpu.SemaphoreType.DMA((12,)), pltpu.SemaphoreType.DMA((12,))],
        compiler_params=pltpu.CompilerParams(
            collective_id=1, has_side_effects=True, vmem_limit_bytes=LIMIT),
        cost_estimate=pl.CostEstimate(flops=0, bytes_accessed=40_000_000, transcendentals=0),
    )(acc)


def body(model, observed, inv_var, psf, target_dec, band, offset_ra, offset_dec):
    n_ra, n_dec = lax.axis_size("ra"), lax.axis_size("dec")
    e_dev = observed.shape[0]
    packed = (((target_dec[:, 0] * 8 + band) * 256 + offset_ra) * 256 + offset_dec).reshape(n_dec, e_dev)
    meta = tile_meta(packed)
    back, slots = photometry(meta, packed, psf, observed, inv_var, model, n_ra, n_dec)
    residual, acc = scatter(meta, packed, slots, back, model.shape, n_dec)
    return residual, fold(acc, n_ra, n_dec)


def solution(mesh):
    placed = (
        P(None, "ra", "dec"),
        P(("ra", "dec"), None),
        P(("ra", "dec"), None),
        P(("ra", "dec"), None),
        P("ra", None),
        P("ra"),
        P("ra"),
        P("ra"),
    )
    return jax.shard_map(
        body,
        mesh=mesh,
        in_specs=placed,
        out_specs=(P(("ra", "dec"), None), P(None, "ra", "dec")),
        check_vma=False,
    )
```

```python
import functools
import math

import jax
import jax.numpy as jnp
import ml_dtypes
import numpy as np
from jax import lax
from jax.experimental import pallas as pl
from jax.experimental.pallas import tpu as pltpu
from jax.sharding import PartitionSpec as P

K = 63
C = 66
CAP = 4
GROUP = 16
RING = 4
PEERS = (
    ((2, 0), (0, 2), (2, 2), (0, 0)),
    ((2, 1), (2, 3), (1, 2), (3, 2)),
    ((1, 1), (3, 3), (1, 3), (3, 1)),
    ((1, 0), (3, 0), (0, 1), (0, 3)),
)
SLOT = 36
B_LAG = 3
N = 128
PAIRS = 33
PAD = 40
PSF_ROWS = 32
EDGE = 64
SIDE = 128
MAIN_LIMIT = 60 * 1024 * 1024
SMALL_LIMIT = 18 * 1024 * 1024
SCATTER_LIMIT = 18 * 1024 * 1024
MESH = pl.DeviceIdType.MESH
F32 = jnp.float32
BF16 = jnp.bfloat16


def np_split(table):
    high = table.astype(np.float32).astype(ml_dtypes.bfloat16)
    low = (table - high.astype(np.float64)).astype(np.float32).astype(ml_dtypes.bfloat16)
    return high, low


def make_tables():
    theta = 2.0 * math.pi * (np.arange(64) + 0.5) / N

    def to_freq(columns):
        angle = np.asarray(columns)[:, None] * theta[None, :]
        return np.concatenate([np.cos(angle), -np.sin(angle)], axis=1)

    def rows_cs(out_index, in_index, sign):
        angle = 2.0 * math.pi * ((out_index[:, None] * in_index[None, :]) % N) / N
        return np.cos(angle), sign * np.sin(angle)

    full = np.arange(N)
    zero = np.zeros((N, N))
    zero16 = zero.astype(ml_dtypes.bfloat16)

    def wide(table):
        high, low = np_split(table)
        return np.block([[high, low], [high, zero16]])

    patch_cols = wide(to_freq(full))
    psf_cols = np.zeros((N, 2 * N))
    psf_cols[:K, :N] = to_freq(np.arange(K))
    psf_cols[K : 2 * K, N:] = to_freq(np.arange(K))
    psf_h, psf_l = np_split(psf_cols)
    psf_cols = np.concatenate([psf_h, psf_h, psf_l], axis=0)

    def left(out_index, in_index, sign, keep_in=None, keep_out=None):
        cosine, sine = rows_cs(out_index, in_index, sign)
        table = np.concatenate([cosine, sine], axis=1)
        if keep_in is not None:
            table = table * np.concatenate([keep_in, keep_in])[None, :]
        if keep_out is not None:
            table = table * keep_out[:, None]
        return np.concatenate(np_split(table), axis=0)

    patch_rows = left(full, full, 1.0)
    psf_index = np.concatenate([2 * np.arange(32), 2 * np.arange(32) + 1])
    psf_rows = left(full, psf_index, 1.0, keep_in=(psf_index < K).astype(np.float64))
    within = (np.arange(PAD) < PAIRS).astype(np.float64)
    inner_keep = np.concatenate([within, within])
    inner_index = np.concatenate([K - 1 + 2 * np.arange(PAD), K + 2 * np.arange(PAD)])
    pred_rows = left(inner_index, full, -1.0, keep_out=inner_keep)
    res_rows = left(full, inner_index, 1.0, keep_in=inner_keep)
    back_rows = left(full, full, -1.0)
    scale = 2.0 / (N * N)
    inner_cols = K - 1 + np.arange(C)
    pred_cols = np.zeros((2 * N, 2 * N))
    pred_cols[:N, :C] = scale * to_freq(inner_cols).T
    pred_cols[N:, C : 2 * C] = scale * to_freq(inner_cols).T
    pred_cols = np.concatenate(np_split(pred_cols), axis=0)
    res_cols = np.zeros((2 * N, 2 * N))
    res_cols[:C, :N] = to_freq(inner_cols)
    res_cols[C : 2 * C, N:] = to_freq(inner_cols)
    res_cols = np.concatenate(np_split(res_cols), axis=0)
    back_cols = wide(scale * to_freq(full).T)
    psf_rows = np.concatenate([np.concatenate([psf_rows[:N], psf_rows[:N]], axis=1),
                               np.concatenate([psf_rows[N:], np.zeros_like(psf_rows[N:])], axis=1)], axis=0)
    tables = (patch_cols, patch_rows, psf_cols, psf_rows, pred_rows, pred_cols, res_cols, res_rows,
              back_rows, back_cols)
    places, at = [], 0
    for table in tables:
        places.append((at, table.shape[0]))
        at += table.shape[0]
    joined = np.zeros((at, 2 * N), ml_dtypes.bfloat16)
    for (start, rows), table in zip(places, tables):
        joined[start : start + rows, : table.shape[1]] = table
    return joined, places


def split(x):
    high = x.astype(BF16)
    return high, (x - high.astype(F32)).astype(BF16)


def dot(a, b):
    return jnp.dot(a, b, preferred_element_type=F32)


def right_wide(x, table_ref):
    high, low = split(x)
    both = dot(jnp.concatenate([high, low], axis=1), table_ref[...])
    return both[:, :N] + both[:, N:]


def right_three(x, table_ref):
    high, low = split(x)
    depth = x.shape[1]
    return (dot(high, table_ref[:depth, :]) + dot(low, table_ref[:depth, :])
            + dot(high, table_ref[depth:, :]))


def left_three(table_ref, x):
    rows = table_ref.shape[0] // 2
    high, low = split(x)
    depth = x.shape[0]
    both = dot(table_ref[:, :depth], high)
    return both[:rows] + both[rows:] + dot(table_ref[:rows, :depth], low)


def turned(y, sign):
    return pltpu.roll(y, 64, 1) * sign


def stacked(parts, sign):
    return jnp.concatenate(
        [jnp.concatenate([y, turned(y, sign)], axis=0) for y in parts], axis=1)


def lanes():
    lane = lax.broadcasted_iota(jnp.int32, (1, N), 1)
    return lane, jnp.where(lane < 64, 1.0, -1.0).astype(F32), lane < 64


def place_of(code):
    code = jnp.maximum(code - 1, 0)
    which = lax.shift_right_logical(code, 16)
    row = lax.bitwise_and(lax.shift_right_logical(code, 8), 255) + (EDGE - K + 1)
    column = lax.bitwise_and(code, 255) + (SIDE - K + 1)
    return which, lax.shift_right_logical(column, 7), row, lax.bitwise_and(column, N - 1)


def cut(code, ext_ref):
    which, at, row, over = place_of(code)
    rows = pl.ds(row, N)
    window = jnp.concatenate([ext_ref[which, at, rows, :], ext_ref[which, at + 1, rows, :]], axis=1)
    return pltpu.roll(window, lax.bitwise_and(2 * N - over, 2 * N - 1), 1)[:, :N]


def halves(k, low_half):
    rk = pltpu.roll(k, 64, 1)
    return jnp.where(low_half, k, rk), jnp.where(low_half, -rk, k)


def predict(patches, psfs, tables):
    patch_cols, patch_rows, psf_cols, psf_rows, pred_rows, pred_cols = tables
    count = len(patches)
    lane, sign, low_half = lanes()
    y = right_wide(jnp.concatenate(patches, axis=0), patch_cols)
    z = left_three(patch_rows, stacked([y[e * N : e * N + N] for e in range(count)], sign))
    pairs = []
    for x in psfs:
        both = jnp.concatenate([pltpu.roll(x, 1, 0), x], axis=1)
        pairs.append(pltpu.roll(both, N, 1, stride=2, stride_axis=0)[:, :N])
    high, low = split(jnp.concatenate(pairs, axis=0))
    y = dot(jnp.concatenate([high, low], axis=1), psf_cols[: 2 * N, :]) + dot(high, psf_cols[2 * N :, :])
    y = stacked([jnp.concatenate([y[32 * e : 32 * e + 32, :N], y[32 * e : 32 * e + 32, N:]], axis=0)
                 for e in range(count)], sign)
    high, low = split(y)
    khat = (dot(psf_rows[:N, :], jnp.concatenate([high, low], axis=0))
            + dot(psf_rows[N:, :N], high))
    khat = [khat[:, e * N : e * N + N] for e in range(count)]
    spec = []
    for e in range(count):
        k_re, k_im = halves(khat[e], low_half)
        p = z[:, e * N : e * N + N]
        rp = pltpu.roll(p, 64, 1)
        spec.append(jnp.concatenate(
            [p * k_re + rp * k_im, (rp * k_re - p * k_im) * sign], axis=0))
    u = left_three(pred_rows, jnp.concatenate(spec, axis=1))
    u = jnp.concatenate(
        [jnp.concatenate([u[:PAD, e * N : e * N + N], u[PAD:, e * N : e * N + N]], axis=1)
         for e in range(count)], axis=0)
    predicted = right_three(u, pred_cols)
    last = lax.broadcasted_iota(jnp.int32, (PAD, 1), 0) == PAIRS - 1
    flat = []
    for e in range(count):
        image = pltpu.roll(predicted[e * PAD : e * PAD + PAD], 0, 1, stride=4, stride_axis=0)
        front, rear = image[:, :N], image[:, N:]
        flat.append(jnp.where(last, 0.0, front) + pltpu.roll(rear, 1, 0)
                    + pltpu.roll(jnp.where(last, front, 0.0), 2, 0))
    return khat, flat


def adjoint(resids, khat, tables):
    res_cols, res_rows, back_rows, back_cols = tables
    count = len(resids)
    lane, sign, low_half = lanes()
    number = lax.broadcasted_iota(jnp.int32, (PAD, 1), 0)
    last = number == PAIRS - 1
    turn = lax.bitwise_and(lane + 4 * number, N - 1)
    pairs = []
    for resid in resids:
        front = jnp.take_along_axis(resid, turn, axis=1, mode="promise_in_bounds")
        rear = jnp.take_along_axis(pltpu.roll(resid, PAD - 1, 0), turn, axis=1, mode="promise_in_bounds")
        pairs.append(jnp.concatenate(
            [jnp.where(lane + 4 * number < N, front, rear),
             jnp.where(last, pltpu.roll(resid, PAD - 2, 0), rear)], axis=1))
    v = right_three(jnp.concatenate(pairs, axis=0), res_cols)
    v = [jnp.concatenate([v[e * PAD : e * PAD + PAD, :N], v[e * PAD : e * PAD + PAD, N:]], axis=0)
         for e in range(count)]
    r = left_three(res_rows, stacked(v, sign))
    spec = []
    for e in range(count):
        k_re, k_im = halves(khat[e], low_half)
        p = r[:, e * N : e * N + N]
        rp = pltpu.roll(p, 64, 1)
        spec.append(jnp.concatenate(
            [p * k_re - rp * k_im, (rp * k_re + p * k_im) * sign], axis=0))
    u = left_three(back_rows, jnp.concatenate(spec, axis=1))
    back = right_wide(jnp.concatenate([u[:, e * N : e * N + N] for e in range(count)], axis=0), back_cols)
    return [back[e * N : e * N + N] for e in range(count)]


def three(x):
    high = x.astype(BF16)
    rest = x - high.astype(F32)
    middle = rest.astype(BF16)
    return jnp.concatenate([high, middle, (rest - middle.astype(F32)).astype(BF16)], axis=0)


def own_places(packed_ref, own):
    row = lax.shift_right_logical(packed_ref[pl.ds(own, 1), :], 19)
    count = row.shape[1]
    first = lax.broadcasted_iota(jnp.int32, (count, count), 0)
    second = lax.broadcasted_iota(jnp.int32, (count, count), 1)
    column = jnp.sum(jnp.where(first == second, row, 0), axis=1, keepdims=True)
    return row, column, first, second


def places_of_tile(packed_ref, own):
    packed = packed_ref[...]
    count = packed.shape[1]
    here = lax.shift_right_logical(packed, 19) == own
    code = lax.bitwise_and(packed, (1 << 19) - 1) + 1
    first = lax.broadcasted_iota(jnp.int32, (count, count), 0)
    second = lax.broadcasted_iota(jnp.int32, (count, count), 1)
    earlier = (first < second).astype(F32).astype(BF16)
    rank = dot(here.astype(F32).astype(BF16), earlier)
    return jnp.concatenate(
        [jnp.sum(jnp.where(jnp.logical_and(here, rank == float(s)), code, 0), axis=1, keepdims=True)
         for s in range(CAP)], axis=1)


def neighbours(n_ra, n_dec):
    ra, dec = lax.axis_index("ra"), lax.axis_index("dec")
    up, down = lax.rem(ra + 1, n_ra), lax.rem(ra + n_ra - 1, n_ra)
    right, left = lax.rem(dec + 1, n_dec), lax.rem(dec + n_dec - 1, n_dec)
    return ra, dec, up, down, right, left


def signal_all(devices):
    for device in devices:
        pl.semaphore_signal(pltpu.get_barrier_semaphore(), inc=1, device_id=device, device_id_type=MESH)


def wait_all(devices):
    pl.semaphore_wait(pltpu.get_barrier_semaphore(), len(devices))


def moved(dec, shift, n_dec, sign):
    rings = n_dec // RING
    outer = lax.rem(dec // RING + rings + sign * shift[0], rings)
    inner = lax.rem(lax.rem(dec, RING) + RING + sign * shift[1], RING)
    return outer * RING + inner


def shifts():
    return [(j * len(PEERS[j]) + i, shift) for j in range(len(PEERS)) for i, shift in enumerate(PEERS[j])
            if shift != (0, 0)]


def edges(n_ra, n_dec, ra, dec):
    zero, one = jnp.zeros((), F32), jnp.ones((), F32)
    return (jnp.where(ra > 0, one, zero), jnp.where(ra < n_ra - 1, one, zero),
            jnp.where(dec > 0, one, zero), jnp.where(dec < n_dec - 1, one, zero))


def sender(send, recv):
    def copy(index, src, dst, other):
        return pltpu.make_async_remote_copy(
            src_ref=src, dst_ref=dst, send_sem=send.at[index], recv_sem=recv.at[index],
            device_id=other, device_id_type=MESH)
    return copy


def rows_of(index, size):
    return pl.ds(pl.multiple_of(index * size, 8), size)


def slot_rows(index, s):
    return pl.ds(pl.multiple_of(index * (CAP * SLOT), 8) + s * SLOT, SLOT)


def slot_chooser(packed_ref, dec, n_dec):
    row, column, first, second = own_places(packed_ref, dec)
    count = row.shape[1]
    slots = CAP * n_dec
    rank = jnp.sum(jnp.where(jnp.logical_and(column == row, first < second), 1, 0), axis=0, keepdims=True)
    place = row * CAP + rank
    chosen = (lax.broadcasted_iota(jnp.int32, (slots, count), 0) == place).astype(F32).astype(BF16)
    return jnp.concatenate([chosen] * 3, axis=1)


def to_slots(chosen, ref, out_ref, rows):
    width, slots = ref.shape[1], chosen.shape[0]
    for start in range(0, rows, 4):
        end = min((start + 4) * N, width)
        if start * N < width:
            y = dot(chosen, three(ref[:, start * N : end]))
            if end < (start + 4) * N:
                y = jnp.concatenate([y, jnp.zeros((slots, (start + 4) * N - end), F32)], axis=1)
        else:
            y = jnp.zeros((slots, 4 * N), F32)
        for t in range(4):
            out_ref[pl.ds(start + t, slots, stride=rows), :] = y[:, t * N : t * N + N]


def photometry_kernel(n_ra, n_dec, places, meta_ref, packed_ref, *refs):
    inputs, refs = refs[:5], refs[5:]
    (back_ref, residual_ref, ext_ref, to_right, to_left, from_left, from_right, corners, psf_out, psf_in,
     obs_slots, var_slots, pred_out, pred_in, resid_in, khat_ref, send, recv, send_psf, recv_psf,
     send_pred, recv_pred, send_res, recv_res, psf_ref, obs_ref, var_ref, model_ref, joined, load) = refs
    tables = [joined.at[pl.ds(start, rows), :] for start, rows in places]
    loads = [pltpu.make_async_copy(src, dst, load.at[i]) for i, (src, dst) in enumerate(
        zip(inputs, (psf_ref, obs_ref, var_ref, model_ref, joined)))]
    for i in (3, 0, 1, 2, 4):
        loads[i].start()
    ra, dec, up, down, right, left = neighbours(n_ra, n_dec)
    peers = [(ra, moved(dec, shift, n_dec, 1)) for _, shift in shifts()] + [(up, dec), (down, dec)]
    signal_all(peers)
    loads[3].wait()
    tra, tdec = model_ref.shape[1], model_ref.shape[2]
    top = EDGE + tra
    low_half = lax.broadcasted_iota(jnp.int32, (1, N), 1) < 64
    copy = sender(send, recv)
    for q in range(3):
        to_right[q] = jnp.where(
            low_half, pltpu.roll(model_ref[2 * q + 1, :, tdec - N :], 64, 1), model_ref[2 * q, :, tdec - N :])
        to_left[q] = jnp.where(
            low_half, model_ref[2 * q, :, :N], pltpu.roll(model_ref[2 * q + 1, :, :N], 64, 1))
    wait_all(peers)
    ends = (slice(tra - EDGE, tra), slice(0, EDGE), slice(EDGE, tra - EDGE))
    sides = []
    for i, rows in enumerate(ends):
        sides += [copy(2 * i, to_right.at[:, rows, :], from_left.at[:, rows, :], (ra, right)),
                  copy(2 * i + 1, to_left.at[:, rows, :], from_right.at[:, rows, :], (ra, left))]
    for c in sides:
        c.start()
    copies = []
    for t in range(2):
        cols = slice(t * N, t * N + N)
        copies += [copy(6 + t, model_ref.at[:, tra - EDGE :, cols], ext_ref.at[:, 1 + t, :EDGE, :], (up, dec)),
                   copy(8 + t, model_ref.at[:, :EDGE, cols], ext_ref.at[:, 1 + t, top:, :], (down, dec))]
    for c in copies:
        c.start()
    chosen = slot_chooser(packed_ref, dec, n_dec)
    loads[0].wait()
    to_slots(chosen, psf_ref, psf_out, PSF_ROWS)
    moves = {}
    here = rows_of(dec, CAP * PSF_ROWS)
    for d, shift in shifts():
        tile = moved(dec, shift, n_dec, 1)
        moves[shift] = sender(send_psf, recv_psf)(
            d, psf_out.at[rows_of(tile, CAP * PSF_ROWS), :], psf_in.at[here, :], (ra, tile))

    def send_psfs(group):
        for shift in group:
            if shift in moves:
                moves[shift].start()

    send_psfs(PEERS[0])
    psf_in[here, :] = psf_out[here, :]
    for t in range(2):
        ext_ref[:, 1 + t, EDGE:top, :] = model_ref[:, :, t * N : t * N + N]
    loads[1].wait()
    to_slots(chosen, obs_ref, obs_slots, SLOT)
    more = []
    for i in range(2):
        for c in sides[2 * i : 2 * i + 2]:
            c.wait_recv()
        other = (up, dec) if i == 0 else (down, dec)
        now = [copy(10 + i, from_left.at[:, ends[i], :], corners.at[i], other),
               copy(12 + i, from_right.at[:, ends[i], :], corners.at[2 + i], other)]
        for c in now:
            c.start()
        more += now
    loads[2].wait()
    to_slots(chosen, var_ref, var_slots, SLOT)
    for c in sides[4:]:
        c.wait_recv()
    for group in PEERS[1:]:
        send_psfs(group)
    in_low, in_high, in_left, in_right = edges(n_ra, n_dec, ra, dec)

    def place(pieces):
        for src, q, col, rows, scale in pieces:
            value = src[...] * scale
            ext_ref[2 * q, col, rows, :] = value
            ext_ref[2 * q + 1, col, rows, :] = pltpu.roll(value, 64, 1)

    middle, low, high = slice(EDGE, top), slice(0, EDGE), slice(top, top + EDGE)
    place([(from_left.at[q], q, 0, middle, in_left) for q in range(3)]
          + [(from_right.at[q], q, 3, middle, in_right) for q in range(3)])
    for c in copies + more:
        c.wait()

    @pl.when(ra == 0)
    def _():
        ext_ref[:, 1:3, :EDGE, :] = jnp.zeros((ext_ref.shape[0], 2, EDGE, N), F32)

    @pl.when(ra == n_ra - 1)
    def _():
        ext_ref[:, 1:3, top:, :] = jnp.zeros((ext_ref.shape[0], 2, EDGE, N), F32)

    for q in range(3):
        place([(corners.at[0, q], q, 0, low, in_low * in_left), (corners.at[1, q], q, 0, high, in_high * in_left),
               (corners.at[2, q], q, 3, low, in_low * in_right), (corners.at[3, q], q, 3, high, in_high * in_right)])
    for c in sides:
        c.wait_send()

    own = rows_of(dec, CAP * SLOT)
    steps = len(PEERS)
    pred_moves, res_moves = {}, {}
    for d, shift in shifts():
        owner, tile = moved(dec, shift, n_dec, -1), moved(dec, shift, n_dec, 1)
        pred_moves[shift] = sender(send_pred, recv_pred)(
            d, pred_out.at[rows_of(owner, CAP * SLOT), :], pred_in.at[own, :], (ra, owner))
        res_moves[shift] = sender(send_res, recv_res)(
            d, residual_ref.at[rows_of(tile, CAP * SLOT), :], resid_in.at[own, :], (ra, tile))

    def owned(j):
        return [(moved(dec, PEERS[j][e // CAP], n_dec, -1), e % CAP) for e in range(GROUP)]

    loads[4].wait()
    for j in range(steps + B_LAG):
        if j < steps:
            for shift in PEERS[j]:
                if shift in moves:
                    moves[shift].wait_recv()
            which = owned(j)
            khat, flat = predict(
                [cut(meta_ref[o, s], ext_ref) for o, s in which],
                [psf_in[rows_of(o * CAP + s, PSF_ROWS), :] for o, s in which],
                tables[:6])
            for (o, s), k, f in zip(which, khat, flat):
                khat_ref[o * CAP + s] = k
                pred_out[slot_rows(o, s), :] = f[:SLOT]
            for shift in PEERS[j]:
                if shift in pred_moves:
                    pred_moves[shift].start()
        if 1 <= j <= steps:
            for shift in PEERS[j - 1]:
                tile = rows_of(moved(dec, shift, n_dec, 1), CAP * SLOT)
                if shift in pred_moves:
                    pred_moves[shift].wait_recv()
                    residual_ref[tile, :] = var_slots[tile, :] * (pred_in[tile, :] - obs_slots[tile, :])
                    res_moves[shift].start()
                else:
                    resid = var_slots[own, :] * (pred_out[own, :] - obs_slots[own, :])
                    residual_ref[own, :] = resid
                    resid_in[own, :] = resid
        if j >= B_LAG:
            for shift in PEERS[j - B_LAG]:
                if shift in res_moves:
                    res_moves[shift].wait_recv()
            which = owned(j - B_LAG)
            back = adjoint(
                [jnp.concatenate([resid_in[slot_rows(o, s), :], jnp.zeros((PAD - SLOT, N), F32)], axis=0)
                 for o, s in which],
                [khat_ref[o * CAP + s] for o, s in which], tables[6:])
            for (o, s), image in zip(which, back):
                back_ref[o * CAP + s] = image
    for shift in pred_moves:
        moves[shift].wait_send()
        pred_moves[shift].wait_send()
        res_moves[shift].wait_send()


def vmem(count):
    return [pl.BlockSpec(memory_space=pltpu.VMEM)] * count


def photometry(meta, packed, psf, obs, var, model, n_ra, n_dec):
    bands, tra, tdec = model.shape
    strip = pltpu.VMEM((3, tra, N), F32)
    slots = n_dec * CAP
    image, small = pltpu.VMEM((slots * SLOT, N), F32), pltpu.VMEM((slots * PSF_ROWS, N), F32)
    several, many = pltpu.SemaphoreType.DMA((14,)), pltpu.SemaphoreType.DMA((n_dec,))
    joined, places = make_tables()
    return pl.pallas_call(
        functools.partial(photometry_kernel, n_ra, n_dec, places),
        out_shape=[
            jax.ShapeDtypeStruct((slots, N, N), F32),
            jax.ShapeDtypeStruct((slots * SLOT, N), F32),
        ],
        in_specs=[pl.BlockSpec(memory_space=pltpu.SMEM)] + vmem(1) + [pl.BlockSpec(memory_space=pltpu.HBM)] * 5,
        out_specs=vmem(2),
        scratch_shapes=[pltpu.VMEM((bands, (tdec + 2 * SIDE) // N, tra + 2 * EDGE, N), F32),
                        strip, strip, strip, strip, pltpu.VMEM((4, 3, EDGE, N), F32), small, small,
                        image, image, image, image, image, pltpu.VMEM((slots, N, N), F32),
                        several, several, many, many, many, many, many, many]
        + [pltpu.VMEM(o.shape, o.dtype) for o in (psf, obs, var, model, joined)]
        + [pltpu.SemaphoreType.DMA((5,))],
        compiler_params=pltpu.CompilerParams(
            collective_id=0, has_side_effects=True, vmem_limit_bytes=MAIN_LIMIT),
        cost_estimate=pl.CostEstimate(flops=0, bytes_accessed=40_000_000, transcendentals=0),
    )(meta, packed, psf, obs, var, model, jnp.asarray(joined))


def meta_kernel(packed_ref, meta_ref):
    meta_ref[...] = places_of_tile(packed_ref, lax.axis_index("dec"))


def tile_meta(packed):
    return pl.pallas_call(
        meta_kernel, out_shape=jax.ShapeDtypeStruct((packed.shape[0], CAP), jnp.int32))(packed)


def scatter_kernel(n_dec, meta_ref, packed_ref, slots_ref, back_ref, residual_ref, acc_ref):
    step = pl.program_id(0)

    @pl.when(step == 0)
    def _():
        acc_ref[...] = jnp.zeros_like(acc_ref)
        row, column, first, second = own_places(packed_ref, lax.axis_index("dec"))
        count = row.shape[1]
        slots = CAP * n_dec
        rank = jnp.sum(jnp.where(jnp.logical_and(column == row, second < first), 1, 0), axis=1, keepdims=True)
        place = column * CAP + rank
        chosen = (lax.broadcasted_iota(jnp.int32, (count, slots), 1) == place).astype(F32).astype(BF16)
        chosen = jnp.concatenate([chosen] * 3, axis=1)
        width = residual_ref.shape[1]
        for start in range(0, SLOT, 4):
            if start * N >= width:
                break
            x = jnp.concatenate(
                [slots_ref[pl.ds(start + t, slots, stride=SLOT), :] for t in range(4)], axis=1)
            y = dot(chosen, three(x))
            end = min((start + 4) * N, width)
            residual_ref[:, start * N : end] = y[:, : end - start * N]

    for e in range(GROUP):
        which, at, row, over = place_of(meta_ref[step * (GROUP // CAP) + e // CAP, e % CAP])
        image = back_ref[e]
        image = pltpu.roll(jnp.concatenate([image, jnp.zeros_like(image)], axis=1), over, 1)
        rows = pl.ds(row, N)
        acc_ref[which, at, rows, :] += image[:, :N]
        acc_ref[which, at + 1, rows, :] += image[:, N:]


def scatter(meta, packed, residual, back, shape, n_dec):
    def whole(block):
        return pl.BlockSpec(block, lambda i, meta: (0,) * len(block), pipeline_mode=pl.Buffered(1))

    bands, tra, tdec = shape
    wide = (bands, (tdec + 2 * SIDE) // N, tra + 2 * EDGE, N)
    out = (packed.shape[1], C * C)
    return pl.pallas_call(
        functools.partial(scatter_kernel, n_dec),
        grid_spec=pltpu.PrefetchScalarGridSpec(
            num_scalar_prefetch=1,
            grid=(back.shape[0] // GROUP,),
            in_specs=[whole(packed.shape), whole(residual.shape), pl.BlockSpec((GROUP, N, N), lambda i, meta: (i, 0, 0))],
            out_specs=[whole(out), whole(wide)],
        ),
        out_shape=[jax.ShapeDtypeStruct(out, F32), jax.ShapeDtypeStruct(wide, F32)],
        compiler_params=pltpu.CompilerParams(vmem_limit_bytes=SCATTER_LIMIT),
    )(meta, packed, residual, back)


def fold_kernel(n_ra, n_dec, acc_ref, out_ref, to_right, to_left, from_left, from_right, out_corners, corners,
                from_up, from_down, send, recv):
    ra, dec, up, down, right, left = neighbours(n_ra, n_dec)
    peers = [(up, dec), (down, dec), (ra, right), (ra, left)]
    signal_all(peers)
    tra, tdec = out_ref.shape[1], out_ref.shape[2]
    top = EDGE + tra
    low_half = lax.broadcasted_iota(jnp.int32, (1, N), 1) < 64
    copy = sender(send, recv)

    def pack_left(q, rows):
        return jnp.where(low_half, pltpu.roll(acc_ref[2 * q + 1, 0, rows, :], 64, 1), acc_ref[2 * q, 0, rows, :])

    def pack_right(q, rows):
        return jnp.where(low_half, acc_ref[2 * q, 3, rows, :], pltpu.roll(acc_ref[2 * q + 1, 3, rows, :], 64, 1))

    middle, lower, upper = slice(EDGE, top), slice(0, EDGE), slice(top, top + EDGE)
    for q in range(3):
        out_corners[0, q] = pack_left(q, lower)
        out_corners[1, q] = pack_left(q, upper)
        out_corners[2, q] = pack_right(q, lower)
        out_corners[3, q] = pack_right(q, upper)
        to_left[q] = pack_left(q, middle)
        to_right[q] = pack_right(q, middle)
    wait_all(peers)
    inner, low_rows, high_rows = slice(EDGE, tra - EDGE), slice(0, EDGE), slice(tra - EDGE, tra)
    turns = [copy(i, out_corners.at[i], corners.at[i], (down if i % 2 == 0 else up, dec)) for i in range(4)]
    copies = [
        copy(4, to_left.at[:, inner, :], from_right.at[:, inner, :], (ra, left)),
        copy(5, to_right.at[:, inner, :], from_left.at[:, inner, :], (ra, right)),
        copy(6, acc_ref.at[:, 1:3, lower, :], from_up, (down, dec)),
        copy(7, acc_ref.at[:, 1:3, upper, :], from_down, (up, dec)),
    ]
    for c in turns + copies:
        c.start()
    in_low, in_high, in_left, in_right = edges(n_ra, n_dec, ra, dec)
    for c in turns:
        c.wait_recv()
    to_left[:, high_rows, :] += corners[0] * in_high
    to_right[:, high_rows, :] += corners[2] * in_high
    more = [
        copy(8, to_left.at[:, high_rows, :], from_right.at[:, high_rows, :], (ra, left)),
        copy(9, to_right.at[:, high_rows, :], from_left.at[:, high_rows, :], (ra, right)),
    ]
    for c in more:
        c.start()
    to_left[:, low_rows, :] += corners[1] * in_low
    to_right[:, low_rows, :] += corners[3] * in_low
    more += [
        copy(10, to_left.at[:, low_rows, :], from_right.at[:, low_rows, :], (ra, left)),
        copy(11, to_right.at[:, low_rows, :], from_left.at[:, low_rows, :], (ra, right)),
    ]
    for c in more[2:]:
        c.start()
    for t in range(2):
        out_ref[:, :, t * N : t * N + N] = acc_ref[:, 1 + t, middle, :]
    for c in turns:
        c.wait_send()
    for c in copies[2:]:
        c.wait()
    for t in range(2):
        cols = slice(t * N, t * N + N)
        out_ref[:, high_rows, cols] += from_up[:, t] * in_high
        out_ref[:, low_rows, cols] += from_down[:, t] * in_low
    for c in copies[:2] + more:
        c.wait()
    for q in range(3):
        for src, scale, at_right in ((from_right.at[q], in_right, True), (from_left.at[q], in_left, False)):
            value = src[...] * scale
            other = pltpu.roll(value, 64, 1)
            if at_right:
                cols, keep = slice(tdec - N, tdec), jnp.logical_not(low_half)
            else:
                cols, keep = slice(0, N), low_half
            out_ref[2 * q, :, cols] += jnp.where(keep, value, 0.0)
            out_ref[2 * q + 1, :, cols] += jnp.where(keep, other, 0.0)


def fold(acc, n_ra, n_dec):
    bands, tra, tdec = acc.shape[0], acc.shape[2] - 2 * EDGE, acc.shape[1] * N - 2 * SIDE
    strip = pltpu.VMEM((3, tra, N), F32)
    corner = pltpu.VMEM((4, 3, EDGE, N), F32)
    band = pltpu.VMEM((bands, 2, EDGE, N), F32)
    return pl.pallas_call(
        functools.partial(fold_kernel, n_ra, n_dec),
        out_shape=jax.ShapeDtypeStruct((bands, tra, tdec), F32),
        in_specs=vmem(1),
        out_specs=pl.BlockSpec(memory_space=pltpu.VMEM),
        scratch_shapes=[strip, strip, strip, strip, corner, corner, band, band,
                        pltpu.SemaphoreType.DMA((12,)), pltpu.SemaphoreType.DMA((12,))],
        compiler_params=pltpu.CompilerParams(
            collective_id=1, has_side_effects=True, vmem_limit_bytes=SMALL_LIMIT),
        cost_estimate=pl.CostEstimate(flops=0, bytes_accessed=40_000_000, transcendentals=0),
    )(acc)


def body(model, observed, inv_var, psf, target_dec, band, offset_ra, offset_dec):
    n_ra, n_dec = lax.axis_size("ra"), lax.axis_size("dec")
    e_dev = observed.shape[0]
    packed = (((target_dec[:, 0] * 8 + band) * 256 + offset_ra) * 256 + offset_dec).reshape(n_dec, e_dev)
    meta = tile_meta(packed)
    back, slots = photometry(meta, packed, psf, observed, inv_var, model, n_ra, n_dec)
    residual, acc = scatter(meta, packed, slots, back, model.shape, n_dec)
    return residual, fold(acc, n_ra, n_dec)


def solution(mesh):
    placed = (
        P(None, "ra", "dec"),
        P(("ra", "dec"), None),
        P(("ra", "dec"), None),
        P(("ra", "dec"), None),
        P("ra", None),
        P("ra"),
        P("ra"),
        P("ra"),
    )
    return jax.shard_map(
        body,
        mesh=mesh,
        in_specs=placed,
        out_specs=(P(("ra", "dec"), None), P(None, "ra", "dec")),
        check_vma=False,
    )
```

```python
import functools
import math

import jax
import jax.numpy as jnp
import ml_dtypes
import numpy as np
from jax import lax
from jax.experimental import pallas as pl
from jax.experimental.pallas import tpu as pltpu
from jax.sharding import PartitionSpec as P

K = 63
C = 66
CAP = 4
GROUP = 16
RING = 4
PEERS = (
    ((2, 0), (0, 2), (2, 2), (0, 0)),
    ((2, 1), (2, 3), (1, 2), (3, 2)),
    ((1, 1), (3, 3), (1, 3), (3, 1)),
    ((1, 0), (3, 0), (0, 1), (0, 3)),
)
SLOT = 36
B_LAG = 3
N = 128
PAIRS = 33
PAD = 40
PSF_ROWS = 32
EDGE = 64
SIDE = 128
MAIN_LIMIT = 60 * 1024 * 1024
SMALL_LIMIT = 18 * 1024 * 1024
SCATTER_LIMIT = 18 * 1024 * 1024
MESH = pl.DeviceIdType.MESH
F32 = jnp.float32
BF16 = jnp.bfloat16


def np_split(table):
    high = table.astype(np.float32).astype(ml_dtypes.bfloat16)
    low = (table - high.astype(np.float64)).astype(np.float32).astype(ml_dtypes.bfloat16)
    return high, low


def make_tables():
    theta = 2.0 * math.pi * (np.arange(64) + 0.5) / N

    def to_freq(columns):
        angle = np.asarray(columns)[:, None] * theta[None, :]
        return np.concatenate([np.cos(angle), -np.sin(angle)], axis=1)

    def rows_cs(out_index, in_index, sign):
        angle = 2.0 * math.pi * ((out_index[:, None] * in_index[None, :]) % N) / N
        return np.cos(angle), sign * np.sin(angle)

    full = np.arange(N)
    zero = np.zeros((N, N))
    zero16 = zero.astype(ml_dtypes.bfloat16)

    def wide(table):
        high, low = np_split(table)
        return np.block([[high, low], [high, zero16]])

    patch_cols = wide(to_freq(full))
    psf_cols = np.zeros((N, 2 * N))
    psf_cols[:K, :N] = to_freq(np.arange(K))
    psf_cols[K : 2 * K, N:] = to_freq(np.arange(K))
    psf_h, psf_l = np_split(psf_cols)
    psf_cols = np.concatenate([psf_h, psf_h, psf_l], axis=0)

    def left(out_index, in_index, sign, keep_in=None, keep_out=None):
        cosine, sine = rows_cs(out_index, in_index, sign)
        table = np.concatenate([cosine, sine], axis=1)
        if keep_in is not None:
            table = table * np.concatenate([keep_in, keep_in])[None, :]
        if keep_out is not None:
            table = table * keep_out[:, None]
        return np.concatenate(np_split(table), axis=0)

    patch_rows = left(full, full, 1.0)
    psf_index = np.concatenate([2 * np.arange(32), 2 * np.arange(32) + 1])
    psf_rows = left(full, psf_index, 1.0, keep_in=(psf_index < K).astype(np.float64))
    within = (np.arange(PAD) < PAIRS).astype(np.float64)
    inner_keep = np.concatenate([within, within])
    inner_index = np.concatenate([K - 1 + 2 * np.arange(PAD), K + 2 * np.arange(PAD)])
    pred_rows = left(inner_index, full, -1.0, keep_out=inner_keep)
    res_rows = left(full, inner_index, 1.0, keep_in=inner_keep)
    back_rows = left(full, full, -1.0)
    scale = 2.0 / (N * N)
    inner_cols = K - 1 + np.arange(C)
    pred_cols = np.zeros((2 * N, 2 * N))
    pred_cols[:N, :C] = scale * to_freq(inner_cols).T
    pred_cols[N:, C : 2 * C] = scale * to_freq(inner_cols).T
    pred_cols = np.concatenate(np_split(pred_cols), axis=0)
    res_cols = np.zeros((2 * N, 2 * N))
    res_cols[:C, :N] = to_freq(inner_cols)
    res_cols[C : 2 * C, N:] = to_freq(inner_cols)
    res_cols = np.concatenate(np_split(res_cols), axis=0)
    back_cols = wide(scale * to_freq(full).T)
    psf_rows = np.concatenate([np.concatenate([psf_rows[:N], psf_rows[:N]], axis=1),
                               np.concatenate([psf_rows[N:], np.zeros_like(psf_rows[N:])], axis=1)], axis=0)
    tables = (patch_cols, patch_rows, psf_cols, psf_rows, pred_rows, pred_cols, res_cols, res_rows,
              back_rows, back_cols)
    places, at = [], 0
    for table in tables:
        places.append((at, table.shape[0]))
        at += table.shape[0]
    joined = np.zeros((at, 2 * N), ml_dtypes.bfloat16)
    for (start, rows), table in zip(places, tables):
        joined[start : start + rows, : table.shape[1]] = table
    return joined, places


def split(x):
    high = x.astype(BF16)
    return high, (x - high.astype(F32)).astype(BF16)


def dot(a, b):
    return jnp.dot(a, b, preferred_element_type=F32)


def right_wide(x, table_ref):
    high, low = split(x)
    both = dot(jnp.concatenate([high, low], axis=1), table_ref[...])
    return both[:, :N] + both[:, N:]


def right_three(x, table_ref):
    high, low = split(x)
    depth = x.shape[1]
    return (dot(high, table_ref[:depth, :]) + dot(low, table_ref[:depth, :])
            + dot(high, table_ref[depth:, :]))


def left_three(table_ref, x):
    rows = table_ref.shape[0] // 2
    high, low = split(x)
    depth = x.shape[0]
    both = dot(table_ref[:, :depth], high)
    return both[:rows] + both[rows:] + dot(table_ref[:rows, :depth], low)


def turned(y, sign):
    return pltpu.roll(y, 64, 1) * sign


def stacked(parts, sign):
    return jnp.concatenate(
        [jnp.concatenate([y, turned(y, sign)], axis=0) for y in parts], axis=1)


def lanes():
    lane = lax.broadcasted_iota(jnp.int32, (1, N), 1)
    return lane, jnp.where(lane < 64, 1.0, -1.0).astype(F32), lane < 64


def place_of(code):
    code = jnp.maximum(code - 1, 0)
    which = lax.shift_right_logical(code, 16)
    row = lax.bitwise_and(lax.shift_right_logical(code, 8), 255) + (EDGE - K + 1)
    column = lax.bitwise_and(code, 255) + (SIDE - K + 1)
    return which, lax.shift_right_logical(column, 7), row, lax.bitwise_and(column, N - 1)


def cut(code, ext_ref):
    which, at, row, over = place_of(code)
    rows = pl.ds(row, N)
    window = jnp.concatenate([ext_ref[which, at, rows, :], ext_ref[which, at + 1, rows, :]], axis=1)
    return pltpu.roll(window, lax.bitwise_and(2 * N - over, 2 * N - 1), 1)[:, :N]


def halves(k, low_half):
    rk = pltpu.roll(k, 64, 1)
    return jnp.where(low_half, k, rk), jnp.where(low_half, -rk, k)


def predict(patches, psfs, tables):
    patch_cols, patch_rows, psf_cols, psf_rows, pred_rows, pred_cols = tables
    count = len(patches)
    lane, sign, low_half = lanes()
    y = right_wide(jnp.concatenate(patches, axis=0), patch_cols)
    z = left_three(patch_rows, stacked([y[e * N : e * N + N] for e in range(count)], sign))
    pairs = []
    for x in psfs:
        both = jnp.concatenate([pltpu.roll(x, 1, 0), x], axis=1)
        pairs.append(pltpu.roll(both, N, 1, stride=2, stride_axis=0)[:, :N])
    high, low = split(jnp.concatenate(pairs, axis=0))
    y = dot(jnp.concatenate([high, low], axis=1), psf_cols[: 2 * N, :]) + dot(high, psf_cols[2 * N :, :])
    y = stacked([jnp.concatenate([y[32 * e : 32 * e + 32, :N], y[32 * e : 32 * e + 32, N:]], axis=0)
                 for e in range(count)], sign)
    high, low = split(y)
    khat = (dot(psf_rows[:N, :], jnp.concatenate([high, low], axis=0))
            + dot(psf_rows[N:, :N], high))
    khat = [khat[:, e * N : e * N + N] for e in range(count)]
    spec = []
    for e in range(count):
        k_re, k_im = halves(khat[e], low_half)
        p = z[:, e * N : e * N + N]
        rp = pltpu.roll(p, 64, 1)
        spec.append(jnp.concatenate(
            [p * k_re + rp * k_im, (rp * k_re - p * k_im) * sign], axis=0))
    u = left_three(pred_rows, jnp.concatenate(spec, axis=1))
    u = jnp.concatenate(
        [jnp.concatenate([u[:PAD, e * N : e * N + N], u[PAD:, e * N : e * N + N]], axis=1)
         for e in range(count)], axis=0)
    predicted = right_three(u, pred_cols)
    last = lax.broadcasted_iota(jnp.int32, (PAD, 1), 0) == PAIRS - 1
    flat = []
    for e in range(count):
        image = pltpu.roll(predicted[e * PAD : e * PAD + PAD], 0, 1, stride=4, stride_axis=0)
        front, rear = image[:, :N], image[:, N:]
        flat.append(jnp.where(last, 0.0, front) + pltpu.roll(rear, 1, 0)
                    + pltpu.roll(jnp.where(last, front, 0.0), 2, 0))
    return khat, flat


def adjoint(resids, khat, tables):
    res_cols, res_rows, back_rows, back_cols = tables
    count = len(resids)
    lane, sign, low_half = lanes()
    number = lax.broadcasted_iota(jnp.int32, (PAD, 1), 0)
    last = number == PAIRS - 1
    turn = lax.bitwise_and(lane + 4 * number, N - 1)
    pairs = []
    for resid in resids:
        front = jnp.take_along_axis(resid, turn, axis=1, mode="promise_in_bounds")
        rear = jnp.take_along_axis(pltpu.roll(resid, PAD - 1, 0), turn, axis=1, mode="promise_in_bounds")
        pairs.append(jnp.concatenate(
            [jnp.where(lane + 4 * number < N, front, rear),
             jnp.where(last, pltpu.roll(resid, PAD - 2, 0), rear)], axis=1))
    v = right_three(jnp.concatenate(pairs, axis=0), res_cols)
    v = [jnp.concatenate([v[e * PAD : e * PAD + PAD, :N], v[e * PAD : e * PAD + PAD, N:]], axis=0)
         for e in range(count)]
    r = left_three(res_rows, stacked(v, sign))
    spec = []
    for e in range(count):
        k_re, k_im = halves(khat[e], low_half)
        p = r[:, e * N : e * N + N]
        rp = pltpu.roll(p, 64, 1)
        spec.append(jnp.concatenate(
            [p * k_re - rp * k_im, (rp * k_re + p * k_im) * sign], axis=0))
    u = left_three(back_rows, jnp.concatenate(spec, axis=1))
    back = right_wide(jnp.concatenate([u[:, e * N : e * N + N] for e in range(count)], axis=0), back_cols)
    return [back[e * N : e * N + N] for e in range(count)]


def three(x):
    high = x.astype(BF16)
    rest = x - high.astype(F32)
    middle = rest.astype(BF16)
    return jnp.concatenate([high, middle, (rest - middle.astype(F32)).astype(BF16)], axis=0)


def own_places(packed_ref, own):
    row = lax.shift_right_logical(packed_ref[pl.ds(own, 1), :], 19)
    count = row.shape[1]
    first = lax.broadcasted_iota(jnp.int32, (count, count), 0)
    second = lax.broadcasted_iota(jnp.int32, (count, count), 1)
    column = jnp.sum(jnp.where(first == second, row, 0), axis=1, keepdims=True)
    return row, column, first, second


def places_of_tile(packed_ref, own):
    packed = packed_ref[...]
    count = packed.shape[1]
    here = lax.shift_right_logical(packed, 19) == own
    code = lax.bitwise_and(packed, (1 << 19) - 1) + 1
    first = lax.broadcasted_iota(jnp.int32, (count, count), 0)
    second = lax.broadcasted_iota(jnp.int32, (count, count), 1)
    earlier = (first < second).astype(F32).astype(BF16)
    rank = dot(here.astype(F32).astype(BF16), earlier)
    return jnp.concatenate(
        [jnp.sum(jnp.where(jnp.logical_and(here, rank == float(s)), code, 0), axis=1, keepdims=True)
         for s in range(CAP)], axis=1)


def neighbours(n_ra, n_dec):
    ra, dec = lax.axis_index("ra"), lax.axis_index("dec")
    up, down = lax.rem(ra + 1, n_ra), lax.rem(ra + n_ra - 1, n_ra)
    right, left = lax.rem(dec + 1, n_dec), lax.rem(dec + n_dec - 1, n_dec)
    return ra, dec, up, down, right, left


def signal_all(devices):
    for device in devices:
        pl.semaphore_signal(pltpu.get_barrier_semaphore(), inc=1, device_id=device, device_id_type=MESH)


def wait_all(devices):
    pl.semaphore_wait(pltpu.get_barrier_semaphore(), len(devices))


def moved(dec, shift, n_dec, sign):
    rings = n_dec // RING
    outer = lax.rem(dec // RING + rings + sign * shift[0], rings)
    inner = lax.rem(lax.rem(dec, RING) + RING + sign * shift[1], RING)
    return outer * RING + inner


def shifts():
    return [(j * len(PEERS[j]) + i, shift) for j in range(len(PEERS)) for i, shift in enumerate(PEERS[j])
            if shift != (0, 0)]


def edges(n_ra, n_dec, ra, dec):
    zero, one = jnp.zeros((), F32), jnp.ones((), F32)
    return (jnp.where(ra > 0, one, zero), jnp.where(ra < n_ra - 1, one, zero),
            jnp.where(dec > 0, one, zero), jnp.where(dec < n_dec - 1, one, zero))


def sender(send, recv):
    def copy(index, src, dst, other):
        return pltpu.make_async_remote_copy(
            src_ref=src, dst_ref=dst, send_sem=send.at[index], recv_sem=recv.at[index],
            device_id=other, device_id_type=MESH)
    return copy


def rows_of(index, size):
    return pl.ds(pl.multiple_of(index * size, 8), size)


def slot_rows(index, s):
    return pl.ds(pl.multiple_of(index * (CAP * SLOT), 8) + s * SLOT, SLOT)


def slot_chooser(packed_ref, dec, n_dec):
    row, column, first, second = own_places(packed_ref, dec)
    count = row.shape[1]
    slots = CAP * n_dec
    rank = jnp.sum(jnp.where(jnp.logical_and(column == row, first < second), 1, 0), axis=0, keepdims=True)
    place = row * CAP + rank
    chosen = (lax.broadcasted_iota(jnp.int32, (slots, count), 0) == place).astype(F32).astype(BF16)
    return jnp.concatenate([chosen] * 3, axis=1)


def to_slots(chosen, ref, out_ref, rows):
    width, slots = ref.shape[1], chosen.shape[0]
    for start in range(0, rows, 4):
        end = min((start + 4) * N, width)
        if start * N < width:
            y = dot(chosen, three(ref[:, start * N : end]))
            if end < (start + 4) * N:
                y = jnp.concatenate([y, jnp.zeros((slots, (start + 4) * N - end), F32)], axis=1)
        else:
            y = jnp.zeros((slots, 4 * N), F32)
        for t in range(4):
            out_ref[pl.ds(start + t, slots, stride=rows), :] = y[:, t * N : t * N + N]


def photometry_kernel(n_ra, n_dec, places, meta_ref, packed_ref, *refs):
    inputs, refs = refs[:5], refs[5:]
    (back_ref, residual_ref, ext_ref, to_right, to_left, from_left, from_right, corners, psf_out, psf_in,
     obs_slots, var_slots, pred_out, pred_in, resid_in, khat_ref, send, recv, send_psf, recv_psf,
     send_pred, recv_pred, send_res, recv_res, psf_ref, obs_ref, var_ref, model_ref, joined, load) = refs
    tables = [joined.at[pl.ds(start, rows), :] for start, rows in places]
    loads = [pltpu.make_async_copy(src, dst, load.at[i]) for i, (src, dst) in enumerate(
        zip(inputs, (psf_ref, obs_ref, var_ref, model_ref, joined)))]
    for i in (3, 0, 1, 2, 4):
        loads[i].start()
    ra, dec, up, down, right, left = neighbours(n_ra, n_dec)
    peers = [(ra, moved(dec, shift, n_dec, 1)) for _, shift in shifts()] + [(up, dec), (down, dec)]
    signal_all(peers)
    loads[3].wait()
    tra, tdec = model_ref.shape[1], model_ref.shape[2]
    top = EDGE + tra
    low_half = lax.broadcasted_iota(jnp.int32, (1, N), 1) < 64
    copy = sender(send, recv)
    for q in range(3):
        to_right[q] = jnp.where(
            low_half, pltpu.roll(model_ref[2 * q + 1, :, tdec - N :], 64, 1), model_ref[2 * q, :, tdec - N :])
        to_left[q] = jnp.where(
            low_half, model_ref[2 * q, :, :N], pltpu.roll(model_ref[2 * q + 1, :, :N], 64, 1))
    wait_all(peers)
    ends = (slice(tra - EDGE, tra), slice(0, EDGE), slice(EDGE, tra - EDGE))
    sides = []
    for i, rows in enumerate(ends):
        sides += [copy(2 * i, to_right.at[:, rows, :], from_left.at[:, rows, :], (ra, right)),
                  copy(2 * i + 1, to_left.at[:, rows, :], from_right.at[:, rows, :], (ra, left))]
    for c in sides:
        c.start()
    copies = []
    for t in range(2):
        cols = slice(t * N, t * N + N)
        copies += [copy(6 + t, model_ref.at[:, tra - EDGE :, cols], ext_ref.at[:, 1 + t, :EDGE, :], (up, dec)),
                   copy(8 + t, model_ref.at[:, :EDGE, cols], ext_ref.at[:, 1 + t, top:, :], (down, dec))]
    for c in copies:
        c.start()
    chosen = slot_chooser(packed_ref, dec, n_dec)
    loads[0].wait()
    to_slots(chosen, psf_ref, psf_out, PSF_ROWS)
    moves = {}
    here = rows_of(dec, CAP * PSF_ROWS)
    for d, shift in shifts():
        tile = moved(dec, shift, n_dec, 1)
        moves[shift] = sender(send_psf, recv_psf)(
            d, psf_out.at[rows_of(tile, CAP * PSF_ROWS), :], psf_in.at[here, :], (ra, tile))

    def send_psfs(group):
        for shift in group:
            if shift in moves:
                moves[shift].start()

    send_psfs(PEERS[0])
    psf_in[here, :] = psf_out[here, :]
    for t in range(2):
        ext_ref[:, 1 + t, EDGE:top, :] = model_ref[:, :, t * N : t * N + N]
    loads[1].wait()
    to_slots(chosen, obs_ref, obs_slots, SLOT)
    more = []
    for i in range(2):
        for c in sides[2 * i : 2 * i + 2]:
            c.wait_recv()
        other = (up, dec) if i == 0 else (down, dec)
        now = [copy(10 + i, from_left.at[:, ends[i], :], corners.at[i], other),
               copy(12 + i, from_right.at[:, ends[i], :], corners.at[2 + i], other)]
        for c in now:
            c.start()
        more += now
    send_psfs(PEERS[1])
    loads[2].wait()
    to_slots(chosen, var_ref, var_slots, SLOT)
    for c in sides[4:]:
        c.wait_recv()
    for group in PEERS[2:]:
        send_psfs(group)
    in_low, in_high, in_left, in_right = edges(n_ra, n_dec, ra, dec)

    def place(pieces):
        for src, q, col, rows, scale in pieces:
            value = src[...] * scale
            ext_ref[2 * q, col, rows, :] = value
            ext_ref[2 * q + 1, col, rows, :] = pltpu.roll(value, 64, 1)

    middle, low, high = slice(EDGE, top), slice(0, EDGE), slice(top, top + EDGE)
    place([(from_left.at[q], q, 0, middle, in_left) for q in range(3)]
          + [(from_right.at[q], q, 3, middle, in_right) for q in range(3)])
    for c in copies + more:
        c.wait()

    @pl.when(ra == 0)
    def _():
        ext_ref[:, 1:3, :EDGE, :] = jnp.zeros((ext_ref.shape[0], 2, EDGE, N), F32)

    @pl.when(ra == n_ra - 1)
    def _():
        ext_ref[:, 1:3, top:, :] = jnp.zeros((ext_ref.shape[0], 2, EDGE, N), F32)

    for q in range(3):
        place([(corners.at[0, q], q, 0, low, in_low * in_left), (corners.at[1, q], q, 0, high, in_high * in_left),
               (corners.at[2, q], q, 3, low, in_low * in_right), (corners.at[3, q], q, 3, high, in_high * in_right)])
    for c in sides:
        c.wait_send()

    own = rows_of(dec, CAP * SLOT)
    steps = len(PEERS)
    pred_moves, res_moves = {}, {}
    for d, shift in shifts():
        owner, tile = moved(dec, shift, n_dec, -1), moved(dec, shift, n_dec, 1)
        pred_moves[shift] = sender(send_pred, recv_pred)(
            d, pred_out.at[rows_of(owner, CAP * SLOT), :], pred_in.at[own, :], (ra, owner))
        res_moves[shift] = sender(send_res, recv_res)(
            d, residual_ref.at[rows_of(tile, CAP * SLOT), :], resid_in.at[own, :], (ra, tile))

    def owned(j):
        return [(moved(dec, PEERS[j][e // CAP], n_dec, -1), e % CAP) for e in range(GROUP)]

    loads[4].wait()
    for j in range(steps + B_LAG):
        if j < steps:
            for shift in PEERS[j]:
                if shift in moves:
                    moves[shift].wait_recv()
            which = owned(j)
            khat, flat = predict(
                [cut(meta_ref[o, s], ext_ref) for o, s in which],
                [psf_in[rows_of(o * CAP + s, PSF_ROWS), :] for o, s in which],
                tables[:6])
            for (o, s), k, f in zip(which, khat, flat):
                khat_ref[o * CAP + s] = k
                pred_out[slot_rows(o, s), :] = f[:SLOT]
            for shift in PEERS[j]:
                if shift in pred_moves:
                    pred_moves[shift].start()
        if 1 <= j <= steps:
            for shift in PEERS[j - 1]:
                tile = rows_of(moved(dec, shift, n_dec, 1), CAP * SLOT)
                if shift in pred_moves:
                    pred_moves[shift].wait_recv()
                    residual_ref[tile, :] = var_slots[tile, :] * (pred_in[tile, :] - obs_slots[tile, :])
                    res_moves[shift].start()
                else:
                    resid = var_slots[own, :] * (pred_out[own, :] - obs_slots[own, :])
                    residual_ref[own, :] = resid
                    resid_in[own, :] = resid
        if j >= B_LAG:
            for shift in PEERS[j - B_LAG]:
                if shift in res_moves:
                    res_moves[shift].wait_recv()
            which = owned(j - B_LAG)
            back = adjoint(
                [jnp.concatenate([resid_in[slot_rows(o, s), :], jnp.zeros((PAD - SLOT, N), F32)], axis=0)
                 for o, s in which],
                [khat_ref[o * CAP + s] for o, s in which], tables[6:])
            for (o, s), image in zip(which, back):
                back_ref[o * CAP + s] = image
    for shift in pred_moves:
        moves[shift].wait_send()
        pred_moves[shift].wait_send()
        res_moves[shift].wait_send()


def vmem(count):
    return [pl.BlockSpec(memory_space=pltpu.VMEM)] * count


def photometry(meta, packed, psf, obs, var, model, n_ra, n_dec):
    bands, tra, tdec = model.shape
    strip = pltpu.VMEM((3, tra, N), F32)
    slots = n_dec * CAP
    image, small = pltpu.VMEM((slots * SLOT, N), F32), pltpu.VMEM((slots * PSF_ROWS, N), F32)
    several, many = pltpu.SemaphoreType.DMA((14,)), pltpu.SemaphoreType.DMA((n_dec,))
    joined, places = make_tables()
    return pl.pallas_call(
        functools.partial(photometry_kernel, n_ra, n_dec, places),
        out_shape=[
            jax.ShapeDtypeStruct((slots, N, N), F32),
            jax.ShapeDtypeStruct((slots * SLOT, N), F32),
        ],
        in_specs=[pl.BlockSpec(memory_space=pltpu.SMEM)] + vmem(1) + [pl.BlockSpec(memory_space=pltpu.HBM)] * 5,
        out_specs=vmem(2),
        scratch_shapes=[pltpu.VMEM((bands, (tdec + 2 * SIDE) // N, tra + 2 * EDGE, N), F32),
                        strip, strip, strip, strip, pltpu.VMEM((4, 3, EDGE, N), F32), small, small,
                        image, image, image, image, image, pltpu.VMEM((slots, N, N), F32),
                        several, several, many, many, many, many, many, many]
        + [pltpu.VMEM(o.shape, o.dtype) for o in (psf, obs, var, model, joined)]
        + [pltpu.SemaphoreType.DMA((5,))],
        compiler_params=pltpu.CompilerParams(
            collective_id=0, has_side_effects=True, vmem_limit_bytes=MAIN_LIMIT),
        cost_estimate=pl.CostEstimate(flops=0, bytes_accessed=40_000_000, transcendentals=0),
    )(meta, packed, psf, obs, var, model, jnp.asarray(joined))


def meta_kernel(packed_ref, meta_ref):
    meta_ref[...] = places_of_tile(packed_ref, lax.axis_index("dec"))


def tile_meta(packed):
    return pl.pallas_call(
        meta_kernel, out_shape=jax.ShapeDtypeStruct((packed.shape[0], CAP), jnp.int32))(packed)


def scatter_kernel(n_dec, meta_ref, packed_ref, slots_ref, back_ref, residual_ref, acc_ref):
    step = pl.program_id(0)

    @pl.when(step == 0)
    def _():
        acc_ref[...] = jnp.zeros_like(acc_ref)
        row, column, first, second = own_places(packed_ref, lax.axis_index("dec"))
        count = row.shape[1]
        slots = CAP * n_dec
        rank = jnp.sum(jnp.where(jnp.logical_and(column == row, second < first), 1, 0), axis=1, keepdims=True)
        place = column * CAP + rank
        chosen = (lax.broadcasted_iota(jnp.int32, (count, slots), 1) == place).astype(F32).astype(BF16)
        chosen = jnp.concatenate([chosen] * 3, axis=1)
        width = residual_ref.shape[1]
        for start in range(0, SLOT, 4):
            if start * N >= width:
                break
            x = jnp.concatenate(
                [slots_ref[pl.ds(start + t, slots, stride=SLOT), :] for t in range(4)], axis=1)
            y = dot(chosen, three(x))
            end = min((start + 4) * N, width)
            residual_ref[:, start * N : end] = y[:, : end - start * N]

    for e in range(GROUP):
        which, at, row, over = place_of(meta_ref[step * (GROUP // CAP) + e // CAP, e % CAP])
        image = back_ref[e]
        image = pltpu.roll(jnp.concatenate([image, jnp.zeros_like(image)], axis=1), over, 1)
        rows = pl.ds(row, N)
        acc_ref[which, at, rows, :] += image[:, :N]
        acc_ref[which, at + 1, rows, :] += image[:, N:]


def scatter(meta, packed, residual, back, shape, n_dec):
    def whole(block):
        return pl.BlockSpec(block, lambda i, meta: (0,) * len(block), pipeline_mode=pl.Buffered(1))

    bands, tra, tdec = shape
    wide = (bands, (tdec + 2 * SIDE) // N, tra + 2 * EDGE, N)
    out = (packed.shape[1], C * C)
    return pl.pallas_call(
        functools.partial(scatter_kernel, n_dec),
        grid_spec=pltpu.PrefetchScalarGridSpec(
            num_scalar_prefetch=1,
            grid=(back.shape[0] // GROUP,),
            in_specs=[whole(packed.shape), whole(residual.shape), pl.BlockSpec((GROUP, N, N), lambda i, meta: (i, 0, 0))],
            out_specs=[whole(out), whole(wide)],
        ),
        out_shape=[jax.ShapeDtypeStruct(out, F32), jax.ShapeDtypeStruct(wide, F32)],
        compiler_params=pltpu.CompilerParams(vmem_limit_bytes=SCATTER_LIMIT),
    )(meta, packed, residual, back)


def fold_kernel(n_ra, n_dec, acc_ref, out_ref, to_right, to_left, from_left, from_right, out_corners, corners,
                from_up, from_down, send, recv):
    ra, dec, up, down, right, left = neighbours(n_ra, n_dec)
    peers = [(up, dec), (down, dec), (ra, right), (ra, left)]
    signal_all(peers)
    tra, tdec = out_ref.shape[1], out_ref.shape[2]
    top = EDGE + tra
    low_half = lax.broadcasted_iota(jnp.int32, (1, N), 1) < 64
    copy = sender(send, recv)

    def pack_left(q, rows):
        return jnp.where(low_half, pltpu.roll(acc_ref[2 * q + 1, 0, rows, :], 64, 1), acc_ref[2 * q, 0, rows, :])

    def pack_right(q, rows):
        return jnp.where(low_half, acc_ref[2 * q, 3, rows, :], pltpu.roll(acc_ref[2 * q + 1, 3, rows, :], 64, 1))

    middle, lower, upper = slice(EDGE, top), slice(0, EDGE), slice(top, top + EDGE)
    for q in range(3):
        out_corners[0, q] = pack_left(q, lower)
        out_corners[1, q] = pack_left(q, upper)
        out_corners[2, q] = pack_right(q, lower)
        out_corners[3, q] = pack_right(q, upper)
        to_left[q] = pack_left(q, middle)
        to_right[q] = pack_right(q, middle)
    wait_all(peers)
    inner, low_rows, high_rows = slice(EDGE, tra - EDGE), slice(0, EDGE), slice(tra - EDGE, tra)
    turns = [copy(i, out_corners.at[i], corners.at[i], (down if i % 2 == 0 else up, dec)) for i in range(4)]
    copies = [
        copy(4, to_left.at[:, inner, :], from_right.at[:, inner, :], (ra, left)),
        copy(5, to_right.at[:, inner, :], from_left.at[:, inner, :], (ra, right)),
        copy(6, acc_ref.at[:, 1:3, lower, :], from_up, (down, dec)),
        copy(7, acc_ref.at[:, 1:3, upper, :], from_down, (up, dec)),
    ]
    for c in turns + copies:
        c.start()
    in_low, in_high, in_left, in_right = edges(n_ra, n_dec, ra, dec)
    for c in turns:
        c.wait_recv()
    to_left[:, high_rows, :] += corners[0] * in_high
    to_right[:, high_rows, :] += corners[2] * in_high
    more = [
        copy(8, to_left.at[:, high_rows, :], from_right.at[:, high_rows, :], (ra, left)),
        copy(9, to_right.at[:, high_rows, :], from_left.at[:, high_rows, :], (ra, right)),
    ]
    for c in more:
        c.start()
    to_left[:, low_rows, :] += corners[1] * in_low
    to_right[:, low_rows, :] += corners[3] * in_low
    more += [
        copy(10, to_left.at[:, low_rows, :], from_right.at[:, low_rows, :], (ra, left)),
        copy(11, to_right.at[:, low_rows, :], from_left.at[:, low_rows, :], (ra, right)),
    ]
    for c in more[2:]:
        c.start()
    for t in range(2):
        out_ref[:, :, t * N : t * N + N] = acc_ref[:, 1 + t, middle, :]
    for c in turns:
        c.wait_send()
    for c in copies[2:]:
        c.wait()
    for t in range(2):
        cols = slice(t * N, t * N + N)
        out_ref[:, high_rows, cols] += from_up[:, t] * in_high
        out_ref[:, low_rows, cols] += from_down[:, t] * in_low
    for c in copies[:2] + more:
        c.wait()
    for q in range(3):
        for src, scale, at_right in ((from_right.at[q], in_right, True), (from_left.at[q], in_left, False)):
            value = src[...] * scale
            other = pltpu.roll(value, 64, 1)
            if at_right:
                cols, keep = slice(tdec - N, tdec), jnp.logical_not(low_half)
            else:
                cols, keep = slice(0, N), low_half
            out_ref[2 * q, :, cols] += jnp.where(keep, value, 0.0)
            out_ref[2 * q + 1, :, cols] += jnp.where(keep, other, 0.0)


def fold(acc, n_ra, n_dec):
    bands, tra, tdec = acc.shape[0], acc.shape[2] - 2 * EDGE, acc.shape[1] * N - 2 * SIDE
    strip = pltpu.VMEM((3, tra, N), F32)
    corner = pltpu.VMEM((4, 3, EDGE, N), F32)
    band = pltpu.VMEM((bands, 2, EDGE, N), F32)
    return pl.pallas_call(
        functools.partial(fold_kernel, n_ra, n_dec),
        out_shape=jax.ShapeDtypeStruct((bands, tra, tdec), F32),
        in_specs=vmem(1),
        out_specs=pl.BlockSpec(memory_space=pltpu.VMEM),
        scratch_shapes=[strip, strip, strip, strip, corner, corner, band, band,
                        pltpu.SemaphoreType.DMA((12,)), pltpu.SemaphoreType.DMA((12,))],
        compiler_params=pltpu.CompilerParams(
            collective_id=1, has_side_effects=True, vmem_limit_bytes=SMALL_LIMIT),
        cost_estimate=pl.CostEstimate(flops=0, bytes_accessed=40_000_000, transcendentals=0),
    )(acc)


def body(model, observed, inv_var, psf, target_dec, band, offset_ra, offset_dec):
    n_ra, n_dec = lax.axis_size("ra"), lax.axis_size("dec")
    e_dev = observed.shape[0]
    packed = (((target_dec[:, 0] * 8 + band) * 256 + offset_ra) * 256 + offset_dec).reshape(n_dec, e_dev)
    meta = tile_meta(packed)
    back, slots = photometry(meta, packed, psf, observed, inv_var, model, n_ra, n_dec)
    residual, acc = scatter(meta, packed, slots, back, model.shape, n_dec)
    return residual, fold(acc, n_ra, n_dec)


def solution(mesh):
    placed = (
        P(None, "ra", "dec"),
        P(("ra", "dec"), None),
        P(("ra", "dec"), None),
        P(("ra", "dec"), None),
        P("ra", None),
        P("ra"),
        P("ra"),
        P("ra"),
    )
    return jax.shard_map(
        body,
        mesh=mesh,
        in_specs=placed,
        out_specs=(P(("ra", "dec"), None), P(None, "ra", "dec")),
        check_vma=False,
    )
```
